32 devices in a mesh: dp: 8 (over y, x, core), expert: 4 (over z).
Axes of the slice: x: 2, y: 2, z: 4, core: 2. Of those that a mesh axis runs over, the one named last changes fastest.
Arguments:
- tokens: bfloat16 [4096, 2048], P(('dp', 'expert')), may hold values from -6 to 6
- cotangent: bfloat16 [4096, 2048], P(('dp', 'expert')), may hold values from -6 to 6
- route: int32 [4096, 1], P(('dp', 'expert')), may hold values from 0 to 3; in each aligned block of 128 rows (0 to 127, 128 to 255, ...) at most 48 rows name the same one
- prob: bfloat16 [4096], P(('dp', 'expert')), may hold values from 0.049804688 to 1
- w_gate: float32 [4, 2048, 512], P('expert'), may hold values from -0.125 to 0.125
- w_up: float32 [4, 2048, 512], P('expert'), may hold values from -0.125 to 0.125
- w_down: float32 [4, 2048, 512], P('expert'), may hold values from -0.25 to 0.25
Outputs:
- grad_input: bfloat16 [4096, 2048], P(('dp', 'expert'))
- grad_prob: bfloat16 [4096], P(('dp', 'expert'))
- grad_gate: float32 [4, 2048, 512], P('expert', 'dp')
- grad_up: float32 [4, 2048, 512], P('expert', 'dp')
- grad_down: float32 [4, 2048, 512], P('expert', 'dp')
The draws below stay inside these ranges and needn't reach their ends.
Inputs may be any that keep to these rules, and one draw needn't show every extreme that they name: `route`: within each device's aligned block of 128 rows (devices in the order of dp, then expert) each hot expert is named by at most 48 rows, a bound that some block reaches.
All inputs are finite; a program needn't handle non-finite values.
Results may differ from the reference program's by a relative error of at most 0.003.
Values may be sent and summed in bfloat16 or wider, within the bound.
No kernel may reach another device: no remote copies, remote signals or barrier semaphores. Data moves between devices by JAX's collectives and lax.ppermute only.
A program may use at most 128 MiB of HBM per device.

```python
import math
import jax
import jax.numpy as jnp
import numpy as np
from jax import lax

D = 2048
FF = 512
HOT = 4
TOK_DEV = 128
FQ = 512
CAP = 48
SHARDS = 4
TOKENS = 4096
N_DP = 8
N_EXPERT = 4


def with_spikes(values, stream_key, source, target, blocks, factor):
    owner, partner = [(jnp.arange(values.shape[dim]) // (values.shape[dim] // blocks)).reshape([-1 if axis == dim else 1 for axis in range(values.ndim)]) for dim in (source, target)]
    chosen = jax.random.permutation(stream_key, blocks)[partner]
    strong = (owner == chosen) | (owner == (partner + blocks // 2) % blocks)
    return jnp.where(strong, factor * values, values)


def block_levels(rng, dims, split, low, high):
    def one(axis_at, parts):
        steps = jax.random.uniform(jax.random.fold_in(jax.random.fold_in(rng, 6), axis_at), (parts,), jnp.float32, low / len(split), high / len(split))
        return jnp.repeat(jnp.exp(steps), dims[axis_at] // parts).reshape((-1,) + (1,) * (len(dims) - axis_at - 1))

    level = one(*split[0])
    for cut in split[1:]:
        level = level * one(*cut)
    return level


def assign_block(rng, own, number, rows, amount, top, bound, lean):
    ranking = jax.random.permutation(rng, amount)
    packed, ordinary = portions_of(amount, rows * top, bound, lean, True), portions_of(amount, rows * top, bound, lean, False)
    places = jnp.arange(amount)

    def named(tallies, turn):
        used = int((tallies > 0).sum())
        fixed = max(1, used // 4)
        passed = fixed + (places - fixed + turn * (used - fixed)) % max(1, amount - fixed)
        return jnp.zeros((amount,), jnp.int32).at[ranking[jnp.where(places < fixed, places, passed)]].set(jnp.asarray(tallies, jnp.int32))

    tallies = jnp.where(number % 4 == 0, named(packed, number // 4), named(ordinary, number - number // 4 - 1))
    mixed = jax.random.permutation(jax.random.fold_in(own, 3), amount)
    donor, receiver = mixed[0:amount // 2 * 2:2], mixed[1:amount // 2 * 2:2]
    room = jnp.minimum(tallies[donor] - 1, bound - tallies[receiver]) // 2
    room = jnp.where((donor == ranking[0]) | (receiver == ranking[0]) | (tallies[receiver] == 0), 0, jnp.maximum(room, 0))
    passed = jax.random.randint(jax.random.fold_in(own, 4), (amount // 2,), 0, 1 << 20) % (room + 1)
    tallies = tallies.at[donor].add(-passed).at[receiver].add(passed)
    labels = jnp.searchsorted(jnp.cumsum(tallies), jnp.arange(rows * top), side="right").astype(jnp.int32)
    table = labels.reshape(top, rows).T
    table = table[jax.random.permutation(jax.random.fold_in(own, 1), rows)]
    turn = jax.random.randint(jax.random.fold_in(own, 2), (rows, 1), 0, top)
    return jnp.take_along_axis(table, (jnp.arange(top)[None, :] + turn) % top, axis=1)


def portions_of(number_of, total, limit, slope, full):
    loads = [(1 << 20) // math.isqrt(rank ** slope) + 1 for rank in range(1, number_of + 1)]
    largest = limit if full else min(limit, max(-(-total // number_of), total * loads[0] // sum(loads)))
    least = 1 if total - largest >= number_of - 1 else 0
    given, spare = [largest] + [least] * (number_of - 1), total - largest - least * (number_of - 1)
    while spare > 0:
        candidates = [i for i in range(1, number_of) if given[i] < largest] or [i for i in range(1, number_of) if given[i] < limit]
        pool, left = sum([loads[i] for i in candidates]), spare
        for i in candidates:
            extra = min(limit - given[i], max(1, left * loads[i] // pool), spare)
            given[i] = given[i] + extra
            spare = spare - extra
    return np.array(given)


def bell_draw(key, dims, scale, most, split=(), kind=jnp.bfloat16):
    entries = jax.random.normal(key, dims, jnp.float32) * scale
    if len(split) > 0:
        entries = block_levels(key, dims, split, -0.22, 0.18) * entries
    return jnp.clip(entries, min=-most, max=most).astype(kind)


def noise_with(own_key, shape, scale, reach, split, heavy, kind=jnp.bfloat16):
    result = scale * jax.random.normal(own_key, shape, jnp.float32)
    if split:
        result = result * block_levels(own_key, shape, split, -0.22, 0.18)
    return jnp.clip(with_spikes(result, jax.random.fold_in(own_key, 3), *heavy), -reach, reach).astype(kind)


def setup_inputs(seed: int = 0) -> dict:
    seeds = jax.random.split(jax.random.key(seed), 8)
    tokens = noise_with(seeds[0], (TOKENS, D), 1.0, 6.0, ((0, 32),), (0, 1, 32, 2.75))
    cotangent = bell_draw(seeds[1], (TOKENS, D), 1.0, 6.0, ((0, 32),))
    route_keys = jax.random.split(jax.random.fold_in(seeds[2], 1), TOKENS // TOK_DEV)
    route_turns = jax.random.permutation(jax.random.fold_in(seeds[2], 3), TOKENS // TOK_DEV)
    route = jax.vmap(lambda own, number: assign_block(jax.random.fold_in(seeds[2], 2), own, number, TOK_DEV, HOT, 1, CAP, 2))(route_keys, route_turns).reshape((TOKENS, 1))
    prob = jnp.clip(0.049804688 + 0.9501953 * jax.random.uniform(seeds[3], (TOKENS,), jnp.float32) ** block_levels(seeds[3], (TOKENS,), ((0, 32),), -0.2, 0.2), 0.049804688, 1.0).astype(jnp.bfloat16)
    w_gate = bell_draw(seeds[4], (SHARDS, D, FQ), D ** -0.5, 0.125, ((0, 4),), jnp.float32)
    w_up = bell_draw(seeds[5], (SHARDS, D, FQ), D ** -0.5, 0.125, ((0, 4),), jnp.float32)
    w_down = bell_draw(seeds[6], (SHARDS, D, FQ), FF ** -0.5, 0.25, ((0, 4),), jnp.float32)
    return {"tokens": tokens, "cotangent": cotangent, "route": route, "prob": prob, "w_gate": w_gate, "w_up": w_up, "w_down": w_down}


highest = lax.Precision.HIGHEST

def expert_rows(row_tokens, row_cotangents, row_probs, gate_weight, up_weight, down_weight):
    tokens_f32 = row_tokens.astype(jnp.float32)
    cotangent_f32 = row_cotangents.astype(jnp.float32)
    probs_f32 = row_probs.astype(jnp.float32)
    gate_pre = jnp.dot(tokens_f32, gate_weight, precision=highest)
    up_pre = jnp.dot(tokens_f32, up_weight, precision=highest)
    sigmoid_val = jax.nn.sigmoid(gate_pre)
    activation = gate_pre * sigmoid_val
    hidden = activation * up_pre
    backward = jnp.dot(cotangent_f32, down_weight, precision=highest)
    prob_part = lax.optimization_barrier(jnp.sum(hidden * backward, axis=1))
    d_hidden = probs_f32[:, None] * backward
    d_up = d_hidden * activation
    d_gate = d_hidden * up_pre * sigmoid_val * (1.0 + gate_pre * (1.0 - sigmoid_val))
    input_part = jnp.dot(d_gate, gate_weight.T, precision=highest) + jnp.dot(d_up, up_weight.T, precision=highest)
    grad_g = jnp.dot(tokens_f32.T, d_gate, precision=highest)
    grad_u = jnp.dot(tokens_f32.T, d_up, precision=highest)
    grad_d = jnp.dot((probs_f32[:, None] * cotangent_f32).T, hidden, precision=highest)
    return (input_part, prob_part, grad_g, grad_u, grad_d)

def slot_positions(route_column):
    onehot = (route_column[:, None] == jnp.arange(HOT, dtype=jnp.int32)[None, :]).astype(jnp.int32)
    earlier = jnp.cumsum(onehot, axis=0) - onehot
    rank_in_expert = lax.optimization_barrier(jnp.sum(earlier * onehot, axis=1))
    return (route_column * CAP + rank_in_expert).astype(jnp.int32)

def join_quarters(weight):
    quarters = N_EXPERT // HOT
    return weight.reshape(HOT, quarters, D, FF // quarters).transpose(0, 2, 1, 3).reshape(HOT, D, FF)

def split_quarters(weight):
    quarters = N_EXPERT // HOT
    return weight.reshape(HOT, D, quarters, FF // quarters).transpose(0, 2, 1, 3).reshape(HOT * quarters, D, FF // quarters)

def place_rows(values, position):
    empty_rows = jnp.zeros((HOT * CAP,) + values.shape[1:], values.dtype)
    return empty_rows.at[position].set(values)

def take_rows(values, position):
    return values[position]

def reference(tokens, cotangent, route, prob, w_gate, w_up, w_down):
    full_gate = join_quarters(w_gate)
    full_up = join_quarters(w_up)
    full_down = join_quarters(w_down)
    tok_blocks = tokens.reshape(N_DP, N_EXPERT, TOK_DEV, D)
    cot_blocks = cotangent.reshape(N_DP, N_EXPERT, TOK_DEV, D)
    route_blocks = route.reshape(N_DP, N_EXPERT, TOK_DEV).astype(jnp.int32)
    prob_blocks = prob.reshape(N_DP, N_EXPERT, TOK_DEV)

    def block_step(grad_carry, block_data):
        tok_b, cot_b, route_b, prob_b = block_data
        position = jax.vmap(slot_positions)(route_b)
        slot_tok = jax.vmap(place_rows)(tok_b, position)
        slot_cot = jax.vmap(place_rows)(cot_b, position)
        slot_prob = jax.vmap(place_rows)(prob_b, position)
        rows_tok = slot_tok.reshape(N_EXPERT, HOT, CAP, D).transpose(1, 0, 2, 3).reshape(HOT, N_EXPERT * CAP, D)
        rows_cot = slot_cot.reshape(N_EXPERT, HOT, CAP, D).transpose(1, 0, 2, 3).reshape(HOT, N_EXPERT * CAP, D)
        rows_prob = slot_prob.reshape(N_EXPERT, HOT, CAP).transpose(1, 0, 2).reshape(HOT, N_EXPERT * CAP)
        input_part, prob_part, grad_g, grad_u, grad_d = jax.vmap(expert_rows)(rows_tok, rows_cot, rows_prob, full_gate, full_up, full_down)
        input_back = input_part.astype(jnp.bfloat16).reshape(HOT, N_EXPERT, CAP, D).transpose(1, 0, 2, 3).reshape(N_EXPERT, HOT * CAP, D)
        prob_back = prob_part.astype(jnp.bfloat16).reshape(HOT, N_EXPERT, CAP).transpose(1, 0, 2).reshape(N_EXPERT, HOT * CAP)
        grad_in = jax.vmap(take_rows)(input_back, position)
        grad_pr = jax.vmap(take_rows)(prob_back, position)
        new_carry = (grad_carry[0] + grad_g, grad_carry[1] + grad_u, grad_carry[2] + grad_d)
        return (new_carry, (grad_in, grad_pr))
    zero_grads = jnp.zeros((HOT, D, FF), jnp.float32)
    grad_sums, outputs = lax.scan(block_step, (zero_grads, zero_grads, zero_grads), (tok_blocks, cot_blocks, route_blocks, prob_blocks))
    grad_scale = lax.rsqrt(jnp.float32(TOKENS))
    grad_input = outputs[0].reshape(TOKENS, D)
    grad_prob = outputs[1].reshape(TOKENS)
    return (grad_input, grad_prob, split_quarters(grad_sums[0] * grad_scale), split_quarters(grad_sums[1] * grad_scale), split_quarters(grad_sums[2] * grad_scale))
```

```python
import math

import jax
import jax.numpy as jnp
from jax import lax
from jax.sharding import PartitionSpec as P

HOT = 4
CAP = 48
LANES = 128

highest = lax.Precision.HIGHEST
f32 = jnp.float32
bf16 = jnp.bfloat16


def shifted(values, axis, by):
    size = lax.axis_size(axis)
    return lax.ppermute(values, axis, [(i, (i + by) % size) for i in range(size)])


def placing_matrix(route_column, me, n_expert):
    quarters = n_expert // HOT
    onehot = (route_column[:, None] == jnp.arange(HOT, dtype=jnp.int32)[None, :]).astype(jnp.int32)
    earlier = jnp.cumsum(onehot, axis=0) - onehot
    rank = jnp.sum(earlier * onehot, axis=1)
    slots = jnp.arange(n_expert * CAP, dtype=jnp.int32)
    owner = lax.rem(me + slots // CAP, n_expert) // quarters
    wanted = (owner[:, None] == route_column[None, :]) & ((slots % CAP)[:, None] == rank[None, :])
    return wanted.astype(bf16)


def shards(tokens, cotangent, route, prob, w_gate, w_up, w_down):
    n_expert = lax.axis_size("expert")
    n_dp = lax.axis_size("dp")
    quarters = n_expert // HOT
    width = tokens.shape[1]
    rows = n_expert * CAP
    scale = 1.0 / math.sqrt(tokens.shape[0] * n_dp * n_expert)
    back_type = bf16 if quarters == 1 else f32
    me = lax.axis_index("expert")
    placing = placing_matrix(route[:, 0], me, n_expert)
    prob_lanes = jnp.broadcast_to(prob[:, None], (prob.shape[0], LANES))
    cot_prob = jnp.concatenate([cotangent, prob_lanes], axis=1)
    slot_tok = jnp.dot(placing, tokens, preferred_element_type=f32).astype(bf16)
    slot_cot = jnp.dot(placing, cot_prob, preferred_element_type=f32).astype(bf16)
    slot_tok = slot_tok.reshape(n_expert, CAP, width)
    slot_cot = slot_cot.reshape(n_expert, CAP, width + LANES)
    row_tok = jnp.concatenate(
        [slot_tok[0]] + [shifted(slot_tok[k], "expert", k) for k in range(1, n_expert)]
    )
    row_cotp = jnp.concatenate(
        [slot_cot[0]] + [shifted(slot_cot[k], "expert", k) for k in range(1, n_expert)]
    )
    row_cot = row_cotp[:, :width]
    row_prob = row_cotp[:, width : width + 1].astype(f32)

    gate_pre = jnp.dot(row_tok, w_gate[0], precision=highest, preferred_element_type=f32)
    up_pre = jnp.dot(row_tok, w_up[0], precision=highest, preferred_element_type=f32)
    sig = jax.nn.sigmoid(gate_pre)
    act = gate_pre * sig
    hidden = act * up_pre
    tok_cols = lax.all_to_all(
        row_tok.reshape(rows, n_dp, width // n_dp).transpose(1, 0, 2),
        "dp", split_axis=0, concat_axis=0, tiled=True,
    ).reshape(n_dp * rows, width // n_dp)
    backward = jnp.dot(row_cot, w_down[0], precision=highest, preferred_element_type=f32)
    cot_cols = lax.all_to_all(
        row_cot.reshape(rows, n_dp, width // n_dp).transpose(1, 0, 2),
        "dp", split_axis=0, concat_axis=0, tiled=True,
    ).reshape(n_dp * rows, width // n_dp)
    prob_part = jnp.sum(hidden * backward, axis=1)
    d_hidden = row_prob * backward
    d_up = d_hidden * act
    d_gate = d_hidden * up_pre * sig * (1.0 + gate_pre * (1.0 - sig))
    terms = jnp.stack(
        [(d_gate * scale).astype(bf16), (d_up * scale).astype(bf16), (row_prob * scale * hidden).astype(bf16)]
    )
    all_terms = lax.all_gather(terms, "dp", axis=1, tiled=True)
    input_part = jnp.dot(d_gate, w_gate[0].T, precision=highest) + jnp.dot(
        d_up, w_up[0].T, precision=highest
    )
    back = jnp.concatenate(
        [
            input_part.astype(back_type),
            jnp.broadcast_to(prob_part.astype(back_type)[:, None], (rows, LANES)),
        ],
        axis=1,
    ).reshape(n_expert, CAP, width + LANES)
    home = jnp.concatenate(
        [back[0]] + [shifted(back[k], "expert", n_expert - k) for k in range(1, n_expert)]
    )
    taken = lax.dot_general(
        placing.astype(back_type), home, (((0,), (0,)), ((), ())),
        precision=None if quarters == 1 else highest, preferred_element_type=f32,
    ).astype(bf16)
    grad_input = taken[:, :width]
    grad_prob = taken[:, width]

    def over_rows(cols, term):
        return lax.dot_general(
            cols, term, (((0,), (0,)), ((), ())), preferred_element_type=f32
        )[None]

    return (
        grad_input,
        grad_prob,
        over_rows(tok_cols, all_terms[0]),
        over_rows(tok_cols, all_terms[1]),
        over_rows(cot_cols, all_terms[2]),
    )


def solution(mesh):
    placed = (
        P(("dp", "expert"), None),
        P(("dp", "expert"), None),
        P(("dp", "expert"), None),
        P(("dp", "expert")),
        P("expert", None, None),
        P("expert", None, None),
        P("expert", None, None),
    )
    return jax.shard_map(
        shards,
        mesh=mesh,
        in_specs=placed,
        out_specs=(
            P(("dp", "expert"), None),
            P(("dp", "expert")),
            P("expert", "dp", None),
            P("expert", "dp", None),
            P("expert", "dp", None),
        ),
        check_vma=False,
    )
```

```python
import math

import jax
import jax.numpy as jnp
from jax import lax
from jax.sharding import PartitionSpec as P

HOT = 4
CAP = 48
LANES = 128
CHUNKS = 2

highest = lax.Precision.HIGHEST
f32 = jnp.float32
bf16 = jnp.bfloat16


def shifted(values, axis, by):
    size = lax.axis_size(axis)
    return lax.ppermute(values, axis, [(i, (i + by) % size) for i in range(size)])


def placing_matrix(route_column, me, n_expert):
    quarters = n_expert // HOT
    onehot = (route_column[:, None] == jnp.arange(HOT, dtype=jnp.int32)[None, :]).astype(jnp.int32)
    earlier = jnp.cumsum(onehot, axis=0) - onehot
    rank = jnp.sum(earlier * onehot, axis=1)
    slots = jnp.arange(n_expert * CAP, dtype=jnp.int32)
    owner = lax.rem(me + slots // CAP, n_expert) // quarters
    wanted = (owner[:, None] == route_column[None, :]) & ((slots % CAP)[:, None] == rank[None, :])
    return wanted.astype(bf16)


def gathered(values, axis):
    size = lax.axis_size(axis)
    chips = [values] + [
        lax.ppermute(values, axis, [(i, i ^ (2 * k)) for i in range(size)]) for k in range(1, size // 2)
    ]
    own = jnp.concatenate(chips, axis=1)
    other = lax.ppermute(own, axis, [(i, i ^ 1) for i in range(size)])
    return own, other


def column_slices(values, axis):
    size = lax.axis_size(axis)
    share = values.shape[2] // size
    at = lax.axis_index(axis)

    def part(to):
        return lax.dynamic_slice_in_dim(values, to * share, share, axis=2)

    chips = range(size // 2)
    mine = [part(at ^ (2 * k)) for k in chips]
    theirs = jnp.stack([part((at ^ 1) ^ (2 * k)) for k in chips])
    theirs = lax.ppermute(theirs, axis, [(i, i ^ 1) for i in range(size)])
    both = [jnp.stack([mine[k], theirs[k]], axis=1) for k in chips]
    got = [both[0]] + [
        lax.ppermute(both[k], axis, [(i, i ^ (2 * k)) for i in range(size)]) for k in chips[1:]
    ]
    return jnp.stack(got, axis=1).reshape(values.shape[0], -1, share)


def expert_chunk(row, w_gate, w_up, w_down, scale, back_type):
    width = w_gate.shape[0]
    row_tok = row[:, :width]
    row_cot = row[:, width : 2 * width]
    row_prob = row[:, 2 * width : 2 * width + 1].astype(f32)
    gate_pre = jnp.dot(row_tok, w_gate, precision=highest, preferred_element_type=f32)
    up_pre = jnp.dot(row_tok, w_up, precision=highest, preferred_element_type=f32)
    backward = jnp.dot(row_cot, w_down, precision=highest, preferred_element_type=f32)
    sig = jax.nn.sigmoid(gate_pre)
    act = gate_pre * sig
    hidden = act * up_pre
    prob_part = jnp.sum(hidden * backward, axis=1)
    d_hidden = row_prob * backward
    d_up = d_hidden * act
    d_gate = d_hidden * up_pre * sig * (1.0 + gate_pre * (1.0 - sig))
    terms = jnp.stack(
        [
            (d_gate * scale).astype(bf16),
            (d_up * scale).astype(bf16),
            (row_prob * scale * hidden).astype(bf16),
        ]
    )
    input_part = jnp.dot(d_gate, w_gate.T, precision=highest) + jnp.dot(
        d_up, w_up.T, precision=highest
    )
    back = jnp.concatenate(
        [
            input_part.astype(back_type),
            jnp.broadcast_to(prob_part.astype(back_type)[:, None], (row.shape[0], LANES)),
        ],
        axis=1,
    )
    return terms, back


def shards(tokens, cotangent, route, prob, w_gate, w_up, w_down):
    n_expert = lax.axis_size("expert")
    n_dp = lax.axis_size("dp")
    quarters = n_expert // HOT
    width = tokens.shape[1]
    scale = 1.0 / math.sqrt(tokens.shape[0] * n_dp * n_expert)
    back_type = bf16 if quarters == 1 else f32
    me = lax.axis_index("expert")
    placing = placing_matrix(route[:, 0], me, n_expert)
    prob_lanes = jnp.broadcast_to(prob[:, None], (prob.shape[0], LANES))
    full_rows = jnp.concatenate([tokens, cotangent, prob_lanes], axis=1)
    part = CAP // CHUNKS
    by_shift = placing.reshape(n_expert, CHUNKS, part, -1)

    def send(chunk):
        slots = jnp.dot(
            by_shift[:, chunk].reshape(n_expert * part, -1), full_rows, preferred_element_type=f32
        ).astype(bf16).reshape(n_expert, part, -1)
        return jnp.concatenate(
            [slots[0]] + [shifted(slots[k], "expert", k) for k in range(1, n_expert)]
        )

    rows = [send(chunk) for chunk in range(CHUNKS)]
    sums = [None, None, None]
    taken = None
    for chunk in range(CHUNKS):
        row = rows[chunk]
        cols = column_slices(jnp.stack([row[:, :width], row[:, width : 2 * width]]), "dp")
        terms, back = expert_chunk(
            rows[chunk], w_gate[0], w_up[0], w_down[0], scale, back_type
        )
        back = back.reshape(n_expert, part, -1)
        home = jnp.concatenate(
            [back[0]] + [shifted(back[k], "expert", n_expert - k) for k in range(1, n_expert)]
        )
        mine = lax.dot_general(
            by_shift[:, chunk].reshape(n_expert * part, -1).astype(back_type), home,
            (((0,), (0,)), ((), ())),
            precision=None if quarters == 1 else highest, preferred_element_type=f32,
        )
        taken = mine if taken is None else taken + mine
        own, other = gathered(terms, "dp")
        count = row.shape[0]
        all_terms = jnp.stack(
            [own.reshape(3, n_dp // 2, count, -1), other.reshape(3, n_dp // 2, count, -1)], axis=2
        ).reshape(3, n_dp * count, -1)
        for which, side in enumerate((0, 0, 1)):
            got = lax.dot_general(
                cols[side], all_terms[which], (((0,), (0,)), ((), ())), preferred_element_type=f32
            )
            sums[which] = got if sums[which] is None else sums[which] + got
    taken = taken.astype(bf16)
    return (
        taken[:, :width],
        taken[:, width],
        sums[0][None],
        sums[1][None],
        sums[2][None],
    )


def solution(mesh):
    placed = (
        P(("dp", "expert"), None),
        P(("dp", "expert"), None),
        P(("dp", "expert"), None),
        P(("dp", "expert")),
        P("expert", None, None),
        P("expert", None, None),
        P("expert", None, None),
    )
    return jax.shard_map(
        shards,
        mesh=mesh,
        in_specs=placed,
        out_specs=(
            P(("dp", "expert"), None),
            P(("dp", "expert")),
            P("expert", "dp", None),
            P("expert", "dp", None),
            P("expert", "dp", None),
        ),
        check_vma=False,
    )
```

```python
import functools
import math

import jax
import jax.numpy as jnp
from jax import lax
from jax.experimental import pallas as pl
from jax.experimental.pallas import tpu as pltpu
from jax.sharding import PartitionSpec as P

HOT = 4
CAP = 48
LANES = 128
BLOCK = 256
MIB = 1 << 20

highest = lax.Precision.HIGHEST
f32 = jnp.float32
bf16 = jnp.bfloat16
i32 = jnp.int32
VMEM = pl.BlockSpec(memory_space=pltpu.VMEM)
SMEM = pl.BlockSpec(memory_space=pltpu.SMEM)


def shifted(values, axis, by):
    size = lax.axis_size(axis)
    return lax.ppermute(values, axis, [(i, (i + by) % size) for i in range(size)])


def flipped(values, axis, mask):
    size = lax.axis_size(axis)
    return lax.ppermute(values, axis, [(i, i ^ mask) for i in range(size)])


def cost(flops, moved):
    return pl.CostEstimate(flops=int(flops), bytes_accessed=int(moved), transcendentals=0)


def place_kernel(n_expert, me_ref, route_ref, prob_ref, tok_ref, placing_ref, *pieces):
    quarters = n_expert // HOT
    count, width = tok_ref.shape
    route = route_ref[...]
    hot = (route == lax.broadcasted_iota(i32, (16, count), 0)).astype(f32)
    before = lax.broadcasted_iota(i32, (count, count), 0) < lax.broadcasted_iota(i32, (count, count), 1)
    earlier = jnp.dot(hot.astype(bf16), before.astype(f32).astype(bf16), preferred_element_type=f32)
    rank = jnp.sum(earlier * hot, axis=0, keepdims=True).astype(i32)
    slot = lax.broadcasted_iota(i32, (CAP, count), 0)
    prob = prob_ref[...].astype(f32)
    for k in range(n_expert):
        owner = lax.rem(me_ref[0] + k, n_expert) // quarters
        block = jnp.where((route == owner) & (rank == slot), 1.0, 0.0)
        placing_ref[k * CAP : (k + 1) * CAP, :] = block.astype(bf16)
        slot_prob = jnp.sum(block * prob, axis=1, keepdims=True)
        pieces[k][:, width:] = jnp.broadcast_to(slot_prob, (CAP, LANES)).astype(bf16)
    for at in range(0, width, 512):
        part = jnp.dot(placing_ref[...], tok_ref[:, at : at + 512], preferred_element_type=f32)
        part = part.astype(bf16)
        for k in range(n_expert):
            pieces[k][:, at : at + 512] = part[k * CAP : (k + 1) * CAP]


def place(me, route, prob, tokens, n_expert):
    count, width = tokens.shape
    piece = jax.ShapeDtypeStruct((CAP, width + LANES), bf16)
    outs = pl.pallas_call(
        functools.partial(place_kernel, n_expert),
        out_shape=[jax.ShapeDtypeStruct((n_expert * CAP, count), bf16)] + [piece] * n_expert,
        in_specs=[SMEM, VMEM, VMEM, VMEM],
        out_specs=[VMEM] * (n_expert + 1),
        cost_estimate=cost(2 * n_expert * CAP * count * width, 2 * MIB),
    )(me.reshape(1), route.reshape(1, count), prob.reshape(1, count), tokens)
    return outs[0], outs[1:]


def split_kernel(*refs):
    half = len(refs) // 3
    for i in range(half):
        whole = refs[i][...]
        high = whole.astype(bf16)
        refs[half + 2 * i][...] = high
        refs[half + 2 * i + 1][...] = (whole - high.astype(f32)).astype(bf16)


def split_weights(*weights):
    depth, units = weights[0].shape
    spec = pl.BlockSpec((BLOCK, units), lambda i: (i, 0))
    return pl.pallas_call(
        split_kernel,
        grid=(depth // BLOCK,),
        out_shape=[jax.ShapeDtypeStruct((depth, units), bf16)] * (2 * len(weights)),
        in_specs=[spec] * len(weights),
        out_specs=[spec] * (2 * len(weights)),
        cost_estimate=cost(0, 8 * depth * units * len(weights)),
    )(*weights)


def forward_kernel(n_expert, *refs):
    pieces = refs[:n_expert]
    gate_hi, gate_lo, up_hi, up_lo = refs[n_expert : n_expert + 4]
    act_ref, slope_ref, hidden_ref, share_ref = refs[n_expert + 4 : n_expert + 8]
    rows, gate_sum, up_sum = refs[n_expert + 8 :]
    step = pl.program_id(0)
    width = pieces[0].shape[1] - LANES

    @pl.when(step == 0)
    def _():
        gate_sum[...] = jnp.zeros_like(gate_sum)
        up_sum[...] = jnp.zeros_like(up_sum)

    for k in range(n_expert):
        rows[k * CAP : (k + 1) * CAP, :] = pieces[k][:, pl.ds(pl.multiple_of(step * BLOCK, BLOCK), BLOCK)]
    row = rows[...]
    gate_sum[...] += jnp.dot(row, gate_hi[...], preferred_element_type=f32) + jnp.dot(
        row, gate_lo[...], preferred_element_type=f32
    )
    up_sum[...] += jnp.dot(row, up_hi[...], preferred_element_type=f32) + jnp.dot(
        row, up_lo[...], preferred_element_type=f32
    )

    @pl.when(step == pl.num_programs(0) - 1)
    def _():
        for k in range(n_expert):
            part = slice(k * CAP, (k + 1) * CAP)
            prob = pieces[k][:, width:].astype(f32)[:, :1]
            gate = gate_sum[part, :]
            up = up_sum[part, :]
            sig = jax.nn.sigmoid(gate)
            act = gate * sig
            hidden = act * up
            act_ref[part, :] = prob * act
            slope_ref[part, :] = prob * (up * sig * (1.0 + gate * (1.0 - sig)))
            hidden_ref[part, :] = hidden
            share_ref[part, :] = (prob * hidden).astype(bf16)


def forward(pieces, weights):
    n_expert = len(pieces)
    depth, units = weights[0].shape
    count = n_expert * CAP
    whole = pl.BlockSpec((CAP, depth + LANES), lambda i: (0, 0))
    block = pl.BlockSpec((BLOCK, units), lambda i: (i, 0))
    out = pl.BlockSpec((count, units), lambda i: (0, 0))
    shape = jax.ShapeDtypeStruct((count, units), f32)
    return pl.pallas_call(
        functools.partial(forward_kernel, n_expert),
        grid=(depth // BLOCK,),
        out_shape=[shape] * 3 + [jax.ShapeDtypeStruct((count, units), bf16)],
        in_specs=[whole] * n_expert + [block] * 4,
        out_specs=[out] * 4,
        scratch_shapes=[
            pltpu.VMEM((count, BLOCK), bf16),
            pltpu.VMEM((count, units), f32),
            pltpu.VMEM((count, units), f32),
        ],
        compiler_params=pltpu.CompilerParams(vmem_limit_bytes=24 * MIB),
        cost_estimate=cost(8 * count * depth * units, 8 * depth * units),
    )(*pieces, *weights)


def backward_kernel(n_expert, *refs):
    pieces = refs[:n_expert]
    down_hi, down_lo, act_ref, slope_ref, hidden_ref = refs[n_expert : n_expert + 5]
    high_ref, low_ref, prob_ref = refs[n_expert + 5 : n_expert + 8]
    rows, back_sum = refs[n_expert + 8 :]
    step = pl.program_id(0)
    units = down_hi.shape[1]

    @pl.when(step == 0)
    def _():
        back_sum[...] = jnp.zeros_like(back_sum)

    for k in range(n_expert):
        rows[k * CAP : (k + 1) * CAP, :] = pieces[k][:, pl.ds(pl.multiple_of(step * BLOCK, BLOCK), BLOCK)]
    row = rows[...]
    back_sum[...] += jnp.dot(row, down_hi[...], preferred_element_type=f32) + jnp.dot(
        row, down_lo[...], preferred_element_type=f32
    )

    @pl.when(step == pl.num_programs(0) - 1)
    def _():
        for k in range(n_expert):
            part = slice(k * CAP, (k + 1) * CAP)
            back = back_sum[part, :]
            total = jnp.sum(hidden_ref[part, :] * back, axis=1, keepdims=True)
            prob_ref[part, :] = jnp.broadcast_to(total, (CAP, LANES))
            for at, factor in ((0, slope_ref), (units, act_ref)):
                grad = factor[part, :] * back
                high = grad.astype(bf16)
                high_ref[part, at : at + units] = high
                low_ref[part, at : at + units] = (grad - high.astype(f32)).astype(bf16)


def backward(pieces, weights, act, slope, hidden):
    n_expert = len(pieces)
    depth, units = weights[0].shape
    count = n_expert * CAP
    whole = pl.BlockSpec((CAP, depth), lambda i: (0, 0))
    block = pl.BlockSpec((BLOCK, units), lambda i: (i, 0))

    def full(width):
        return pl.BlockSpec((count, width), lambda i: (0, 0))

    return pl.pallas_call(
        functools.partial(backward_kernel, n_expert),
        grid=(depth // BLOCK,),
        out_shape=[jax.ShapeDtypeStruct((count, 2 * units), bf16)] * 2
        + [jax.ShapeDtypeStruct((count, LANES), f32)],
        in_specs=[whole] * n_expert + [block] * 2 + [full(units)] * 3,
        out_specs=[full(2 * units)] * 2 + [full(LANES)],
        scratch_shapes=[pltpu.VMEM((count, BLOCK), bf16), pltpu.VMEM((count, units), f32)],
        compiler_params=pltpu.CompilerParams(vmem_limit_bytes=24 * MIB),
        cost_estimate=cost(4 * count * depth * units, 4 * depth * units),
    )(*pieces, *weights, act, slope, hidden)


def input_kernel(n_expert, *refs):
    high_ref, low_ref, prob_ref, gate_hi, gate_lo, up_hi, up_lo = refs[:7]
    pieces = refs[7:]
    step = pl.program_id(0)
    units = gate_hi.shape[1]
    width = pieces[0].shape[1] - LANES

    def against(left, right):
        return lax.dot_general(left, right, (((1,), (1,)), ((), ())), preferred_element_type=f32)

    grad_hi, grad_lo = high_ref[:, :units], low_ref[:, :units]
    total = against(grad_hi, gate_hi[...]) + against(grad_lo, gate_hi[...])
    total += against(grad_hi, gate_lo[...])
    grad_hi, grad_lo = high_ref[:, units:], low_ref[:, units:]
    total += against(grad_hi, up_hi[...]) + against(grad_lo, up_hi[...])
    total += against(grad_hi, up_lo[...])
    for k in range(n_expert):
        part = slice(k * CAP, (k + 1) * CAP)
        here = pl.ds(pl.multiple_of(step * BLOCK, BLOCK), BLOCK)
        pieces[k][:, here] = total[part].astype(pieces[k].dtype)

    @pl.when(step == 0)
    def _():
        for k in range(n_expert):
            pieces[k][:, width:] = prob_ref[k * CAP : (k + 1) * CAP, :].astype(pieces[k].dtype)


def input_gradient(high, low, prob_part, weights, n_expert, back_type):
    depth, units = weights[0].shape
    count = n_expert * CAP
    block = pl.BlockSpec((BLOCK, units), lambda i: (i, 0))

    def full(rows, width):
        return pl.BlockSpec((rows, width), lambda i: (0, 0))

    return pl.pallas_call(
        functools.partial(input_kernel, n_expert),
        grid=(depth // BLOCK,),
        out_shape=[jax.ShapeDtypeStruct((CAP, depth + LANES), back_type)] * n_expert,
        in_specs=[full(count, 2 * units)] * 2 + [full(count, LANES)] + [block] * 4,
        out_specs=[full(CAP, depth + LANES)] * n_expert,
        compiler_params=pltpu.CompilerParams(vmem_limit_bytes=24 * MIB),
        cost_estimate=cost(12 * count * depth * units, 8 * depth * units),
    )(high, low, prob_part, *weights)


def take_kernel(n_expert, placing_ref, *refs):
    pieces = refs[:n_expert]
    out_ref, prob_ref, rows = refs[n_expert:]
    count, width = out_ref.shape
    exact = rows.dtype != bf16
    for k in range(n_expert):
        rows[k * CAP : (k + 1) * CAP, :] = pieces[k][...]
    placing = placing_ref[...].astype(rows.dtype)
    for at in range(0, width, 512):
        part = lax.dot_general(
            placing, rows[:, at : at + 512], (((0,), (0,)), ((), ())),
            precision=highest if exact else None, preferred_element_type=f32,
        )
        out_ref[:, at : at + 512] = part.astype(bf16)
    column = rows[:, width:].astype(f32)[:, :1]
    prob_ref[...] = jnp.sum(placing_ref[...].astype(f32) * column, axis=0, keepdims=True).astype(bf16)


def take(placing, pieces):
    n_expert = len(pieces)
    count = placing.shape[1]
    width = pieces[0].shape[1] - LANES
    grad, prob = pl.pallas_call(
        functools.partial(take_kernel, n_expert),
        out_shape=[
            jax.ShapeDtypeStruct((count, width), bf16),
            jax.ShapeDtypeStruct((1, count), bf16),
        ],
        in_specs=[VMEM] * (n_expert + 1),
        out_specs=[VMEM] * 2,
        scratch_shapes=[pltpu.VMEM((n_expert * CAP, width + LANES), pieces[0].dtype)],
        compiler_params=pltpu.CompilerParams(vmem_limit_bytes=32 * MIB),
        cost_estimate=cost(2 * n_expert * CAP * count * width, 2 * MIB),
    )(placing, *pieces)
    return grad, prob.reshape(count)


def in_plane(rows, terms):
    size = lax.axis_size("dp")
    share = rows.shape[1] // size
    units = terms.shape[1]
    at = lax.axis_index("dp")
    chips = range(size // 2)

    def part(to):
        return lax.dynamic_slice_in_dim(rows, to * share, share, axis=1)

    theirs = flipped(jnp.stack([part((at ^ 1) ^ (2 * k)) for k in chips]), "dp", 1)
    payload = [
        jnp.concatenate([part(at ^ (2 * k)), theirs[k], terms], axis=1) for k in chips
    ]
    got = [payload[0]] + [flipped(payload[k], "dp", 2 * k) for k in chips[1:]]
    own_cols = jnp.concatenate([g[:, :share] for g in got])
    other_cols = jnp.concatenate([g[:, share : 2 * share] for g in got])
    own_terms = jnp.concatenate([g[:, 2 * share :] for g in got])
    other_terms = flipped(own_terms, "dp", 1)
    return own_cols, other_cols, own_terms, other_terms


def over_rows(own_cols, other_cols, own_terms, other_terms, scale):
    def dot(cols, term):
        return lax.dot_general(cols, term, (((0,), (0,)), ((), ())), preferred_element_type=f32)

    return ((dot(own_cols, own_terms) + dot(other_cols, other_terms)) * scale)[None]


def shards(tokens, cotangent, route, prob, w_gate, w_up, w_down):
    n_expert = lax.axis_size("expert")
    n_dp = lax.axis_size("dp")
    width = tokens.shape[1]
    units = w_gate.shape[2]
    scale = 1.0 / math.sqrt(tokens.shape[0] * n_dp * n_expert)
    back_type = bf16 if n_expert == HOT else f32
    me = lax.axis_index("expert").astype(i32)

    placing, slot_tok = place(me, route, prob, tokens, n_expert)
    tok_pieces = [slot_tok[0]] + [shifted(slot_tok[k], "expert", k) for k in range(1, n_expert)]

    weights, _ = lax.optimization_barrier(((w_gate[0], w_up[0], w_down[0]), slot_tok[0]))
    gate_hi, gate_lo, up_hi, up_lo, down_hi, down_lo = split_weights(*weights)
    (late_cot, _) = lax.optimization_barrier((cotangent, down_lo))
    slot_cot = jnp.dot(placing, late_cot, preferred_element_type=f32).astype(bf16)
    slot_cot = slot_cot.reshape(n_expert, CAP, width)
    cot_pieces = [slot_cot[0]] + [shifted(slot_cot[k], "expert", k) for k in range(1, n_expert)]

    act, slope, hidden, weighted = forward(tok_pieces, (gate_hi, gate_lo, up_hi, up_lo))
    row_tok = jnp.concatenate([p[:, :width] for p in tok_pieces])
    tok_own, tok_other, weighted_own, weighted_other = in_plane(row_tok, weighted)

    cot_pieces, act = lax.optimization_barrier((cot_pieces, act))
    high, low, prob_part = backward(cot_pieces, (down_hi, down_lo), act, slope, hidden)
    row_cot = jnp.concatenate(cot_pieces)
    cot_own, cot_other, grads_own, grads_other = in_plane(row_cot, high)
    back = input_gradient(
        high, low, prob_part, (gate_hi, gate_lo, up_hi, up_lo), n_expert, back_type
    )
    home = [back[0]] + [shifted(back[k], "expert", n_expert - k) for k in range(1, n_expert)]
    grad_input, grad_prob = take(placing, home)

    return (
        grad_input,
        grad_prob,
        over_rows(tok_own, tok_other, grads_own[:, :units], grads_other[:, :units], scale),
        over_rows(tok_own, tok_other, grads_own[:, units:], grads_other[:, units:], scale),
        over_rows(cot_own, cot_other, weighted_own, weighted_other, scale),
    )


def solution(mesh):
    placed = (
        P(("dp", "expert"), None),
        P(("dp", "expert"), None),
        P(("dp", "expert"), None),
        P(("dp", "expert")),
        P("expert", None, None),
        P("expert", None, None),
        P("expert", None, None),
    )
    return jax.shard_map(
        shards,
        mesh=mesh,
        in_specs=placed,
        out_specs=(
            P(("dp", "expert"), None),
            P(("dp", "expert")),
            P("expert", "dp", None),
            P("expert", "dp", None),
            P("expert", "dp", None),
        ),
        check_vma=False,
    )
```

```python
import functools
import math

import jax
import jax.numpy as jnp
from jax import lax
from jax.experimental import pallas as pl
from jax.experimental.pallas import tpu as pltpu
from jax.sharding import PartitionSpec as P

HOT = 4
CAP = 48
LANES = 128
BLOCK = 256
MIB = 1 << 20

highest = lax.Precision.HIGHEST
f32 = jnp.float32
bf16 = jnp.bfloat16
i32 = jnp.int32
VMEM = pl.BlockSpec(memory_space=pltpu.VMEM)
SMEM = pl.BlockSpec(memory_space=pltpu.SMEM)
PARAMS = pltpu.CompilerParams(vmem_limit_bytes=14 * MIB)
SMALL = pl.CostEstimate(flops=0, bytes_accessed=1024, transcendentals=0)


def shifted(values, axis, by):
    size = lax.axis_size(axis)
    return lax.ppermute(values, axis, [(i, (i + by) % size) for i in range(size)])


def flipped(values, axis, mask):
    size = lax.axis_size(axis)
    return lax.ppermute(values, axis, [(i, i ^ mask) for i in range(size)])


def cut_kernel(count, at_ref, *refs):
    pieces, (mine, theirs) = refs[:count], refs[count:]
    chips, _, share = mine.shape
    for k in range(chips):
        for target, core in ((mine, at_ref[0]), (theirs, 1 - at_ref[0])):
            start = pl.multiple_of((2 * k + core) * share, share)
            for i in range(count):
                target[k, i * CAP : (i + 1) * CAP, :] = pieces[i][:, pl.ds(start, share)]


def cut(pieces, width):
    size = lax.axis_size("dp")
    share = width // size
    core = lax.axis_index("dp").astype(i32) % 2
    chips = size // 2
    if share % LANES:
        rows = jnp.concatenate([p[:, :width] for p in pieces])

        def part(which):
            return lax.dynamic_slice_in_dim(rows, which * share, share, axis=1)

        return (
            jnp.stack([part(2 * k + core) for k in range(chips)]),
            jnp.stack([part(2 * k + 1 - core) for k in range(chips)]),
        )
    shape = jax.ShapeDtypeStruct((chips, len(pieces) * CAP, share), bf16)
    return pl.pallas_call(
        functools.partial(cut_kernel, len(pieces)),
        out_shape=[shape, shape],
        in_specs=[SMEM] + [VMEM] * len(pieces),
        out_specs=[VMEM] * 2,
        compiler_params=PARAMS,
        cost_estimate=SMALL,
    )(core.reshape(1), *pieces)


def place_kernel(n_expert, me_ref, route_ref, prob_ref, tok_ref, cot_ref, placing_ref, *refs):
    quarters = n_expert // HOT
    count, width = tok_ref.shape
    pieces, cot_pieces = refs[:n_expert], refs[n_expert:]
    route = route_ref[...]
    hot = (route == lax.broadcasted_iota(i32, (16, count), 0)).astype(f32)
    before = lax.broadcasted_iota(i32, (count, count), 0) < lax.broadcasted_iota(i32, (count, count), 1)
    earlier = jnp.dot(hot.astype(bf16), before.astype(f32).astype(bf16), preferred_element_type=f32)
    rank = jnp.sum(earlier * hot, axis=0, keepdims=True).astype(i32)
    slot = lax.broadcasted_iota(i32, (CAP, count), 0)
    prob = prob_ref[...].astype(f32)
    for k in range(n_expert):
        owner = lax.rem(me_ref[0] + k, n_expert) // quarters
        block = jnp.where((route == owner) & (rank == slot), 1.0, 0.0)
        placing_ref[k * CAP : (k + 1) * CAP, :] = block.astype(bf16)
        slot_prob = jnp.sum(block * prob, axis=1, keepdims=True)
        pieces[k][:, width:] = jnp.broadcast_to(slot_prob, (CAP, LANES)).astype(bf16)
    for source, targets in ((tok_ref, pieces), (cot_ref, cot_pieces)):
        for at in range(0, width, 512):
            part = jnp.dot(placing_ref[...], source[:, at : at + 512], preferred_element_type=f32)
            part = part.astype(bf16)
            for k in range(n_expert):
                targets[k][:, at : at + 512] = part[k * CAP : (k + 1) * CAP]


def place(me, route, prob, tokens, cotangent, n_expert):
    count, width = tokens.shape
    outs = pl.pallas_call(
        functools.partial(place_kernel, n_expert),
        out_shape=[jax.ShapeDtypeStruct((n_expert * CAP, count), bf16)]
        + [jax.ShapeDtypeStruct((CAP, width + LANES), bf16)] * n_expert
        + [jax.ShapeDtypeStruct((CAP, width), bf16)] * n_expert,
        in_specs=[SMEM] + [VMEM] * 4,
        out_specs=[VMEM] * (2 * n_expert + 1),
        compiler_params=PARAMS,
        cost_estimate=SMALL,
    )(me.reshape(1), route.reshape(1, count), prob.reshape(1, count), tokens, cotangent)
    return outs[0], outs[1 : n_expert + 1], outs[n_expert + 1 :]


def halves(whole):
    high = whole.astype(bf16)
    return high, (whole - high.astype(f32)).astype(bf16)


def fill(rows, pieces, width):
    for k, piece in enumerate(pieces):
        rows[k * CAP : (k + 1) * CAP, :] = piece[:, :width]


def times_weight(rows, weight, total):
    depth = weight.shape[0]
    for at in range(0, depth, BLOCK):
        high, low = halves(weight[at : at + BLOCK, :])
        row = rows[:, at : at + BLOCK]
        part = jnp.dot(row, high, preferred_element_type=f32)
        part += jnp.dot(row, low, preferred_element_type=f32)
        if at == 0:
            total[...] = part
        else:
            total[...] += part


def gate_factors(gate, up, prob):
    sig = jax.nn.sigmoid(gate)
    act = gate * sig
    hidden = act * up
    return prob * act, prob * (up * sig * (1.0 + gate * (1.0 - sig))), hidden


def forward_kernel(count, *refs):
    pieces, (w_gate, w_up, act_ref, slope_ref, hidden_ref, share_ref, rows, gate_sum, up_sum) = (
        refs[:count], refs[count:]
    )
    fill(rows, pieces, rows.shape[1])
    times_weight(rows, w_gate, gate_sum)
    times_weight(rows, w_up, up_sum)
    for k in range(count):
        part = slice(k * CAP, (k + 1) * CAP)
        prob = pieces[k][:, rows.shape[1] :].astype(f32)[:, :1]
        act, slope, hidden = gate_factors(gate_sum[part, :], up_sum[part, :], prob)
        act_ref[part, :] = act
        slope_ref[part, :] = slope
        hidden_ref[part, :] = hidden
        share_ref[part, :] = (prob * hidden).astype(bf16)


def forward(pieces, w_gate, w_up):
    count = len(pieces)
    depth, units = w_gate.shape
    shape = jax.ShapeDtypeStruct((count * CAP, units), f32)
    return pl.pallas_call(
        functools.partial(forward_kernel, count),
        out_shape=[shape] * 3 + [jax.ShapeDtypeStruct((count * CAP, units), bf16)],
        in_specs=[VMEM] * (count + 2),
        out_specs=[VMEM] * 4,
        scratch_shapes=[
            pltpu.VMEM((count * CAP, depth), bf16),
            pltpu.VMEM((count * CAP, units), f32),
            pltpu.VMEM((count * CAP, units), f32),
        ],
        compiler_params=PARAMS,
        cost_estimate=SMALL,
    )(*pieces, w_gate, w_up)


def backward_kernel(count, *refs):
    pieces, (w_down, act_ref, slope_ref, hidden_ref, high_ref, low_ref, prob_ref, rows, back_sum) = (
        refs[:count], refs[count:]
    )
    units = w_down.shape[1]
    fill(rows, pieces, rows.shape[1])
    times_weight(rows, w_down, back_sum)
    for k in range(count):
        part = slice(k * CAP, (k + 1) * CAP)
        back = back_sum[part, :]
        total = jnp.sum(hidden_ref[part, :] * back, axis=1, keepdims=True)
        prob_ref[part, :] = jnp.broadcast_to(total, (CAP, LANES))
        for at, factor in ((0, slope_ref), (units, act_ref)):
            high, low = halves(factor[part, :] * back)
            high_ref[part, at : at + units] = high
            low_ref[part, at : at + units] = low


def backward(pieces, w_down, act, slope, hidden):
    count = len(pieces)
    depth, units = w_down.shape
    rows = count * CAP
    return pl.pallas_call(
        functools.partial(backward_kernel, count),
        out_shape=[jax.ShapeDtypeStruct((rows, 2 * units), bf16)] * 2
        + [jax.ShapeDtypeStruct((rows, LANES), f32)],
        in_specs=[VMEM] * (count + 4),
        out_specs=[VMEM] * 3,
        scratch_shapes=[pltpu.VMEM((rows, depth), bf16), pltpu.VMEM((rows, units), f32)],
        compiler_params=PARAMS,
        cost_estimate=SMALL,
    )(*pieces, w_down, act, slope, hidden)


def against(left, right):
    return lax.dot_general(left, right, (((1,), (1,)), ((), ())), preferred_element_type=f32)


def write_input(high_ref, low_ref, prob_ref, w_gate, w_up, pieces):
    depth, units = w_gate.shape
    for at in range(0, depth, BLOCK):
        total = None
        for start, weight in ((0, w_gate), (units, w_up)):
            weight_hi, weight_lo = halves(weight[at : at + BLOCK, :])
            grad_hi = high_ref[:, start : start + units]
            grad_lo = low_ref[:, start : start + units]
            part = against(grad_hi, weight_hi) + against(grad_lo, weight_hi)
            part += against(grad_hi, weight_lo)
            total = part if total is None else total + part
        for k, piece in enumerate(pieces):
            piece[:, at : at + BLOCK] = total[k * CAP : (k + 1) * CAP].astype(piece.dtype)
    for k, piece in enumerate(pieces):
        piece[:, depth:] = prob_ref[k * CAP : (k + 1) * CAP, :].astype(piece.dtype)


def input_kernel(high_ref, low_ref, prob_ref, w_gate, w_up, *pieces):
    write_input(high_ref, low_ref, prob_ref, w_gate, w_up, pieces)


def input_gradient(high, low, prob_part, w_gate, w_up, back_type):
    depth = w_gate.shape[0]
    count = high.shape[0] // CAP
    return pl.pallas_call(
        input_kernel,
        out_shape=[jax.ShapeDtypeStruct((CAP, depth + LANES), back_type)] * count,
        in_specs=[VMEM] * 5,
        out_specs=[VMEM] * count,
        compiler_params=PARAMS,
        cost_estimate=SMALL,
    )(high, low, prob_part, w_gate, w_up)


def local_kernel(
    tok_ref, cot_ref, w_gate, w_up, w_down, terms_ref, piece_ref,
    rows, gate_sum, up_sum, back_sum, low_ref, prob_ref,
):
    units = w_gate.shape[1]
    width = rows.shape[1]
    fill(rows, (tok_ref,), width)
    times_weight(rows, w_gate, gate_sum)
    times_weight(rows, w_up, up_sum)
    times_weight(cot_ref, w_down, back_sum)
    prob = tok_ref[:, width:].astype(f32)[:, :1]
    act, slope, hidden = gate_factors(gate_sum[...], up_sum[...], prob)
    back = back_sum[...]
    total = jnp.sum(hidden * back, axis=1, keepdims=True)
    prob_ref[...] = jnp.broadcast_to(total, prob_ref.shape)
    for at, factor in ((0, slope), (units, act)):
        high, low = halves(factor * back)
        terms_ref[:, at : at + units] = high
        low_ref[:, at : at + units] = low
    terms_ref[:, 2 * units :] = (prob * hidden).astype(bf16)
    write_input(terms_ref, low_ref, prob_ref, w_gate, w_up, (piece_ref,))


def local_rows(tok, cot, w_gate, w_up, w_down, back_type):
    depth, units = w_gate.shape
    return pl.pallas_call(
        local_kernel,
        out_shape=[
            jax.ShapeDtypeStruct((CAP, 3 * units), bf16),
            jax.ShapeDtypeStruct((CAP, depth + LANES), back_type),
        ],
        in_specs=[VMEM] * 5,
        out_specs=[VMEM] * 2,
        scratch_shapes=[pltpu.VMEM((CAP, depth), bf16)]
        + [pltpu.VMEM((CAP, units), f32)] * 3
        + [pltpu.VMEM((CAP, 2 * units), bf16), pltpu.VMEM((CAP, LANES), f32)],
        compiler_params=PARAMS,
        cost_estimate=SMALL,
    )(tok, cot, w_gate, w_up, w_down)


def take_kernel(n_expert, placing_ref, *refs):
    pieces = refs[:n_expert]
    out_ref, prob_ref, rows = refs[n_expert:]
    count, width = out_ref.shape
    exact = rows.dtype != bf16
    for k in range(n_expert):
        rows[k * CAP : (k + 1) * CAP, :] = pieces[k][...]
    placing = placing_ref[...].astype(rows.dtype)
    for at in range(0, width, 512):
        part = lax.dot_general(
            placing, rows[:, at : at + 512], (((0,), (0,)), ((), ())),
            precision=highest if exact else None, preferred_element_type=f32,
        )
        out_ref[:, at : at + 512] = part.astype(bf16)
    column = rows[:, width:].astype(f32)[:, :1]
    prob_ref[...] = jnp.sum(placing_ref[...].astype(f32) * column, axis=0, keepdims=True).astype(bf16)


def take(placing, pieces):
    n_expert = len(pieces)
    count = placing.shape[1]
    width = pieces[0].shape[1] - LANES
    grad, prob = pl.pallas_call(
        functools.partial(take_kernel, n_expert),
        out_shape=[
            jax.ShapeDtypeStruct((count, width), bf16),
            jax.ShapeDtypeStruct((1, count), bf16),
        ],
        in_specs=[VMEM] * (n_expert + 1),
        out_specs=[VMEM] * 2,
        scratch_shapes=[pltpu.VMEM((n_expert * CAP, width + LANES), pieces[0].dtype)],
        compiler_params=pltpu.CompilerParams(vmem_limit_bytes=32 * MIB) if pieces[0].dtype != bf16 else PARAMS,
        cost_estimate=SMALL,
    )(placing, *pieces)
    return grad, prob.reshape(count)


def over_chips(mine, theirs, terms):
    chips, rows, share = mine.shape
    payload = jnp.concatenate(
        [mine, theirs, jnp.broadcast_to(terms[None], (chips,) + terms.shape)], axis=2
    )
    groups = [[2 * k + core for k in range(chips)] for core in range(2)]
    got = lax.all_to_all(
        payload, "dp", split_axis=0, concat_axis=0, tiled=True, axis_index_groups=groups
    ).reshape(chips * rows, -1)
    return got[:, :share], got[:, share : 2 * share], got[:, 2 * share :]


def shards(tokens, cotangent, route, prob, w_gate, w_up, w_down):
    n_expert = lax.axis_size("expert")
    n_dp = lax.axis_size("dp")
    width = tokens.shape[1]
    units = w_gate.shape[2]
    share = width // n_dp
    scale = 1.0 / math.sqrt(tokens.shape[0] * n_dp * n_expert)
    back_type = bf16 if n_expert == HOT else f32
    me = lax.axis_index("expert").astype(i32)
    gate, up, down = w_gate[0], w_up[0], w_down[0]
    ahead = range(1, n_expert)

    placing, slot_tok, slot_cot = place(me, route, prob, tokens, cotangent, n_expert)
    tok = [shifted(slot_tok[k], "expert", k) for k in ahead]

    local_cut = [cut((piece,), width) for piece in (slot_tok[0], slot_cot[0])]
    local_theirs = flipped(jnp.concatenate([c[1] for c in local_cut], axis=2), "dp", 1)
    own_cot, local_theirs = lax.optimization_barrier((slot_cot[0], local_theirs))
    local_terms, local_back = local_rows(slot_tok[0], own_cot, gate, up, down, back_type)
    cot = []
    for k in ahead:
        late, tok[k - 1], local_terms = lax.optimization_barrier(
            (slot_cot[k], tok[k - 1], local_terms)
        )
        cot.append(shifted(late, "expert", k))
    local_mine = jnp.concatenate([c[0] for c in local_cut], axis=2)
    local_own_cols, local_other_cols, local_own = over_chips(local_mine, local_theirs, local_terms)
    local_other = flipped(local_own, "dp", 1)

    mine, theirs = cut(tok, width)
    theirs = flipped(theirs, "dp", 1)
    tok, theirs, local_own = lax.optimization_barrier((tok, theirs, local_own))
    act, slope, hidden, weighted = forward(tok, gate, up)
    tok_own, tok_other, weighted_own = over_chips(mine, theirs, weighted)

    cot, act, local_other = lax.optimization_barrier((cot, act, local_other))
    mine, theirs = cut(cot, width)
    theirs = flipped(theirs, "dp", 1)
    high, low, prob_part = backward(cot, down, act, slope, hidden)
    high, theirs = lax.optimization_barrier((high, theirs))
    back = list(input_gradient(high, low, prob_part, gate, up, back_type))
    back[-1], weighted_own = lax.optimization_barrier((back[-1], weighted_own))
    home = [local_back] + [shifted(back[k - 1], "expert", n_expert - k) for k in ahead]
    weighted_other = flipped(weighted_own, "dp", 1)
    cot_own, cot_other, grads_own = over_chips(mine, theirs, high)
    grads_other = flipped(grads_own, "dp", 1)
    grad_input, grad_prob = take(placing, home)

    def dot(cols, term):
        return lax.dot_general(cols, term, (((0,), (0,)), ((), ())), preferred_element_type=f32)

    def over_rows(first, local, remote):
        local_cols = slice(first * share, (first + 1) * share)
        total = dot(local_own_cols[:, local_cols], local[0])
        total += dot(local_other_cols[:, local_cols], local[1])
        for cols, term in remote:
            total += dot(cols, term)
        return (total * scale)[None]

    def part(values, at):
        return values[:, at * units : (at + 1) * units]

    results = [
        over_rows(
            0,
            (part(local_own, at), part(local_other, at)),
            ((tok_own, part(grads_own, at)), (tok_other, part(grads_other, at))),
        )
        for at in range(2)
    ]
    results.append(
        over_rows(
            1,
            (part(local_own, 2), part(local_other, 2)),
            ((cot_own, weighted_own), (cot_other, weighted_other)),
        )
    )
    return (grad_input, grad_prob, *results)


def solution(mesh):
    placed = (
        P(("dp", "expert"), None),
        P(("dp", "expert"), None),
        P(("dp", "expert"), None),
        P(("dp", "expert")),
        P("expert", None, None),
        P("expert", None, None),
        P("expert", None, None),
    )
    return jax.shard_map(
        shards,
        mesh=mesh,
        in_specs=placed,
        out_specs=(
            P(("dp", "expert"), None),
            P(("dp", "expert")),
            P("expert", "dp", None),
            P("expert", "dp", None),
            P("expert", "dp", None),
        ),
        check_vma=False,
    )
```

```python
import functools
import math

import jax
import jax.numpy as jnp
from jax import lax
from jax.experimental import pallas as pl
from jax.experimental.pallas import tpu as pltpu
from jax.sharding import PartitionSpec as P

HOT = 4
CAP = 48
LANES = 128
BLOCK = 256
MIB = 1 << 20

highest = lax.Precision.HIGHEST
f32 = jnp.float32
bf16 = jnp.bfloat16
i32 = jnp.int32
VMEM = pl.BlockSpec(memory_space=pltpu.VMEM)
SMEM = pl.BlockSpec(memory_space=pltpu.SMEM)
HBM = pl.BlockSpec(memory_space=pltpu.HBM)
PARAMS = pltpu.CompilerParams(vmem_limit_bytes=14 * MIB)
ALONE = pltpu.CompilerParams(vmem_limit_bytes=52 * MIB)
SMALL = pl.CostEstimate(flops=0, bytes_accessed=1024, transcendentals=0)


def shifted(values, axis, by):
    size = lax.axis_size(axis)
    return lax.ppermute(values, axis, [(i, (i + by) % size) for i in range(size)])


def flipped(values, axis, mask):
    size = lax.axis_size(axis)
    return lax.ppermute(values, axis, [(i, i ^ mask) for i in range(size)])


def cut_kernel(count, at_ref, *refs):
    pieces, theirs = refs[:count], refs[count]
    chips, _, double = theirs.shape
    share = double // 2
    width = 2 * chips * share
    for k in range(chips):
        start = pl.multiple_of((at_ref[0] ^ (2 * k + 1)) * share, share)
        for i in range(count):
            part = slice(i * CAP, (i + 1) * CAP)
            theirs[k, part, :share] = pieces[i][:, pl.ds(start, share)]
            theirs[k, part, share:] = pieces[i][:, pl.ds(width + start, share)]


def pack_kernel(count, at_ref, *refs):
    pieces, theirs, terms, payload = refs[:count], refs[count], refs[count + 1], refs[count + 2 :]
    chips, _, double = theirs.shape
    share = double // 2
    width = 2 * chips * share
    for k in range(chips):
        start = pl.multiple_of((at_ref[0] ^ (2 * k)) * share, share)
        for i in range(count):
            part = slice(i * CAP, (i + 1) * CAP)
            payload[k][part, :share] = pieces[i][:, pl.ds(start, share)]
            payload[k][part, share:double] = pieces[i][:, pl.ds(width + start, share)]
        payload[k][:, double : 2 * double] = theirs[k]
        payload[k][:, 2 * double :] = terms[...]


def slices_of(pieces, width, share, flips):
    at = lax.axis_index("dp").astype(i32)
    rows = jnp.concatenate(pieces)
    return [
        jnp.concatenate(
            [
                lax.dynamic_slice_in_dim(rows, base + (at ^ flip) * share, share, axis=1)
                for base in (0, width)
            ],
            axis=1,
        )
        for flip in flips
    ]


def cut(pieces, width):
    size = lax.axis_size("dp")
    share = width // size
    if share % LANES:
        return jnp.stack(slices_of(pieces, width, share, range(1, size, 2)))
    return pl.pallas_call(
        functools.partial(cut_kernel, len(pieces)),
        out_shape=jax.ShapeDtypeStruct((size // 2, len(pieces) * CAP, 2 * share), bf16),
        in_specs=[SMEM] + [VMEM] * len(pieces),
        out_specs=VMEM,
        compiler_params=PARAMS,
        cost_estimate=SMALL,
    )(lax.axis_index("dp").astype(i32).reshape(1), *pieces)


def pack(pieces, theirs, terms, width):
    size = lax.axis_size("dp")
    share = width // size
    if share % LANES:
        own = slices_of(pieces, width, share, range(0, size, 2))
        return [jnp.concatenate([own[k], theirs[k], terms], axis=1) for k in range(size // 2)]
    shape = jax.ShapeDtypeStruct((terms.shape[0], 4 * share + terms.shape[1]), bf16)
    return pl.pallas_call(
        functools.partial(pack_kernel, len(pieces)),
        out_shape=[shape] * (size // 2),
        in_specs=[SMEM] + [VMEM] * (len(pieces) + 2),
        out_specs=[VMEM] * (size // 2),
        compiler_params=PARAMS,
        cost_estimate=SMALL,
    )(lax.axis_index("dp").astype(i32).reshape(1), *pieces, theirs, terms)


def sum_kernel(chips, share, units, scale, first, *refs):
    got, others = refs[:chips], refs[chips]
    past = () if first else refs[chips + 1 : chips + 4]
    outs = refs[-5:-2]
    cols, terms = refs[-2:]
    rows = got[0].shape[0]
    for k in range(chips):
        for core in range(2):
            part = slice((2 * k + core) * rows, (2 * k + core + 1) * rows)
            cols[part, :] = got[k][:, 2 * core * share : 2 * (core + 1) * share]
        terms[2 * k * rows : (2 * k + 1) * rows, :] = got[k][:, 4 * share :]
        terms[(2 * k + 1) * rows : (2 * k + 2) * rows, :] = others[k * rows : (k + 1) * rows, :]
    for i in range(3):
        column = share if i == 2 else 0
        total = lax.dot_general(
            cols[:, column : column + share], terms[:, i * units : (i + 1) * units],
            (((0,), (0,)), ((), ())), preferred_element_type=f32,
        )
        if not first:
            total += past[i][...]
        outs[i][...] = total if scale is None else total * scale


def weight_sums(got, others, past, share, scale):
    chips = len(got)
    rows = got[0].shape[0]
    units = others.shape[1] // 3
    if share % LANES:
        wide = [jnp.concatenate([g[:, 2 * c * share : 2 * (c + 1) * share] for g in got]) for c in range(2)]
        near = jnp.concatenate([g[:, 4 * share :] for g in got])
        sums = []
        for i in range(3):
            total = 0.0 if past is None else past[i]
            for cols, terms in zip(wide, (near, others)):
                column = share if i == 2 else 0
                total += lax.dot_general(
                    cols[:, column : column + share], terms[:, i * units : (i + 1) * units],
                    (((0,), (0,)), ((), ())), preferred_element_type=f32,
                )
            sums.append(total if scale is None else total * scale)
        return sums
    past = [] if past is None else list(past)
    return pl.pallas_call(
        functools.partial(sum_kernel, chips, share, units, scale, not past),
        out_shape=[jax.ShapeDtypeStruct((share, units), f32)] * 3,
        in_specs=[VMEM] * (chips + 1 + len(past)),
        out_specs=[VMEM] * 3,
        scratch_shapes=[
            pltpu.VMEM((2 * chips * rows, 2 * share), bf16),
            pltpu.VMEM((2 * chips * rows, 3 * units), bf16),
        ],
        compiler_params=PARAMS,
        cost_estimate=SMALL,
    )(*got, others, *past)


def place_kernel(n_expert, me_ref, route_ref, prob_ref, tok_ref, cot_ref, placing_ref, *pieces):
    quarters = n_expert // HOT
    count, width = tok_ref.shape
    route = route_ref[...]
    hot = (route == lax.broadcasted_iota(i32, (16, count), 0)).astype(f32)
    before = lax.broadcasted_iota(i32, (count, count), 0) < lax.broadcasted_iota(i32, (count, count), 1)
    earlier = jnp.dot(hot.astype(bf16), before.astype(f32).astype(bf16), preferred_element_type=f32)
    rank = jnp.sum(earlier * hot, axis=0, keepdims=True).astype(i32)
    slot = lax.broadcasted_iota(i32, (CAP, count), 0)
    prob = prob_ref[...].astype(f32)
    for k in range(n_expert):
        owner = lax.rem(me_ref[0] + k, n_expert) // quarters
        block = jnp.where((route == owner) & (rank == slot), 1.0, 0.0)
        placing_ref[k * CAP : (k + 1) * CAP, :] = block.astype(bf16)
        slot_prob = jnp.sum(block * prob, axis=1, keepdims=True)
        pieces[k][:, 2 * width :] = jnp.broadcast_to(slot_prob, (CAP, LANES)).astype(bf16)
    for start, source in ((0, tok_ref), (width, cot_ref)):
        for at in range(0, width, 512):
            part = jnp.dot(placing_ref[...], source[:, at : at + 512], preferred_element_type=f32)
            part = part.astype(bf16)
            for k in range(n_expert):
                pieces[k][:, start + at : start + at + 512] = part[k * CAP : (k + 1) * CAP]


def place(me, route, prob, tokens, cotangent, n_expert):
    count, width = tokens.shape
    outs = pl.pallas_call(
        functools.partial(place_kernel, n_expert),
        out_shape=[jax.ShapeDtypeStruct((n_expert * CAP, count), bf16)]
        + [jax.ShapeDtypeStruct((CAP, 2 * width + LANES), bf16)] * n_expert,
        in_specs=[SMEM] + [VMEM] * 4,
        out_specs=[VMEM] * (n_expert + 1),
        compiler_params=PARAMS,
        cost_estimate=SMALL,
    )(me.reshape(1), route.reshape(1, count), prob.reshape(1, count), tokens, cotangent)
    return outs[0], outs[1:]


def halves(whole):
    high = whole.astype(bf16)
    return high, (whole - high.astype(f32)).astype(bf16)


def weight_scratch(count, depth, units):
    return [
        pltpu.VMEM((count, depth, units), f32),
        pltpu.SemaphoreType.DMA((count, depth // BLOCK)),
    ]


def fetch(weights, buffer, arrived):
    copies = []
    for at in range(weights[0].shape[0] // BLOCK):
        here = slice(at * BLOCK, (at + 1) * BLOCK)
        for i, weight in enumerate(weights):
            copy = pltpu.make_async_copy(weight.at[here, :], buffer.at[i, here, :], arrived.at[i, at])
            copy.start()
            copies.append(copy)
    return copies


def times_weights(factors, buffer, copies):
    depth = buffer.shape[1]
    for at in range(depth // BLOCK):
        here = slice(at * BLOCK, (at + 1) * BLOCK)
        for i, (rows, total) in enumerate(factors):
            copies[at * len(factors) + i].wait()
            high, low = halves(buffer[i, here, :])
            row = rows[:, here]
            part = jnp.dot(row, high, preferred_element_type=f32)
            part += jnp.dot(row, low, preferred_element_type=f32)
            if at == 0:
                total[...] = part
            else:
                total[...] += part


def gate_factors(gate, up, prob):
    sig = jax.nn.sigmoid(gate)
    act = gate * sig
    hidden = act * up
    return prob * act, prob * (up * sig * (1.0 + gate * (1.0 - sig))), hidden


def against(left, right):
    return lax.dot_general(left, right, (((1,), (1,)), ((), ())), preferred_element_type=f32)


def chunk_kernel(count, *refs):
    pieces, weights, terms_ref = refs[:count], refs[count : count + 3], refs[count + 3]
    outs = refs[count + 4 : 2 * count + 4]
    tok, cot, gate_sum, up_sum, back_sum, low_ref, buffer, arrived = refs[2 * count + 4 :]
    depth, units = weights[0].shape
    copies = fetch(weights, buffer, arrived)
    for k, piece in enumerate(pieces):
        part = slice(k * CAP, (k + 1) * CAP)
        tok[part, :] = piece[:, :depth]
        cot[part, :] = piece[:, depth : 2 * depth]
    times_weights(((tok, gate_sum), (tok, up_sum), (cot, back_sum)), buffer, copies)
    for k, piece in enumerate(pieces):
        part = slice(k * CAP, (k + 1) * CAP)
        prob = piece[:, 2 * depth :].astype(f32)[:, :1]
        act, slope, hidden = gate_factors(gate_sum[part, :], up_sum[part, :], prob)
        back = back_sum[part, :]
        total = jnp.sum(hidden * back, axis=1, keepdims=True)
        outs[k][:, depth:] = jnp.broadcast_to(total, (CAP, LANES)).astype(outs[k].dtype)
        for at, factor in ((0, slope), (units, act)):
            high, low = halves(factor * back)
            terms_ref[part, at : at + units] = high
            low_ref[part, at : at + units] = low
        terms_ref[part, 2 * units :] = (prob * hidden).astype(bf16)
    for at in range(0, depth, BLOCK):
        total = None
        for i in range(2):
            high, low = halves(buffer[i, at : at + BLOCK, :])
            grad_hi = terms_ref[:, i * units : (i + 1) * units]
            grad_lo = low_ref[:, i * units : (i + 1) * units]
            part = against(grad_hi, high) + against(grad_lo, high) + against(grad_hi, low)
            total = part if total is None else total + part
        for k, out in enumerate(outs):
            out[:, at : at + BLOCK] = total[k * CAP : (k + 1) * CAP].astype(out.dtype)


def chunk_rows(pieces, weights, back_type):
    count = len(pieces)
    depth, units = weights[0].shape
    rows = count * CAP
    outs = pl.pallas_call(
        functools.partial(chunk_kernel, count),
        out_shape=[jax.ShapeDtypeStruct((rows, 3 * units), bf16)]
        + [jax.ShapeDtypeStruct((CAP, depth + LANES), back_type)] * count,
        in_specs=[VMEM] * count + [HBM] * 3,
        out_specs=[VMEM] * (count + 1),
        scratch_shapes=[pltpu.VMEM((rows, depth), bf16)] * 2
        + [pltpu.VMEM((rows, units), f32)] * 3
        + [pltpu.VMEM((rows, 2 * units), bf16)]
        + weight_scratch(3, depth, units),
        compiler_params=ALONE,
        cost_estimate=pl.CostEstimate(flops=36 * 192 * depth * units, bytes_accessed=MIB, transcendentals=0),
    )(*pieces, *weights)
    return outs[0], outs[1:]


def take_kernel(n_expert, placing_ref, *refs):
    pieces = refs[:n_expert]
    out_ref, prob_ref, rows = refs[n_expert:]
    count, width = out_ref.shape
    exact = rows.dtype != bf16
    for k in range(n_expert):
        rows[k * CAP : (k + 1) * CAP, :] = pieces[k][...]
    placing = placing_ref[...].astype(rows.dtype)
    for at in range(0, width, 512):
        part = lax.dot_general(
            placing, rows[:, at : at + 512], (((0,), (0,)), ((), ())),
            precision=highest if exact else None, preferred_element_type=f32,
        )
        out_ref[:, at : at + 512] = part.astype(bf16)
    column = rows[:, width:].astype(f32)[:, :1]
    prob_ref[...] = jnp.sum(placing_ref[...].astype(f32) * column, axis=0, keepdims=True).astype(bf16)


def take(placing, pieces):
    n_expert = len(pieces)
    count = placing.shape[1]
    width = pieces[0].shape[1] - LANES
    grad, prob = pl.pallas_call(
        functools.partial(take_kernel, n_expert),
        out_shape=[
            jax.ShapeDtypeStruct((count, width), bf16),
            jax.ShapeDtypeStruct((1, count), bf16),
        ],
        in_specs=[VMEM] * (n_expert + 1),
        out_specs=[VMEM] * 2,
        scratch_shapes=[pltpu.VMEM((n_expert * CAP, width + LANES), pieces[0].dtype)],
        compiler_params=pltpu.CompilerParams(vmem_limit_bytes=32 * MIB) if pieces[0].dtype != bf16 else PARAMS,
        cost_estimate=SMALL,
    )(placing, *pieces)
    return grad, prob.reshape(count)


def shards(tokens, cotangent, route, prob, w_gate, w_up, w_down):
    n_expert = lax.axis_size("expert")
    n_dp = lax.axis_size("dp")
    width = tokens.shape[1]
    share = width // n_dp
    scale = 1.0 / math.sqrt(tokens.shape[0] * n_dp * n_expert)
    back_type = bf16 if n_expert == HOT else f32
    me = lax.axis_index("expert").astype(i32)
    weights = (w_gate[0], w_up[0], w_down[0])
    chips = range(n_dp // 2)
    home = [None] * n_expert

    def exchange(payload):
        return [payload[0]] + [flipped(payload[k], "dp", 2 * k) for k in chips[1:]]

    def swap(got):
        return flipped(jnp.concatenate([g[:, 4 * share :] for g in got]), "dp", 1)

    def give_back(home, shifts, back):
        home = list(home)
        for i, k in enumerate(shifts):
            home[k] = shifted(back[i], "expert", n_expert - k)
        return home

    placing, pieces = place(me, route, prob, tokens, cotangent, n_expert)
    odd = list(range(1, n_expert, 2))
    even = list(range(2, n_expert, 2))
    first = [shifted(pieces[k], "expert", k) for k in odd]

    theirs = flipped(cut(pieces[:1], width), "dp", 1)
    terms, back = chunk_rows(pieces[:1], weights, back_type)
    home[0] = back[0]
    payload = pack(pieces[:1], theirs, terms, width)
    got_local = exchange(payload)
    late, first, got_local = lax.optimization_barrier(
        ([pieces[k] for k in even], first, got_local)
    )
    second = [shifted(piece, "expert", k) for piece, k in zip(late, even)]

    theirs = flipped(cut(first, width), "dp", 1)
    terms, back = chunk_rows(first, weights, back_type)
    got_first = exchange(pack(first, theirs, terms, width))
    home = give_back(home, odd[:-1], back[:-1])
    last = back[-1]
    sums = weight_sums(got_local, swap(got_local), None, share, None)

    second, sums, home, last = lax.optimization_barrier((second, sums, home, last))
    home = give_back(home, odd[-1:], [last])
    theirs = flipped(cut(second, width), "dp", 1)
    terms, back = chunk_rows(second, weights, back_type)
    home = give_back(home, even, back)
    payload, got_first = lax.optimization_barrier((pack(second, theirs, terms, width), got_first))
    sums = weight_sums(got_first, swap(got_first), sums, share, None)
    got_second, home, sums = lax.optimization_barrier((exchange(payload), home, sums))
    sums = weight_sums(got_second, swap(got_second), sums, share, scale)

    grad_input, grad_prob = take(placing, home)
    return (grad_input, grad_prob, *[total[None] for total in sums])


def solution(mesh):
    placed = (
        P(("dp", "expert"), None),
        P(("dp", "expert"), None),
        P(("dp", "expert"), None),
        P(("dp", "expert")),
        P("expert", None, None),
        P("expert", None, None),
        P("expert", None, None),
    )
    return jax.shard_map(
        shards,
        mesh=mesh,
        in_specs=placed,
        out_specs=(
            P(("dp", "expert"), None),
            P(("dp", "expert")),
            P("expert", "dp", None),
            P("expert", "dp", None),
            P("expert", "dp", None),
        ),
        check_vma=False,
    )
```

```python
import functools
import math

import jax
import jax.numpy as jnp
from jax import lax
from jax.experimental import pallas as pl
from jax.experimental.pallas import tpu as pltpu
from jax.sharding import PartitionSpec as P

HOT = 4
CAP = 48
LANES = 128
BLOCK = 256
MIB = 1 << 20

highest = lax.Precision.HIGHEST
f32 = jnp.float32
bf16 = jnp.bfloat16
i32 = jnp.int32
VMEM = pl.BlockSpec(memory_space=pltpu.VMEM)
SMEM = pl.BlockSpec(memory_space=pltpu.SMEM)
HBM = pl.BlockSpec(memory_space=pltpu.HBM)
PARAMS = pltpu.CompilerParams(vmem_limit_bytes=14 * MIB)
ALONE = pltpu.CompilerParams(vmem_limit_bytes=52 * MIB)
SMALL = pl.CostEstimate(flops=0, bytes_accessed=1024, transcendentals=0)


def shifted(values, axis, by):
    size = lax.axis_size(axis)
    return lax.ppermute(values, axis, [(i, (i + by) % size) for i in range(size)])


def flipped(values, axis, mask):
    size = lax.axis_size(axis)
    return lax.ppermute(values, axis, [(i, i ^ mask) for i in range(size)])


def cut_kernel(count, at_ref, *refs):
    pieces, theirs = refs[:count], refs[count]
    chips, _, double = theirs.shape
    share = double // 2
    width = 2 * chips * share
    for k in range(chips):
        start = pl.multiple_of((at_ref[0] ^ (2 * k + 1)) * share, share)
        for i in range(count):
            part = slice(i * CAP, (i + 1) * CAP)
            theirs[k, part, :share] = pieces[i][:, pl.ds(start, share)]
            theirs[k, part, share:] = pieces[i][:, pl.ds(width + start, share)]


def pack_kernel(count, at_ref, *refs):
    pieces, theirs, terms, payload = refs[:count], refs[count], refs[count + 1], refs[count + 2 :]
    chips, _, double = theirs.shape
    share = double // 2
    width = 2 * chips * share
    for k in range(chips):
        start = pl.multiple_of((at_ref[0] ^ (2 * k)) * share, share)
        for i in range(count):
            part = slice(i * CAP, (i + 1) * CAP)
            payload[k][part, :share] = pieces[i][:, pl.ds(start, share)]
            payload[k][part, share:double] = pieces[i][:, pl.ds(width + start, share)]
        payload[k][:, double : 2 * double] = theirs[k]
        payload[k][:, 2 * double :] = terms[...]


def slices_of(pieces, width, share, flips):
    at = lax.axis_index("dp").astype(i32)
    rows = jnp.concatenate(pieces)
    return [
        jnp.concatenate(
            [
                lax.dynamic_slice_in_dim(rows, base + (at ^ flip) * share, share, axis=1)
                for base in (0, width)
            ],
            axis=1,
        )
        for flip in flips
    ]


def cut(pieces, width):
    size = lax.axis_size("dp")
    share = width // size
    if share % LANES:
        return jnp.stack(slices_of(pieces, width, share, range(1, size, 2)))
    return pl.pallas_call(
        functools.partial(cut_kernel, len(pieces)),
        out_shape=jax.ShapeDtypeStruct((size // 2, len(pieces) * CAP, 2 * share), bf16),
        in_specs=[SMEM] + [VMEM] * len(pieces),
        out_specs=VMEM,
        compiler_params=PARAMS,
        cost_estimate=SMALL,
    )(lax.axis_index("dp").astype(i32).reshape(1), *pieces)


def pack(pieces, theirs, terms, width):
    return list(packed(pieces, theirs, terms, width))


def packed(pieces, theirs, terms, width):
    size = lax.axis_size("dp")
    share = width // size
    if share % LANES:
        own = slices_of(pieces, width, share, range(0, size, 2))
        return [jnp.concatenate([own[k], theirs[k], terms], axis=1) for k in range(size // 2)]
    shape = jax.ShapeDtypeStruct((terms.shape[0], 4 * share + terms.shape[1]), bf16)
    return pl.pallas_call(
        functools.partial(pack_kernel, len(pieces)),
        out_shape=[shape] * (size // 2),
        in_specs=[SMEM] + [VMEM] * (len(pieces) + 2),
        out_specs=[VMEM] * (size // 2),
        compiler_params=PARAMS,
        cost_estimate=SMALL,
    )(lax.axis_index("dp").astype(i32).reshape(1), *pieces, theirs, terms)


def sum_kernel(chips, share, units, scale, first, *refs):
    got, others = refs[:chips], refs[chips]
    past = () if first else refs[chips + 1 : chips + 4]
    outs = refs[-5:-2]
    cols, terms = refs[-2:]
    rows = got[0].shape[0]
    for k in range(chips):
        for core in range(2):
            part = slice((2 * k + core) * rows, (2 * k + core + 1) * rows)
            cols[part, :] = got[k][:, 2 * core * share : 2 * (core + 1) * share]
        terms[2 * k * rows : (2 * k + 1) * rows, :] = got[k][:, 4 * share :]
        terms[(2 * k + 1) * rows : (2 * k + 2) * rows, :] = others[k * rows : (k + 1) * rows, :]
    for i in range(3):
        column = share if i == 2 else 0
        total = lax.dot_general(
            cols[:, column : column + share], terms[:, i * units : (i + 1) * units],
            (((0,), (0,)), ((), ())), preferred_element_type=f32,
        )
        if not first:
            total += past[i][...]
        outs[i][...] = total if scale is None else total * scale


def weight_sums(got, others, past, share, scale):
    chips = len(got)
    rows = got[0].shape[0]
    units = others.shape[1] // 3
    if share % LANES:
        wide = [jnp.concatenate([g[:, 2 * c * share : 2 * (c + 1) * share] for g in got]) for c in range(2)]
        near = jnp.concatenate([g[:, 4 * share :] for g in got])
        sums = []
        for i in range(3):
            total = 0.0 if past is None else past[i]
            for cols, terms in zip(wide, (near, others)):
                column = share if i == 2 else 0
                total += lax.dot_general(
                    cols[:, column : column + share], terms[:, i * units : (i + 1) * units],
                    (((0,), (0,)), ((), ())), preferred_element_type=f32,
                )
            sums.append(total if scale is None else total * scale)
        return sums
    past = [] if past is None else list(past)
    return pl.pallas_call(
        functools.partial(sum_kernel, chips, share, units, scale, not past),
        out_shape=[jax.ShapeDtypeStruct((share, units), f32)] * 3,
        in_specs=[VMEM] * (chips + 1 + len(past)),
        out_specs=[VMEM] * 3,
        scratch_shapes=[
            pltpu.VMEM((2 * chips * rows, 2 * share), bf16),
            pltpu.VMEM((2 * chips * rows, 3 * units), bf16),
        ],
        compiler_params=PARAMS,
        cost_estimate=SMALL,
    )(*got, others, *past)


def place_kernel(n_expert, me_ref, route_ref, prob_ref, tok_ref, cot_ref, placing_ref, *pieces):
    quarters = n_expert // HOT
    count, width = tok_ref.shape
    route = route_ref[...]
    hot = (route == lax.broadcasted_iota(i32, (16, count), 0)).astype(f32)
    before = lax.broadcasted_iota(i32, (count, count), 0) < lax.broadcasted_iota(i32, (count, count), 1)
    earlier = jnp.dot(hot.astype(bf16), before.astype(f32).astype(bf16), preferred_element_type=f32)
    rank = jnp.sum(earlier * hot, axis=0, keepdims=True).astype(i32)
    slot = lax.broadcasted_iota(i32, (CAP, count), 0)
    prob = prob_ref[...].astype(f32)
    for k in range(n_expert):
        owner = lax.rem(me_ref[0] + k, n_expert) // quarters
        block = jnp.where((route == owner) & (rank == slot), 1.0, 0.0)
        placing_ref[k * CAP : (k + 1) * CAP, :] = block.astype(bf16)
        slot_prob = jnp.sum(block * prob, axis=1, keepdims=True)
        pieces[k][:, 2 * width :] = jnp.broadcast_to(slot_prob, (CAP, LANES)).astype(bf16)
    for start, source in ((0, tok_ref), (width, cot_ref)):
        for at in range(0, width, 512):
            part = jnp.dot(placing_ref[...], source[:, at : at + 512], preferred_element_type=f32)
            part = part.astype(bf16)
            for k in range(n_expert):
                pieces[k][:, start + at : start + at + 512] = part[k * CAP : (k + 1) * CAP]


def place(me, route, prob, tokens, cotangent, n_expert):
    count, width = tokens.shape
    outs = pl.pallas_call(
        functools.partial(place_kernel, n_expert),
        out_shape=[jax.ShapeDtypeStruct((n_expert * CAP, count), bf16)]
        + [jax.ShapeDtypeStruct((CAP, 2 * width + LANES), bf16)] * n_expert,
        in_specs=[SMEM] + [VMEM] * 4,
        out_specs=[VMEM] * (n_expert + 1),
        cost_estimate=SMALL,
    )(me.reshape(1), route.reshape(1, count), prob.reshape(1, count), tokens, cotangent)
    return outs[0], outs[1:]


def halves(whole):
    high = whole.astype(bf16)
    return high, (whole - high.astype(f32)).astype(bf16)


def weight_scratch(count, depth, units):
    return [
        pltpu.VMEM((count, depth, units), f32),
        pltpu.SemaphoreType.DMA((count, depth // BLOCK)),
    ]


def fetch(weights, buffer, arrived):
    copies = []
    for at in range(weights[0].shape[0] // BLOCK):
        here = slice(at * BLOCK, (at + 1) * BLOCK)
        for i, weight in enumerate(weights):
            copy = pltpu.make_async_copy(weight.at[here, :], buffer.at[i, here, :], arrived.at[i, at])
            copy.start()
            copies.append(copy)
    return copies


def times_weights(factors, buffer, copies):
    depth = buffer.shape[1]
    for at in range(depth // BLOCK):
        here = slice(at * BLOCK, (at + 1) * BLOCK)
        for i, (rows, total) in enumerate(factors):
            copies[at * len(factors) + i].wait()
            high, low = halves(buffer[i, here, :])
            row = rows[:, here]
            part = jnp.dot(row, high, preferred_element_type=f32)
            part += jnp.dot(row, low, preferred_element_type=f32)
            if at == 0:
                total[...] = part
            else:
                total[...] += part


def gate_factors(gate, up, prob):
    sig = jax.nn.sigmoid(gate)
    act = gate * sig
    hidden = act * up
    return prob * act, prob * (up * sig * (1.0 + gate * (1.0 - sig))), hidden


def against(left, right):
    return lax.dot_general(left, right, (((1,), (1,)), ((), ())), preferred_element_type=f32)


def chunk_kernel(count, *refs):
    pieces, weights, terms_ref = refs[:count], refs[count : count + 3], refs[count + 3]
    outs = refs[count + 4 : 2 * count + 4]
    tok, cot, gate_sum, up_sum, back_sum, low_ref, buffer, arrived = refs[2 * count + 4 :]
    depth, units = weights[0].shape
    copies = fetch(weights, buffer, arrived)
    for k, piece in enumerate(pieces):
        part = slice(k * CAP, (k + 1) * CAP)
        tok[part, :] = piece[:, :depth]
        cot[part, :] = piece[:, depth : 2 * depth]
    times_weights(((tok, gate_sum), (tok, up_sum), (cot, back_sum)), buffer, copies)
    for k, piece in enumerate(pieces):
        part = slice(k * CAP, (k + 1) * CAP)
        prob = piece[:, 2 * depth :].astype(f32)[:, :1]
        act, slope, hidden = gate_factors(gate_sum[part, :], up_sum[part, :], prob)
        back = back_sum[part, :]
        total = jnp.sum(hidden * back, axis=1, keepdims=True)
        outs[k][:, depth:] = jnp.broadcast_to(total, (CAP, LANES)).astype(outs[k].dtype)
        for at, factor in ((0, slope), (units, act)):
            high, low = halves(factor * back)
            terms_ref[part, at : at + units] = high
            low_ref[part, at : at + units] = low
        terms_ref[part, 2 * units :] = (prob * hidden).astype(bf16)
    for at in range(0, depth, BLOCK):
        total = None
        for i in range(2):
            high, low = halves(buffer[i, at : at + BLOCK, :])
            grad_hi = terms_ref[:, i * units : (i + 1) * units]
            grad_lo = low_ref[:, i * units : (i + 1) * units]
            part = against(high, grad_hi) + against(high, grad_lo) + against(low, grad_hi)
            total = part if total is None else total + part
        total = total.T
        for k, out in enumerate(outs):
            out[:, at : at + BLOCK] = total[k * CAP : (k + 1) * CAP].astype(out.dtype)


def chunk_rows(pieces, weights, back_type):
    count = len(pieces)
    depth, units = weights[0].shape
    rows = count * CAP
    outs = pl.pallas_call(
        functools.partial(chunk_kernel, count),
        out_shape=[jax.ShapeDtypeStruct((rows, 3 * units), bf16)]
        + [jax.ShapeDtypeStruct((CAP, depth + LANES), back_type)] * count,
        in_specs=[VMEM] * count + [HBM] * 3,
        out_specs=[VMEM] * (count + 1),
        scratch_shapes=[pltpu.VMEM((rows, depth), bf16)] * 2
        + [pltpu.VMEM((rows, units), f32)] * 3
        + [pltpu.VMEM((rows, 2 * units), bf16)]
        + weight_scratch(3, depth, units),
        compiler_params=ALONE,
        cost_estimate=pl.CostEstimate(flops=36 * 192 * depth * units, bytes_accessed=MIB, transcendentals=0),
    )(*pieces, *weights)
    return outs[0], outs[1:]


def take_kernel(n_expert, placing_ref, *refs):
    pieces = refs[:n_expert]
    out_ref, prob_ref, rows = refs[n_expert:]
    count, width = out_ref.shape
    exact = rows.dtype != bf16
    for k in range(n_expert):
        rows[k * CAP : (k + 1) * CAP, :] = pieces[k][...]
    placing = placing_ref[...].astype(rows.dtype)
    for at in range(0, width, 512):
        part = lax.dot_general(
            placing, rows[:, at : at + 512], (((0,), (0,)), ((), ())),
            precision=highest if exact else None, preferred_element_type=f32,
        )
        out_ref[:, at : at + 512] = part.astype(bf16)
    column = rows[:, width:].astype(f32)[:, :1]
    prob_ref[...] = jnp.sum(placing_ref[...].astype(f32) * column, axis=0, keepdims=True).astype(bf16)


def take(placing, pieces):
    n_expert = len(pieces)
    count = placing.shape[1]
    width = pieces[0].shape[1] - LANES
    grad, prob = pl.pallas_call(
        functools.partial(take_kernel, n_expert),
        out_shape=[
            jax.ShapeDtypeStruct((count, width), bf16),
            jax.ShapeDtypeStruct((1, count), bf16),
        ],
        in_specs=[VMEM] * (n_expert + 1),
        out_specs=[VMEM] * 2,
        scratch_shapes=[pltpu.VMEM((n_expert * CAP, width + LANES), pieces[0].dtype)],
        compiler_params=pltpu.CompilerParams(vmem_limit_bytes=32 * MIB) if pieces[0].dtype != bf16 else PARAMS,
        cost_estimate=SMALL,
    )(placing, *pieces)
    return grad, prob.reshape(count)


def shards(tokens, cotangent, route, prob, w_gate, w_up, w_down):
    n_expert = lax.axis_size("expert")
    n_dp = lax.axis_size("dp")
    width = tokens.shape[1]
    share = width // n_dp
    scale = 1.0 / math.sqrt(tokens.shape[0] * n_dp * n_expert)
    back_type = bf16 if n_expert == HOT else f32
    me = lax.axis_index("expert").astype(i32)
    weights = (w_gate[0], w_up[0], w_down[0])
    chips = range(n_dp // 2)
    home = [None] * n_expert

    def exchange(payload):
        return [payload[0]] + [flipped(payload[k], "dp", 2 * k) for k in chips[1:]]

    def swap(got):
        return flipped(jnp.concatenate([g[:, 4 * share :] for g in got]), "dp", 1)

    def give_back(home, shifts, back):
        home = list(home)
        for i, k in enumerate(shifts):
            home[k] = shifted(back[i], "expert", n_expert - k)
        return home

    placing, pieces = place(me, route, prob, tokens, cotangent, n_expert)
    odd = list(range(1, n_expert, 2))
    even = list(range(2, n_expert, 2))
    first = [shifted(pieces[k], "expert", k) for k in odd]

    theirs = flipped(cut(pieces[:1], width), "dp", 1)
    terms, back = chunk_rows(pieces[:1], weights, back_type)
    home[0] = back[0]
    payload = pack(pieces[:1], theirs, terms, width)
    late, _ = lax.optimization_barrier(([pieces[k] for k in even], payload[0]))
    second = [shifted(piece, "expert", k) for piece, k in zip(late, even)]
    payload[-1], first = lax.optimization_barrier((payload[-1], first))
    got_local = exchange(payload)

    theirs = flipped(cut(first, width), "dp", 1)
    terms, back = chunk_rows(first, weights, back_type)
    payload = pack(first, theirs, terms, width)
    got_first = exchange(payload)

    second, back, got_local, _ = lax.optimization_barrier((second, back, got_local, payload))
    home = give_back(home, odd, back)
    theirs = flipped(cut(second, width), "dp", 1)
    terms, back = chunk_rows(second, weights, back_type)
    sums = weight_sums(got_local, swap(got_local), None, share, None)
    payload, got_first, sums, back, home = lax.optimization_barrier(
        (pack(second, theirs, terms, width), got_first, sums, back, home)
    )
    home = give_back(home, even, back)
    got_second = exchange(payload)
    sums = weight_sums(got_first, swap(got_first), sums, share, None)
    got_second, home, sums = lax.optimization_barrier((got_second, home, sums))
    sums = weight_sums(got_second, swap(got_second), sums, share, scale)

    grad_input, grad_prob = take(placing, home)
    return (grad_input, grad_prob, *[total[None] for total in sums])


def solution(mesh):
    placed = (
        P(("dp", "expert"), None),
        P(("dp", "expert"), None),
        P(("dp", "expert"), None),
        P(("dp", "expert")),
        P("expert", None, None),
        P("expert", None, None),
        P("expert", None, None),
    )
    return jax.shard_map(
        shards,
        mesh=mesh,
        in_specs=placed,
        out_specs=(
            P(("dp", "expert"), None),
            P(("dp", "expert")),
            P("expert", "dp", None),
            P("expert", "dp", None),
            P("expert", "dp", None),
        ),
        check_vma=False,
    )
```

```python
import functools
import math

import jax
import jax.numpy as jnp
from jax import lax
from jax.experimental import pallas as pl
from jax.experimental.pallas import tpu as pltpu
from jax.sharding import PartitionSpec as P

HOT = 4
CAP = 48
LANES = 128
BLOCK = 256
MIB = 1 << 20

highest = lax.Precision.HIGHEST
f32 = jnp.float32
bf16 = jnp.bfloat16
i32 = jnp.int32
VMEM = pl.BlockSpec(memory_space=pltpu.VMEM)
SMEM = pl.BlockSpec(memory_space=pltpu.SMEM)
HBM = pl.BlockSpec(memory_space=pltpu.HBM)
PARAMS = pltpu.CompilerParams(vmem_limit_bytes=14 * MIB)
ALONE = pltpu.CompilerParams(vmem_limit_bytes=52 * MIB)
SMALL = pl.CostEstimate(flops=0, bytes_accessed=1024, transcendentals=0)


def shifted(values, axis, by):
    size = lax.axis_size(axis)
    return lax.ppermute(values, axis, [(i, (i + by) % size) for i in range(size)])


def flipped(values, axis, mask):
    size = lax.axis_size(axis)
    return lax.ppermute(values, axis, [(i, i ^ mask) for i in range(size)])


def cut_kernel(count, at_ref, *refs):
    pieces, theirs = refs[:count], refs[count]
    chips, _, double = theirs.shape
    share = double // 2
    width = 2 * chips * share
    for k in range(chips):
        start = pl.multiple_of((at_ref[0] ^ (2 * k + 1)) * share, share)
        for i in range(count):
            part = slice(i * CAP, (i + 1) * CAP)
            theirs[k, part, :share] = pieces[i][:, pl.ds(start, share)]
            theirs[k, part, share:] = pieces[i][:, pl.ds(width + start, share)]


def pack_kernel(count, at_ref, *refs):
    pieces, theirs, terms, payload = refs[:count], refs[count], refs[count + 1], refs[count + 2 :]
    chips, _, double = theirs.shape
    share = double // 2
    width = 2 * chips * share
    for k in range(chips):
        start = pl.multiple_of((at_ref[0] ^ (2 * k)) * share, share)
        for i in range(count):
            part = slice(i * CAP, (i + 1) * CAP)
            payload[k][part, :share] = pieces[i][:, pl.ds(start, share)]
            payload[k][part, share:double] = pieces[i][:, pl.ds(width + start, share)]
        payload[k][:, double : 2 * double] = theirs[k]
        payload[k][:, 2 * double :] = terms[...]


def slices_of(pieces, width, share, flips):
    at = lax.axis_index("dp").astype(i32)
    rows = jnp.concatenate(pieces)
    return [
        jnp.concatenate(
            [
                lax.dynamic_slice_in_dim(rows, base + (at ^ flip) * share, share, axis=1)
                for base in (0, width)
            ],
            axis=1,
        )
        for flip in flips
    ]


def cut(pieces, width):
    size = lax.axis_size("dp")
    share = width // size
    if share % LANES:
        return jnp.stack(slices_of(pieces, width, share, range(1, size, 2)))
    return pl.pallas_call(
        functools.partial(cut_kernel, len(pieces)),
        out_shape=jax.ShapeDtypeStruct((size // 2, len(pieces) * CAP, 2 * share), bf16),
        in_specs=[SMEM] + [VMEM] * len(pieces),
        out_specs=VMEM,
        compiler_params=PARAMS,
        cost_estimate=SMALL,
    )(lax.axis_index("dp").astype(i32).reshape(1), *pieces)


def pack(pieces, theirs, terms, width):
    return list(packed(pieces, theirs, terms, width))


def packed(pieces, theirs, terms, width):
    size = lax.axis_size("dp")
    share = width // size
    if share % LANES:
        own = slices_of(pieces, width, share, range(0, size, 2))
        return [jnp.concatenate([own[k], theirs[k], terms], axis=1) for k in range(size // 2)]
    shape = jax.ShapeDtypeStruct((terms.shape[0], 4 * share + terms.shape[1]), bf16)
    return pl.pallas_call(
        functools.partial(pack_kernel, len(pieces)),
        out_shape=[shape] * (size // 2),
        in_specs=[SMEM] + [VMEM] * (len(pieces) + 2),
        out_specs=[VMEM] * (size // 2),
        compiler_params=PARAMS,
        cost_estimate=SMALL,
    )(lax.axis_index("dp").astype(i32).reshape(1), *pieces, theirs, terms)


def sum_kernel(chips, share, units, scale, first, *refs):
    got, others = refs[:chips], refs[chips]
    past = () if first else refs[chips + 1 : chips + 4]
    outs = refs[-5:-2]
    cols, terms = refs[-2:]
    rows = got[0].shape[0]
    for k in range(chips):
        for core in range(2):
            part = slice((2 * k + core) * rows, (2 * k + core + 1) * rows)
            cols[part, :] = got[k][:, 2 * core * share : 2 * (core + 1) * share]
        terms[2 * k * rows : (2 * k + 1) * rows, :] = got[k][:, 4 * share :]
        terms[(2 * k + 1) * rows : (2 * k + 2) * rows, :] = others[k * rows : (k + 1) * rows, :]
    for i in range(3):
        column = share if i == 2 else 0
        total = lax.dot_general(
            cols[:, column : column + share], terms[:, i * units : (i + 1) * units],
            (((0,), (0,)), ((), ())), preferred_element_type=f32,
        )
        if not first:
            total += past[i][...]
        outs[i][...] = total if scale is None else total * scale


def weight_sums(got, others, past, share, scale):
    chips = len(got)
    rows = got[0].shape[0]
    units = others.shape[1] // 3
    if share % LANES:
        wide = [jnp.concatenate([g[:, 2 * c * share : 2 * (c + 1) * share] for g in got]) for c in range(2)]
        near = jnp.concatenate([g[:, 4 * share :] for g in got])
        sums = []
        for i in range(3):
            total = 0.0 if past is None else past[i]
            for cols, terms in zip(wide, (near, others)):
                column = share if i == 2 else 0
                total += lax.dot_general(
                    cols[:, column : column + share], terms[:, i * units : (i + 1) * units],
                    (((0,), (0,)), ((), ())), preferred_element_type=f32,
                )
            sums.append(total if scale is None else total * scale)
        return sums
    past = [] if past is None else list(past)
    return pl.pallas_call(
        functools.partial(sum_kernel, chips, share, units, scale, not past),
        out_shape=[jax.ShapeDtypeStruct((share, units), f32)] * 3,
        in_specs=[VMEM] * (chips + 1 + len(past)),
        out_specs=[VMEM] * 3,
        scratch_shapes=[
            pltpu.VMEM((2 * chips * rows, 2 * share), bf16),
            pltpu.VMEM((2 * chips * rows, 3 * units), bf16),
        ],
        compiler_params=PARAMS,
        cost_estimate=SMALL,
    )(*got, others, *past)


def place_kernel(n_expert, me_ref, route_ref, prob_ref, tok_ref, cot_ref, placing_ref, *pieces):
    quarters = n_expert // HOT
    count, width = tok_ref.shape
    route = route_ref[...]
    hot = (route == lax.broadcasted_iota(i32, (16, count), 0)).astype(f32)
    before = lax.broadcasted_iota(i32, (count, count), 0) < lax.broadcasted_iota(i32, (count, count), 1)
    earlier = jnp.dot(hot.astype(bf16), before.astype(f32).astype(bf16), preferred_element_type=f32)
    rank = jnp.sum(earlier * hot, axis=0, keepdims=True).astype(i32)
    slot = lax.broadcasted_iota(i32, (CAP, count), 0)
    prob = prob_ref[...].astype(f32)
    for k in range(n_expert):
        owner = lax.rem(me_ref[0] + k, n_expert) // quarters
        block = jnp.where((route == owner) & (rank == slot), 1.0, 0.0)
        placing_ref[k * CAP : (k + 1) * CAP, :] = block.astype(bf16)
        slot_prob = jnp.sum(block * prob, axis=1, keepdims=True)
        pieces[k][:, 2 * width :] = jnp.broadcast_to(slot_prob, (CAP, LANES)).astype(bf16)
    for start, source in ((0, tok_ref), (width, cot_ref)):
        for at in range(0, width, 512):
            part = jnp.dot(placing_ref[...], source[:, at : at + 512], preferred_element_type=f32)
            part = part.astype(bf16)
            for k in range(n_expert):
                pieces[k][:, start + at : start + at + 512] = part[k * CAP : (k + 1) * CAP]


def place(me, route, prob, tokens, cotangent, n_expert):
    count, width = tokens.shape
    outs = pl.pallas_call(
        functools.partial(place_kernel, n_expert),
        out_shape=[jax.ShapeDtypeStruct((n_expert * CAP, count), bf16)]
        + [jax.ShapeDtypeStruct((CAP, 2 * width + LANES), bf16)] * n_expert,
        in_specs=[SMEM] + [VMEM] * 4,
        out_specs=[VMEM] * (n_expert + 1),
        cost_estimate=SMALL,
    )(me.reshape(1), route.reshape(1, count), prob.reshape(1, count), tokens, cotangent)
    return outs[0], outs[1:]


def halves(whole):
    high = whole.astype(bf16)
    return high, (whole - high.astype(f32)).astype(bf16)


def weight_scratch(count, depth, units):
    return [
        pltpu.VMEM((count, depth, units), f32),
        pltpu.SemaphoreType.DMA((count, depth // BLOCK)),
    ]


def fetch(weights, buffer, arrived):
    copies = []
    for at in range(weights[0].shape[0] // BLOCK):
        here = slice(at * BLOCK, (at + 1) * BLOCK)
        for i, weight in enumerate(weights):
            copy = pltpu.make_async_copy(weight.at[here, :], buffer.at[i, here, :], arrived.at[i, at])
            copy.start()
            copies.append(copy)
    return copies


def times_weights(factors, buffer, copies):
    depth = buffer.shape[1]
    for at in range(depth // BLOCK):
        here = slice(at * BLOCK, (at + 1) * BLOCK)
        for i, (rows, total) in enumerate(factors):
            copies[at * len(factors) + i].wait()
            high, low = halves(buffer[i, here, :])
            row = rows[:, here]
            part = jnp.dot(row, high, preferred_element_type=f32)
            part += jnp.dot(row, low, preferred_element_type=f32)
            if at == 0:
                total[...] = part
            else:
                total[...] += part


def gate_factors(gate, up, prob):
    sig = jax.nn.sigmoid(gate)
    act = gate * sig
    hidden = act * up
    return prob * act, prob * (up * sig * (1.0 + gate * (1.0 - sig))), hidden


def against(left, right):
    return lax.dot_general(left, right, (((1,), (1,)), ((), ())), preferred_element_type=f32)


def chunk_kernel(count, *refs):
    pieces, weights, terms_ref = refs[:count], refs[count : count + 3], refs[count + 3]
    outs = refs[count + 4 : 2 * count + 4]
    tok, cot, gate_sum, up_sum, back_sum, low_ref, buffer, arrived = refs[2 * count + 4 :]
    depth, units = weights[0].shape
    copies = fetch(weights, buffer, arrived)
    for k, piece in enumerate(pieces):
        part = slice(k * CAP, (k + 1) * CAP)
        tok[part, :] = piece[:, :depth]
        cot[part, :] = piece[:, depth : 2 * depth]
    times_weights(((tok, gate_sum), (tok, up_sum), (cot, back_sum)), buffer, copies)
    for k, piece in enumerate(pieces):
        part = slice(k * CAP, (k + 1) * CAP)
        prob = piece[:, 2 * depth :].astype(f32)[:, :1]
        act, slope, hidden = gate_factors(gate_sum[part, :], up_sum[part, :], prob)
        back = back_sum[part, :]
        total = jnp.sum(hidden * back, axis=1, keepdims=True)
        outs[k][:, depth:] = jnp.broadcast_to(total, (CAP, LANES)).astype(outs[k].dtype)
        for at, factor in ((0, slope), (units, act)):
            high, low = halves(factor * back)
            terms_ref[part, at : at + units] = high
            low_ref[part, at : at + units] = low
        terms_ref[part, 2 * units :] = (prob * hidden).astype(bf16)
    for at in range(0, depth, BLOCK):
        total = None
        for i in range(2):
            high, low = halves(buffer[i, at : at + BLOCK, :])
            grad_hi = terms_ref[:, i * units : (i + 1) * units]
            grad_lo = low_ref[:, i * units : (i + 1) * units]
            both = against(high, jnp.concatenate([grad_hi, grad_lo], axis=0)).T
            part = both[: count * CAP] + both[count * CAP :] + against(low, grad_hi).T
            total = part if total is None else total + part
        for k, out in enumerate(outs):
            out[:, at : at + BLOCK] = total[k * CAP : (k + 1) * CAP].astype(out.dtype)


def chunk_rows(pieces, weights, back_type, passes):
    count = len(pieces)
    depth, units = weights[0].shape
    rows = count * CAP
    outs = pl.pallas_call(
        functools.partial(chunk_kernel, count),
        out_shape=[jax.ShapeDtypeStruct((rows, 3 * units), bf16)]
        + [jax.ShapeDtypeStruct((CAP, depth + LANES), back_type)] * count,
        in_specs=[VMEM] * count + [HBM] * 3,
        out_specs=[VMEM] * (count + 1),
        scratch_shapes=[pltpu.VMEM((rows, depth), bf16)] * 2
        + [pltpu.VMEM((rows, units), f32)] * 3
        + [pltpu.VMEM((rows, 2 * units), bf16)]
        + weight_scratch(3, depth, units),
        compiler_params=ALONE,
        cost_estimate=pl.CostEstimate(flops=passes * 192 * depth * units, bytes_accessed=MIB, transcendentals=0),
    )(*pieces, *weights)
    return outs[0], outs[1:]


def take_kernel(n_expert, placing_ref, *refs):
    pieces = refs[:n_expert]
    out_ref, prob_ref, rows = refs[n_expert:]
    count, width = out_ref.shape
    exact = rows.dtype != bf16
    for k in range(n_expert):
        rows[k * CAP : (k + 1) * CAP, :] = pieces[k][...]
    placing = placing_ref[...].astype(rows.dtype)
    for at in range(0, width, 512):
        part = lax.dot_general(
            placing, rows[:, at : at + 512], (((0,), (0,)), ((), ())),
            precision=highest if exact else None, preferred_element_type=f32,
        )
        out_ref[:, at : at + 512] = part.astype(bf16)
    column = rows[:, width:].astype(f32)[:, :1]
    prob_ref[...] = jnp.sum(placing_ref[...].astype(f32) * column, axis=0, keepdims=True).astype(bf16)


def take(placing, pieces):
    n_expert = len(pieces)
    count = placing.shape[1]
    width = pieces[0].shape[1] - LANES
    grad, prob = pl.pallas_call(
        functools.partial(take_kernel, n_expert),
        out_shape=[
            jax.ShapeDtypeStruct((count, width), bf16),
            jax.ShapeDtypeStruct((1, count), bf16),
        ],
        in_specs=[VMEM] * (n_expert + 1),
        out_specs=[VMEM] * 2,
        scratch_shapes=[pltpu.VMEM((n_expert * CAP, width + LANES), pieces[0].dtype)],
        compiler_params=pltpu.CompilerParams(vmem_limit_bytes=32 * MIB) if pieces[0].dtype != bf16 else PARAMS,
        cost_estimate=SMALL,
    )(placing, *pieces)
    return grad, prob.reshape(count)


def shards(tokens, cotangent, route, prob, w_gate, w_up, w_down):
    n_expert = lax.axis_size("expert")
    n_dp = lax.axis_size("dp")
    width = tokens.shape[1]
    share = width // n_dp
    scale = 1.0 / math.sqrt(tokens.shape[0] * n_dp * n_expert)
    back_type = bf16 if n_expert == HOT else f32
    me = lax.axis_index("expert").astype(i32)
    weights = (w_gate[0], w_up[0], w_down[0])
    chips = range(n_dp // 2)
    home = [None] * n_expert

    def exchange(payload):
        return [payload[0]] + [flipped(payload[k], "dp", 2 * k) for k in chips[1:]]

    def swap(*groups):
        terms = [g[:, 4 * share :] for got in groups for g in got]
        other = flipped(jnp.concatenate(terms), "dp", 1)
        cuts, at = [], 0
        for got in groups:
            count = len(got) * got[0].shape[0]
            cuts.append(other[at : at + count])
            at += count
        return cuts

    def give_back(home, shifts, back):
        home = list(home)
        for i, k in enumerate(shifts):
            home[k] = shifted(back[i], "expert", n_expert - k)
        return home

    placing, pieces = place(me, route, prob, tokens, cotangent, n_expert)
    odd = list(range(1, n_expert, 2))
    even = list(range(2, n_expert, 2))
    first = [shifted(pieces[k], "expert", k) for k in odd]

    theirs = flipped(cut(pieces[:1], width), "dp", 1)
    terms, back = chunk_rows(pieces[:1], weights, back_type, 36)
    home[0] = back[0]
    payload = pack(pieces[:1], theirs, terms, width)
    late, _ = lax.optimization_barrier(([pieces[k] for k in even], payload[0]))
    second = [shifted(piece, "expert", k) for piece, k in zip(late, even)]
    payload[-1], first = lax.optimization_barrier((payload[-1], first))
    got_local = exchange(payload)

    theirs = flipped(cut(first, width), "dp", 1)
    terms, back = chunk_rows(first, weights, back_type, 36)
    payload = pack(first, theirs, terms, width)
    payload, got_local = lax.optimization_barrier((payload, got_local))
    got_first = exchange(payload)

    second, back, _ = lax.optimization_barrier((second, back, payload))
    home = give_back(home, odd, back)
    theirs = flipped(cut(second, width), "dp", 1)
    terms, back = chunk_rows(second, weights, back_type, 12)
    payload, got_first, back, home = lax.optimization_barrier(
        (pack(second, theirs, terms, width), got_first, back, home)
    )
    home = give_back(home, even, back)
    got_second = exchange(payload)
    local_other, first_other = swap(got_local, got_first)
    sums = weight_sums(got_local, local_other, None, share, None)
    sums = weight_sums(got_first, first_other, sums, share, None)
    got_second, home, sums = lax.optimization_barrier((got_second, home, sums))
    sums = weight_sums(got_second, swap(got_second)[0], sums, share, scale)

    grad_input, grad_prob = take(placing, home)
    return (grad_input, grad_prob, *[total[None] for total in sums])


def solution(mesh):
    placed = (
        P(("dp", "expert"), None),
        P(("dp", "expert"), None),
        P(("dp", "expert"), None),
        P(("dp", "expert")),
        P("expert", None, None),
        P("expert", None, None),
        P("expert", None, None),
    )
    return jax.shard_map(
        shards,
        mesh=mesh,
        in_specs=placed,
        out_specs=(
            P(("dp", "expert"), None),
            P(("dp", "expert")),
            P("expert", "dp", None),
            P("expert", "dp", None),
            P("expert", "dp", None),
        ),
        check_vma=False,
    )
```

```python
import functools
import math

import jax
import jax.numpy as jnp
from jax import lax
from jax.experimental import pallas as pl
from jax.experimental.pallas import tpu as pltpu
from jax.sharding import PartitionSpec as P

HOT = 4
CAP = 48
LANES = 128
BLOCK = 256
MIB = 1 << 20

highest = lax.Precision.HIGHEST
f32 = jnp.float32
bf16 = jnp.bfloat16
i32 = jnp.int32
VMEM = pl.BlockSpec(memory_space=pltpu.VMEM)
SMEM = pl.BlockSpec(memory_space=pltpu.SMEM)
HBM = pl.BlockSpec(memory_space=pltpu.HBM)
PARAMS = pltpu.CompilerParams(vmem_limit_bytes=14 * MIB)
ALONE = pltpu.CompilerParams(vmem_limit_bytes=52 * MIB)
SMALL = pl.CostEstimate(flops=0, bytes_accessed=1024, transcendentals=0)


def shifted(values, axis, by):
    size = lax.axis_size(axis)
    return lax.ppermute(values, axis, [(i, (i + by) % size) for i in range(size)])


def flipped(values, axis, mask):
    size = lax.axis_size(axis)
    return lax.ppermute(values, axis, [(i, i ^ mask) for i in range(size)])


def cut_kernel(count, at_ref, *refs):
    pieces, theirs = refs[:count], refs[count]
    chips, _, double = theirs.shape
    share = double // 2
    width = 2 * chips * share
    for k in range(chips):
        start = pl.multiple_of((at_ref[0] ^ (2 * k + 1)) * share, share)
        for i in range(count):
            part = slice(i * CAP, (i + 1) * CAP)
            theirs[k, part, :share] = pieces[i][:, pl.ds(start, share)]
            theirs[k, part, share:] = pieces[i][:, pl.ds(width + start, share)]


def pack_kernel(count, at_ref, *refs):
    pieces, theirs, terms, payload = refs[:count], refs[count], refs[count + 1], refs[count + 2 :]
    chips, _, double = theirs.shape
    share = double // 2
    width = 2 * chips * share
    for k in range(chips):
        start = pl.multiple_of((at_ref[0] ^ (2 * k)) * share, share)
        for i in range(count):
            part = slice(i * CAP, (i + 1) * CAP)
            payload[k][part, :share] = pieces[i][:, pl.ds(start, share)]
            payload[k][part, share:double] = pieces[i][:, pl.ds(width + start, share)]
        payload[k][:, double : 2 * double] = theirs[k]
        payload[k][:, 2 * double :] = terms[...]


def slices_of(pieces, width, share, flips):
    at = lax.axis_index("dp").astype(i32)
    rows = jnp.concatenate(pieces)
    return [
        jnp.concatenate(
            [
                lax.dynamic_slice_in_dim(rows, base + (at ^ flip) * share, share, axis=1)
                for base in (0, width)
            ],
            axis=1,
        )
        for flip in flips
    ]


def cut(pieces, width):
    size = lax.axis_size("dp")
    share = width // size
    if share % LANES:
        return jnp.stack(slices_of(pieces, width, share, range(1, size, 2)))
    return pl.pallas_call(
        functools.partial(cut_kernel, len(pieces)),
        out_shape=jax.ShapeDtypeStruct((size // 2, len(pieces) * CAP, 2 * share), bf16),
        in_specs=[SMEM] + [VMEM] * len(pieces),
        out_specs=VMEM,
        compiler_params=PARAMS,
        cost_estimate=SMALL,
    )(lax.axis_index("dp").astype(i32).reshape(1), *pieces)


def pack(pieces, theirs, terms, width):
    return list(packed(pieces, theirs, terms, width))


def packed(pieces, theirs, terms, width):
    size = lax.axis_size("dp")
    share = width // size
    if share % LANES:
        own = slices_of(pieces, width, share, range(0, size, 2))
        return [jnp.concatenate([own[k], theirs[k], terms], axis=1) for k in range(size // 2)]
    shape = jax.ShapeDtypeStruct((terms.shape[0], 4 * share + terms.shape[1]), bf16)
    return pl.pallas_call(
        functools.partial(pack_kernel, len(pieces)),
        out_shape=[shape] * (size // 2),
        in_specs=[SMEM] + [VMEM] * (len(pieces) + 2),
        out_specs=[VMEM] * (size // 2),
        compiler_params=PARAMS,
        cost_estimate=SMALL,
    )(lax.axis_index("dp").astype(i32).reshape(1), *pieces, theirs, terms)


def sum_kernel(chips, share, units, scale, first, *refs):
    got, others = refs[:chips], refs[chips]
    past = () if first else refs[chips + 1 : chips + 4]
    outs = refs[-5:-2]
    cols, terms = refs[-2:]
    rows = got[0].shape[0]
    for k in range(chips):
        for core in range(2):
            part = slice((2 * k + core) * rows, (2 * k + core + 1) * rows)
            cols[part, :] = got[k][:, 2 * core * share : 2 * (core + 1) * share]
        terms[2 * k * rows : (2 * k + 1) * rows, :] = got[k][:, 4 * share :]
        terms[(2 * k + 1) * rows : (2 * k + 2) * rows, :] = others[k * rows : (k + 1) * rows, :]
    for i in range(3):
        column = share if i == 2 else 0
        total = lax.dot_general(
            cols[:, column : column + share], terms[:, i * units : (i + 1) * units],
            (((0,), (0,)), ((), ())), preferred_element_type=f32,
        )
        if not first:
            total += past[i][...]
        outs[i][...] = total if scale is None else total * scale


def weight_sums(got, others, past, share, scale):
    chips = len(got)
    rows = got[0].shape[0]
    units = others.shape[1] // 3
    if share % LANES:
        wide = [jnp.concatenate([g[:, 2 * c * share : 2 * (c + 1) * share] for g in got]) for c in range(2)]
        near = jnp.concatenate([g[:, 4 * share :] for g in got])
        sums = []
        for i in range(3):
            total = 0.0 if past is None else past[i]
            for cols, terms in zip(wide, (near, others)):
                column = share if i == 2 else 0
                total += lax.dot_general(
                    cols[:, column : column + share], terms[:, i * units : (i + 1) * units],
                    (((0,), (0,)), ((), ())), preferred_element_type=f32,
                )
            sums.append(total if scale is None else total * scale)
        return sums
    past = [] if past is None else list(past)
    return pl.pallas_call(
        functools.partial(sum_kernel, chips, share, units, scale, not past),
        out_shape=[jax.ShapeDtypeStruct((share, units), f32)] * 3,
        in_specs=[VMEM] * (chips + 1 + len(past)),
        out_specs=[VMEM] * 3,
        scratch_shapes=[
            pltpu.VMEM((2 * chips * rows, 2 * share), bf16),
            pltpu.VMEM((2 * chips * rows, 3 * units), bf16),
        ],
        compiler_params=PARAMS,
        cost_estimate=SMALL,
    )(*got, others, *past)


def place_kernel(n_expert, me_ref, route_ref, prob_ref, tok_ref, cot_ref, placing_ref, *pieces):
    quarters = n_expert // HOT
    count, width = tok_ref.shape
    route = route_ref[...]
    hot = (route == lax.broadcasted_iota(i32, (16, count), 0)).astype(f32)
    before = lax.broadcasted_iota(i32, (count, count), 0) < lax.broadcasted_iota(i32, (count, count), 1)
    earlier = jnp.dot(hot.astype(bf16), before.astype(f32).astype(bf16), preferred_element_type=f32)
    rank = jnp.sum(earlier * hot, axis=0, keepdims=True).astype(i32)
    slot = lax.broadcasted_iota(i32, (CAP, count), 0)
    prob = prob_ref[...].astype(f32)
    for k in range(n_expert):
        owner = lax.rem(me_ref[0] + k, n_expert) // quarters
        block = jnp.where((route == owner) & (rank == slot), 1.0, 0.0)
        placing_ref[k * CAP : (k + 1) * CAP, :] = block.astype(bf16)
        slot_prob = jnp.sum(block * prob, axis=1, keepdims=True)
        pieces[k][:, 2 * width :] = jnp.broadcast_to(slot_prob, (CAP, LANES)).astype(bf16)
    for start, source in ((0, tok_ref), (width, cot_ref)):
        for at in range(0, width, 512):
            part = jnp.dot(placing_ref[...], source[:, at : at + 512], preferred_element_type=f32)
            part = part.astype(bf16)
            for k in range(n_expert):
                pieces[k][:, start + at : start + at + 512] = part[k * CAP : (k + 1) * CAP]


def place(me, route, prob, tokens, cotangent, n_expert):
    count, width = tokens.shape
    outs = pl.pallas_call(
        functools.partial(place_kernel, n_expert),
        out_shape=[jax.ShapeDtypeStruct((n_expert * CAP, count), bf16)]
        + [jax.ShapeDtypeStruct((CAP, 2 * width + LANES), bf16)] * n_expert,
        in_specs=[SMEM] + [VMEM] * 4,
        out_specs=[VMEM] * (n_expert + 1),
        cost_estimate=SMALL,
    )(me.reshape(1), route.reshape(1, count), prob.reshape(1, count), tokens, cotangent)
    return outs[0], outs[1:]


def halves(whole):
    high = whole.astype(bf16)
    return high, (whole - high.astype(f32)).astype(bf16)


def weight_scratch(count, depth, units):
    return [
        pltpu.VMEM((count, depth, units), f32),
        pltpu.SemaphoreType.DMA((count, depth // BLOCK)),
    ]


def fetch(weights, buffer, arrived):
    copies = []
    for at in range(weights[0].shape[0] // BLOCK):
        here = slice(at * BLOCK, (at + 1) * BLOCK)
        for i, weight in enumerate(weights):
            copy = pltpu.make_async_copy(weight.at[here, :], buffer.at[i, here, :], arrived.at[i, at])
            copy.start()
            copies.append(copy)
    return copies


def times_weights(factors, buffer, copies):
    depth = buffer.shape[1]
    for at in range(depth // BLOCK):
        here = slice(at * BLOCK, (at + 1) * BLOCK)
        for i, (rows, total) in enumerate(factors):
            copies[at * len(factors) + i].wait()
            high, low = halves(buffer[i, here, :])
            row = rows[:, here]
            part = jnp.dot(row, high, preferred_element_type=f32)
            part += jnp.dot(row, low, preferred_element_type=f32)
            if at == 0:
                total[...] = part
            else:
                total[...] += part


def gate_factors(gate, up, prob):
    sig = jax.nn.sigmoid(gate)
    act = gate * sig
    hidden = act * up
    return prob * act, prob * (up * sig * (1.0 + gate * (1.0 - sig))), hidden


def against(left, right):
    return lax.dot_general(left, right, (((1,), (1,)), ((), ())), preferred_element_type=f32)


def chunk_kernel(count, *refs):
    pieces, weights, terms_ref = refs[:count], refs[count : count + 3], refs[count + 3]
    outs = refs[count + 4 : 2 * count + 4]
    tok, cot, gate_sum, up_sum, back_sum, low_ref, buffer, arrived = refs[2 * count + 4 :]
    depth, units = weights[0].shape
    copies = fetch(weights, buffer, arrived)
    for k, piece in enumerate(pieces):
        part = slice(k * CAP, (k + 1) * CAP)
        tok[part, :] = piece[:, :depth]
        cot[part, :] = piece[:, depth : 2 * depth]
    times_weights(((tok, gate_sum), (tok, up_sum), (cot, back_sum)), buffer, copies)
    for k, piece in enumerate(pieces):
        part = slice(k * CAP, (k + 1) * CAP)
        prob = piece[:, 2 * depth :].astype(f32)[:, :1]
        act, slope, hidden = gate_factors(gate_sum[part, :], up_sum[part, :], prob)
        back = back_sum[part, :]
        total = jnp.sum(hidden * back, axis=1, keepdims=True)
        outs[k][:, depth:] = jnp.broadcast_to(total, (CAP, LANES)).astype(outs[k].dtype)
        for at, factor in ((0, slope), (units, act)):
            high, low = halves(factor * back)
            terms_ref[part, at : at + units] = high
            low_ref[part, at : at + units] = low
        terms_ref[part, 2 * units :] = (prob * hidden).astype(bf16)
    for at in range(0, depth, BLOCK):
        total = None
        for i in range(2):
            high, low = halves(buffer[i, at : at + BLOCK, :])
            grad_hi = terms_ref[:, i * units : (i + 1) * units]
            grad_lo = low_ref[:, i * units : (i + 1) * units]
            both = against(high, jnp.concatenate([grad_hi, grad_lo], axis=0)).T
            part = both[: count * CAP] + both[count * CAP :] + against(low, grad_hi).T
            total = part if total is None else total + part
        for k, out in enumerate(outs):
            out[:, at : at + BLOCK] = total[k * CAP : (k + 1) * CAP].astype(out.dtype)


def chunk_rows(pieces, weights, back_type, passes):
    count = len(pieces)
    depth, units = weights[0].shape
    rows = count * CAP
    outs = pl.pallas_call(
        functools.partial(chunk_kernel, count),
        out_shape=[jax.ShapeDtypeStruct((rows, 3 * units), bf16)]
        + [jax.ShapeDtypeStruct((CAP, depth + LANES), back_type)] * count,
        in_specs=[VMEM] * count + [HBM] * 3,
        out_specs=[VMEM] * (count + 1),
        scratch_shapes=[pltpu.VMEM((rows, depth), bf16)] * 2
        + [pltpu.VMEM((rows, units), f32)] * 3
        + [pltpu.VMEM((rows, 2 * units), bf16)]
        + weight_scratch(3, depth, units),
        compiler_params=ALONE,
        cost_estimate=pl.CostEstimate(flops=passes * 192 * depth * units, bytes_accessed=MIB, transcendentals=0),
    )(*pieces, *weights)
    return outs[0], outs[1:]


def take_kernel(n_expert, placing_ref, *refs):
    pieces = refs[:n_expert]
    out_ref, prob_ref, rows = refs[n_expert:]
    count, width = out_ref.shape
    exact = rows.dtype != bf16
    for k in range(n_expert):
        rows[k * CAP : (k + 1) * CAP, :] = pieces[k][...]
    placing = placing_ref[...].astype(rows.dtype)
    for at in range(0, width, 512):
        part = lax.dot_general(
            placing, rows[:, at : at + 512], (((0,), (0,)), ((), ())),
            precision=highest if exact else None, preferred_element_type=f32,
        )
        out_ref[:, at : at + 512] = part.astype(bf16)
    column = rows[:, width:].astype(f32)[:, :1]
    prob_ref[...] = jnp.sum(placing_ref[...].astype(f32) * column, axis=0, keepdims=True).astype(bf16)


def take(placing, pieces):
    n_expert = len(pieces)
    count = placing.shape[1]
    width = pieces[0].shape[1] - LANES
    grad, prob = pl.pallas_call(
        functools.partial(take_kernel, n_expert),
        out_shape=[
            jax.ShapeDtypeStruct((count, width), bf16),
            jax.ShapeDtypeStruct((1, count), bf16),
        ],
        in_specs=[VMEM] * (n_expert + 1),
        out_specs=[VMEM] * 2,
        scratch_shapes=[pltpu.VMEM((n_expert * CAP, width + LANES), pieces[0].dtype)],
        compiler_params=pltpu.CompilerParams(vmem_limit_bytes=32 * MIB) if pieces[0].dtype != bf16 else PARAMS,
        cost_estimate=SMALL,
    )(placing, *pieces)
    return grad, prob.reshape(count)


def shards(tokens, cotangent, route, prob, w_gate, w_up, w_down):
    n_expert = lax.axis_size("expert")
    n_dp = lax.axis_size("dp")
    width = tokens.shape[1]
    share = width // n_dp
    scale = 1.0 / math.sqrt(tokens.shape[0] * n_dp * n_expert)
    back_type = bf16 if n_expert == HOT else f32
    me = lax.axis_index("expert").astype(i32)
    weights = (w_gate[0], w_up[0], w_down[0])
    chips = range(n_dp // 2)
    home = [None] * n_expert

    def exchange(payload):
        return [payload[0]] + [flipped(payload[k], "dp", 2 * k) for k in chips[1:]]

    def swap(*groups):
        terms = [g[:, 4 * share :] for got in groups for g in got]
        other = flipped(jnp.concatenate(terms), "dp", 1)
        cuts, at = [], 0
        for got in groups:
            count = len(got) * got[0].shape[0]
            cuts.append(other[at : at + count])
            at += count
        return cuts

    def give_back(home, shifts, back):
        home = list(home)
        for i, k in enumerate(shifts):
            home[k] = shifted(back[i], "expert", n_expert - k)
        return home

    placing, pieces = place(me, route, prob, tokens, cotangent, n_expert)
    odd = list(range(1, n_expert, 2))
    even = list(range(2, n_expert, 2))
    first = [shifted(pieces[k], "expert", k) for k in odd]

    theirs = flipped(cut(pieces[:1], width), "dp", 1)
    terms, back = chunk_rows(pieces[:1], weights, back_type, 36)
    home[0] = back[0]
    payload = pack(pieces[:1], theirs, terms, width)
    late, payload[-1], first, _ = lax.optimization_barrier(
        ([pieces[k] for k in even], payload[-1], first, payload[0])
    )
    second = [shifted(piece, "expert", k) for piece, k in zip(late, even)]
    got_local = exchange(payload)

    theirs = flipped(cut(first, width), "dp", 1)
    terms, back = chunk_rows(first, weights, back_type, 24)
    payload = pack(first, theirs, terms, width)
    payload, got_local = lax.optimization_barrier((payload, got_local))
    got_first = exchange(payload)

    second, back, _ = lax.optimization_barrier((second, back, payload))
    home = give_back(home, odd, back)
    theirs = flipped(cut(second, width), "dp", 1)
    terms, back = chunk_rows(second, weights, back_type, 12)
    payload, got_first, back, home = lax.optimization_barrier(
        (pack(second, theirs, terms, width), got_first, back, home)
    )
    home = give_back(home, even, back)
    got_second = exchange(payload)
    local_other, first_other = swap(got_local, got_first)
    sums = weight_sums(got_local, local_other, None, share, None)
    sums = weight_sums(got_first, first_other, sums, share, None)
    got_second, home, sums = lax.optimization_barrier((got_second, home, sums))
    sums = weight_sums(got_second, swap(got_second)[0], sums, share, scale)

    grad_input, grad_prob = take(placing, home)
    return (grad_input, grad_prob, *[total[None] for total in sums])


def solution(mesh):
    placed = (
        P(("dp", "expert"), None),
        P(("dp", "expert"), None),
        P(("dp", "expert"), None),
        P(("dp", "expert")),
        P("expert", None, None),
        P("expert", None, None),
        P("expert", None, None),
    )
    return jax.shard_map(
        shards,
        mesh=mesh,
        in_specs=placed,
        out_specs=(
            P(("dp", "expert"), None),
            P(("dp", "expert")),
            P("expert", "dp", None),
            P("expert", "dp", None),
            P("expert", "dp", None),
        ),
        check_vma=False,
    )
```

```python
import functools
import math

import jax
import jax.numpy as jnp
from jax import lax
from jax.experimental import pallas as pl
from jax.experimental.pallas import tpu as pltpu
from jax.sharding import PartitionSpec as P

HOT = 4
CAP = 48
LANES = 128
BLOCK = 256
MIB = 1 << 20

highest = lax.Precision.HIGHEST
f32 = jnp.float32
bf16 = jnp.bfloat16
i32 = jnp.int32
VMEM = pl.BlockSpec(memory_space=pltpu.VMEM)
SMEM = pl.BlockSpec(memory_space=pltpu.SMEM)
HBM = pl.BlockSpec(memory_space=pltpu.HBM)
PARAMS = pltpu.CompilerParams(vmem_limit_bytes=14 * MIB)
ALONE = pltpu.CompilerParams(vmem_limit_bytes=52 * MIB)
SMALL = pl.CostEstimate(flops=0, bytes_accessed=1024, transcendentals=0)


def shifted(values, axis, by):
    size = lax.axis_size(axis)
    return lax.ppermute(values, axis, [(i, (i + by) % size) for i in range(size)])


def flipped(values, axis, mask):
    size = lax.axis_size(axis)
    return lax.ppermute(values, axis, [(i, i ^ mask) for i in range(size)])


def cut_kernel(count, at_ref, *refs):
    pieces, theirs = refs[:count], refs[count]
    chips, _, double = theirs.shape
    share = double // 2
    width = 2 * chips * share
    for k in range(chips):
        start = pl.multiple_of((at_ref[0] ^ (2 * k + 1)) * share, share)
        for i in range(count):
            part = slice(i * CAP, (i + 1) * CAP)
            theirs[k, part, :share] = pieces[i][:, pl.ds(start, share)]
            theirs[k, part, share:] = pieces[i][:, pl.ds(width + start, share)]


def pack_kernel(count, at_ref, *refs):
    pieces, theirs = refs[:count], refs[count]
    chips, _, double = theirs.shape
    payload, terms = refs[-chips:], refs[count + 1 : -chips]
    share = double // 2
    width = 2 * chips * share
    for k in range(chips):
        start = pl.multiple_of((at_ref[0] ^ (2 * k)) * share, share)
        for i in range(count):
            part = slice(i * CAP, (i + 1) * CAP)
            payload[k][part, :share] = pieces[i][:, pl.ds(start, share)]
            payload[k][part, share:double] = pieces[i][:, pl.ds(width + start, share)]
        payload[k][:, double : 2 * double] = theirs[k]
        for term in terms:
            payload[k][:, 2 * double :] = term[...]


def slices_of(pieces, width, share, flips):
    at = lax.axis_index("dp").astype(i32)
    rows = jnp.concatenate(pieces)
    return [
        jnp.concatenate(
            [
                lax.dynamic_slice_in_dim(rows, base + (at ^ flip) * share, share, axis=1)
                for base in (0, width)
            ],
            axis=1,
        )
        for flip in flips
    ]


def cut(pieces, width):
    size = lax.axis_size("dp")
    share = width // size
    if share % LANES:
        return jnp.stack(slices_of(pieces, width, share, range(1, size, 2)))
    return pl.pallas_call(
        functools.partial(cut_kernel, len(pieces)),
        out_shape=jax.ShapeDtypeStruct((size // 2, len(pieces) * CAP, 2 * share), bf16),
        in_specs=[SMEM] + [VMEM] * len(pieces),
        out_specs=VMEM,
        compiler_params=PARAMS,
        cost_estimate=SMALL,
    )(lax.axis_index("dp").astype(i32).reshape(1), *pieces)


def pack(pieces, theirs, width, *terms):
    size = lax.axis_size("dp")
    share = width // size
    if share % LANES:
        own = slices_of(pieces, width, share, range(0, size, 2))
        return [jnp.concatenate([own[k], theirs[k], *terms], axis=1) for k in range(size // 2)]
    wide = 4 * share + sum(term.shape[1] for term in terms)
    shape = jax.ShapeDtypeStruct((theirs.shape[1], wide), bf16)
    return list(
        pl.pallas_call(
            functools.partial(pack_kernel, len(pieces)),
            out_shape=[shape] * (size // 2),
            in_specs=[SMEM] + [VMEM] * (len(pieces) + 1 + len(terms)),
            out_specs=[VMEM] * (size // 2),
            compiler_params=PARAMS,
            cost_estimate=SMALL,
        )(lax.axis_index("dp").astype(i32).reshape(1), *pieces, theirs, *terms)
    )


def sum_kernel(chips, share, units, scale, first, *refs):
    got, near, others = refs[:chips], refs[chips : 2 * chips], refs[2 * chips]
    past = () if first else refs[2 * chips + 1 : 2 * chips + 4]
    outs = refs[-5:-2]
    cols, terms = refs[-2:]
    rows = got[0].shape[0]
    start = near[0].shape[1] - 3 * units
    for k in range(chips):
        for core in range(2):
            part = slice((2 * k + core) * rows, (2 * k + core + 1) * rows)
            cols[part, :] = got[k][:, 2 * core * share : 2 * (core + 1) * share]
        terms[2 * k * rows : (2 * k + 1) * rows, :] = near[k][:, start:]
        terms[(2 * k + 1) * rows : (2 * k + 2) * rows, :] = others[k * rows : (k + 1) * rows, :]
    for i in range(3):
        column = share if i == 2 else 0
        total = lax.dot_general(
            cols[:, column : column + share], terms[:, i * units : (i + 1) * units],
            (((0,), (0,)), ((), ())), preferred_element_type=f32,
        )
        if not first:
            total += past[i][...]
        outs[i][...] = total if scale is None else total * scale


def weight_sums(got, near, others, past, share, scale):
    chips = len(got)
    rows = got[0].shape[0]
    units = others.shape[1] // 3
    if share % LANES:
        wide = [jnp.concatenate([g[:, 2 * c * share : 2 * (c + 1) * share] for g in got]) for c in range(2)]
        own = jnp.concatenate([n[:, -3 * units :] for n in near])
        sums = []
        for i in range(3):
            total = 0.0 if past is None else past[i]
            for cols, terms in zip(wide, (own, others)):
                column = share if i == 2 else 0
                total += lax.dot_general(
                    cols[:, column : column + share], terms[:, i * units : (i + 1) * units],
                    (((0,), (0,)), ((), ())), preferred_element_type=f32,
                )
            sums.append(total if scale is None else total * scale)
        return sums
    past = [] if past is None else list(past)
    return pl.pallas_call(
        functools.partial(sum_kernel, chips, share, units, scale, not past),
        out_shape=[jax.ShapeDtypeStruct((share, units), f32)] * 3,
        in_specs=[VMEM] * (2 * chips + 1 + len(past)),
        out_specs=[VMEM] * 3,
        scratch_shapes=[
            pltpu.VMEM((2 * chips * rows, 2 * share), bf16),
            pltpu.VMEM((2 * chips * rows, 3 * units), bf16),
        ],
        compiler_params=PARAMS,
        cost_estimate=SMALL,
    )(*got, *near, others, *past)


def place_kernel(n_expert, me_ref, route_ref, prob_ref, tok_ref, cot_ref, placing_ref, *pieces):
    quarters = n_expert // HOT
    count, width = tok_ref.shape
    route = route_ref[...]
    hot = (route == lax.broadcasted_iota(i32, (16, count), 0)).astype(f32)
    before = lax.broadcasted_iota(i32, (count, count), 0) < lax.broadcasted_iota(i32, (count, count), 1)
    earlier = jnp.dot(hot.astype(bf16), before.astype(f32).astype(bf16), preferred_element_type=f32)
    rank = jnp.sum(earlier * hot, axis=0, keepdims=True).astype(i32)
    slot = lax.broadcasted_iota(i32, (CAP, count), 0)
    prob = prob_ref[...].astype(f32)
    for k in range(n_expert):
        owner = lax.rem(me_ref[0] + k, n_expert) // quarters
        block = jnp.where((route == owner) & (rank == slot), 1.0, 0.0)
        placing_ref[k * CAP : (k + 1) * CAP, :] = block.astype(bf16)
        slot_prob = jnp.sum(block * prob, axis=1, keepdims=True)
        pieces[k][:, 2 * width :] = jnp.broadcast_to(slot_prob, (CAP, LANES)).astype(bf16)
    for start, source in ((0, tok_ref), (width, cot_ref)):
        for at in range(0, width, 512):
            part = jnp.dot(placing_ref[...], source[:, at : at + 512], preferred_element_type=f32)
            part = part.astype(bf16)
            for k in range(n_expert):
                pieces[k][:, start + at : start + at + 512] = part[k * CAP : (k + 1) * CAP]


def place(me, route, prob, tokens, cotangent, n_expert):
    count, width = tokens.shape
    outs = pl.pallas_call(
        functools.partial(place_kernel, n_expert),
        out_shape=[jax.ShapeDtypeStruct((n_expert * CAP, count), bf16)]
        + [jax.ShapeDtypeStruct((CAP, 2 * width + LANES), bf16)] * n_expert,
        in_specs=[SMEM] + [VMEM] * 4,
        out_specs=[VMEM] * (n_expert + 1),
        cost_estimate=SMALL,
    )(me.reshape(1), route.reshape(1, count), prob.reshape(1, count), tokens, cotangent)
    return outs[0], outs[1:]


def halves(whole):
    high = whole.astype(bf16)
    return high, (whole - high.astype(f32)).astype(bf16)


def weight_scratch(count, depth, units):
    return [
        pltpu.VMEM((count, depth, units), f32),
        pltpu.SemaphoreType.DMA((count, depth // BLOCK)),
    ]


def fetch(weights, buffer, arrived):
    copies = []
    for at in range(weights[0].shape[0] // BLOCK):
        here = slice(at * BLOCK, (at + 1) * BLOCK)
        for i, weight in enumerate(weights):
            copy = pltpu.make_async_copy(weight.at[here, :], buffer.at[i, here, :], arrived.at[i, at])
            copy.start()
            copies.append(copy)
    return copies


def times_weights(factors, buffer, copies):
    depth = buffer.shape[1]
    for at in range(depth // BLOCK):
        here = slice(at * BLOCK, (at + 1) * BLOCK)
        for i, (rows, total) in enumerate(factors):
            copies[at * len(factors) + i].wait()
            high, low = halves(buffer[i, here, :])
            row = rows[:, here]
            part = jnp.dot(row, high, preferred_element_type=f32)
            part += jnp.dot(row, low, preferred_element_type=f32)
            if at == 0:
                total[...] = part
            else:
                total[...] += part


def gate_factors(gate, up, prob):
    sig = jax.nn.sigmoid(gate)
    act = gate * sig
    hidden = act * up
    return prob * act, prob * (up * sig * (1.0 + gate * (1.0 - sig))), hidden


def against(left, right):
    return lax.dot_general(left, right, (((1,), (1,)), ((), ())), preferred_element_type=f32)


def chunk_kernel(count, *refs):
    pieces, weights, terms_ref = refs[:count], refs[count : count + 3], refs[count + 3]
    outs = refs[count + 4 : 2 * count + 4]
    tok, cot, gate_sum, up_sum, back_sum, low_ref, buffer, arrived = refs[2 * count + 4 :]
    depth, units = weights[0].shape
    copies = fetch(weights, buffer, arrived)
    for k, piece in enumerate(pieces):
        part = slice(k * CAP, (k + 1) * CAP)
        tok[part, :] = piece[:, :depth]
        cot[part, :] = piece[:, depth : 2 * depth]
    times_weights(((tok, gate_sum), (tok, up_sum), (cot, back_sum)), buffer, copies)
    for k, piece in enumerate(pieces):
        part = slice(k * CAP, (k + 1) * CAP)
        prob = piece[:, 2 * depth :].astype(f32)[:, :1]
        act, slope, hidden = gate_factors(gate_sum[part, :], up_sum[part, :], prob)
        back = back_sum[part, :]
        total = jnp.sum(hidden * back, axis=1, keepdims=True)
        outs[k][:, depth:] = jnp.broadcast_to(total, (CAP, LANES)).astype(outs[k].dtype)
        for at, factor in ((0, slope), (units, act)):
            high, low = halves(factor * back)
            terms_ref[part, at : at + units] = high
            low_ref[part, at : at + units] = low
        terms_ref[part, 2 * units :] = (prob * hidden).astype(bf16)
    for at in range(0, depth, BLOCK):
        total = None
        for i in range(2):
            high, low = halves(buffer[i, at : at + BLOCK, :])
            grad_hi = terms_ref[:, i * units : (i + 1) * units]
            grad_lo = low_ref[:, i * units : (i + 1) * units]
            both = against(high, jnp.concatenate([grad_hi, grad_lo], axis=0)).T
            part = both[: count * CAP] + both[count * CAP :] + against(low, grad_hi).T
            total = part if total is None else total + part
        for k, out in enumerate(outs):
            out[:, at : at + BLOCK] = total[k * CAP : (k + 1) * CAP].astype(out.dtype)


def chunk_rows(pieces, weights, back_type, passes):
    count = len(pieces)
    depth, units = weights[0].shape
    rows = count * CAP
    outs = pl.pallas_call(
        functools.partial(chunk_kernel, count),
        out_shape=[jax.ShapeDtypeStruct((rows, 3 * units), bf16)]
        + [jax.ShapeDtypeStruct((CAP, depth + LANES), back_type)] * count,
        in_specs=[VMEM] * count + [HBM] * 3,
        out_specs=[VMEM] * (count + 1),
        scratch_shapes=[pltpu.VMEM((rows, depth), bf16)] * 2
        + [pltpu.VMEM((rows, units), f32)] * 3
        + [pltpu.VMEM((rows, 2 * units), bf16)]
        + weight_scratch(3, depth, units),
        compiler_params=ALONE,
        cost_estimate=pl.CostEstimate(flops=passes * 192 * depth * units, bytes_accessed=MIB, transcendentals=0),
    )(*pieces, *weights)
    return outs[0], outs[1:]


def take_kernel(n_expert, placing_ref, *refs):
    pieces = refs[:n_expert]
    out_ref, prob_ref, rows = refs[n_expert:]
    count, width = out_ref.shape
    exact = rows.dtype != bf16
    for k in range(n_expert):
        rows[k * CAP : (k + 1) * CAP, :] = pieces[k][...]
    placing = placing_ref[...].astype(rows.dtype)
    for at in range(0, width, 512):
        part = lax.dot_general(
            placing, rows[:, at : at + 512], (((0,), (0,)), ((), ())),
            precision=highest if exact else None, preferred_element_type=f32,
        )
        out_ref[:, at : at + 512] = part.astype(bf16)
    column = rows[:, width:].astype(f32)[:, :1]
    prob_ref[...] = jnp.sum(placing_ref[...].astype(f32) * column, axis=0, keepdims=True).astype(bf16)


def take(placing, pieces):
    n_expert = len(pieces)
    count = placing.shape[1]
    width = pieces[0].shape[1] - LANES
    grad, prob = pl.pallas_call(
        functools.partial(take_kernel, n_expert),
        out_shape=[
            jax.ShapeDtypeStruct((count, width), bf16),
            jax.ShapeDtypeStruct((1, count), bf16),
        ],
        in_specs=[VMEM] * (n_expert + 1),
        out_specs=[VMEM] * 2,
        scratch_shapes=[pltpu.VMEM((n_expert * CAP, width + LANES), pieces[0].dtype)],
        compiler_params=pltpu.CompilerParams(vmem_limit_bytes=32 * MIB) if pieces[0].dtype != bf16 else PARAMS,
        cost_estimate=SMALL,
    )(placing, *pieces)
    return grad, prob.reshape(count)


def shards(tokens, cotangent, route, prob, w_gate, w_up, w_down):
    n_expert = lax.axis_size("expert")
    n_dp = lax.axis_size("dp")
    width = tokens.shape[1]
    units = w_gate.shape[2]
    share = width // n_dp
    scale = 1.0 / math.sqrt(tokens.shape[0] * n_dp * n_expert)
    back_type = bf16 if n_expert == HOT else f32
    me = lax.axis_index("expert").astype(i32)
    weights = (w_gate[0], w_up[0], w_down[0])
    chips = range(n_dp // 2)
    home = [None] * n_expert

    def exchange(payload):
        return [payload[0]] + [flipped(payload[k], "dp", 2 * k) for k in chips[1:]]

    def swap(*groups):
        terms = [near[:, -3 * units :] for group in groups for near in group]
        other = flipped(jnp.concatenate(terms), "dp", 1)
        cuts, at = [], 0
        for group in groups:
            count = len(group) * group[0].shape[0]
            cuts.append(other[at : at + count])
            at += count
        return cuts

    def give_back(home, shifts, back):
        home = list(home)
        for i, k in enumerate(shifts):
            home[k] = shifted(back[i], "expert", n_expert - k)
        return home

    placing, pieces = place(me, route, prob, tokens, cotangent, n_expert)
    odd = list(range(1, n_expert, 2))
    even = list(range(2, n_expert, 2))
    first = [shifted(pieces[k], "expert", k) for k in odd]

    theirs = flipped(cut(pieces[:1], width), "dp", 1)
    terms, back = chunk_rows(pieces[:1], weights, back_type, 36)
    home[0] = back[0]
    payload = pack(pieces[:1], theirs, width, terms)
    got_local = exchange(payload)
    late, first, got_local[1:] = lax.optimization_barrier(
        ([pieces[k] for k in even], first, got_local[1:])
    )
    second = [shifted(piece, "expert", k) for piece, k in zip(late, even)]

    theirs = flipped(cut(first, width), "dp", 1)
    got_first = exchange(pack(first, theirs, width))
    terms, back = chunk_rows(first, weights, back_type, 24)
    terms, got_first, got_local = lax.optimization_barrier((terms, got_first, got_local))
    near_first = exchange([terms] * len(chips))

    second, back, _ = lax.optimization_barrier((second, back, terms))
    home = give_back(home, odd[:-1], back[:-1])
    theirs = flipped(cut(second, width), "dp", 1)
    terms, back_even = chunk_rows(second, weights, back_type, 12)
    payload, near_first, back_even, home = lax.optimization_barrier(
        (pack(second, theirs, width, terms), near_first, back_even, home)
    )
    home = give_back(home, even, back_even)
    home = give_back(home, odd[-1:], back[-1:])
    got_second = exchange(payload)
    local_other, first_other = swap(got_local, near_first)
    sums = weight_sums(got_local, got_local, local_other, None, share, None)
    sums = weight_sums(got_first, near_first, first_other, sums, share, None)
    got_second, home, sums = lax.optimization_barrier((got_second, home, sums))
    sums = weight_sums(got_second, got_second, swap(got_second)[0], sums, share, scale)

    grad_input, grad_prob = take(placing, home)
    return (grad_input, grad_prob, *[total[None] for total in sums])


def solution(mesh):
    placed = (
        P(("dp", "expert"), None),
        P(("dp", "expert"), None),
        P(("dp", "expert"), None),
        P(("dp", "expert")),
        P("expert", None, None),
        P("expert", None, None),
        P("expert", None, None),
    )
    return jax.shard_map(
        shards,
        mesh=mesh,
        in_specs=placed,
        out_specs=(
            P(("dp", "expert"), None),
            P(("dp", "expert")),
            P("expert", "dp", None),
            P("expert", "dp", None),
            P("expert", "dp", None),
        ),
        check_vma=False,
    )
```

```python
import functools
import math

import jax
import jax.numpy as jnp
from jax import lax
from jax.experimental import pallas as pl
from jax.experimental.pallas import tpu as pltpu
from jax.sharding import PartitionSpec as P

HOT = 4
CAP = 48
LANES = 128
BLOCK = 256
MIB = 1 << 20

highest = lax.Precision.HIGHEST
f32 = jnp.float32
bf16 = jnp.bfloat16
i32 = jnp.int32
VMEM = pl.BlockSpec(memory_space=pltpu.VMEM)
SMEM = pl.BlockSpec(memory_space=pltpu.SMEM)
HBM = pl.BlockSpec(memory_space=pltpu.HBM)
PARAMS = pltpu.CompilerParams(vmem_limit_bytes=14 * MIB)
ALONE = pltpu.CompilerParams(vmem_limit_bytes=52 * MIB)
SMALL = pl.CostEstimate(flops=0, bytes_accessed=1024, transcendentals=0)


def shifted(values, axis, by):
    size = lax.axis_size(axis)
    return lax.ppermute(values, axis, [(i, (i + by) % size) for i in range(size)])


def flipped(values, axis, mask):
    size = lax.axis_size(axis)
    return lax.ppermute(values, axis, [(i, i ^ mask) for i in range(size)])


def cut_kernel(count, at_ref, *refs):
    pieces, theirs = refs[:count], refs[count]
    chips, _, double = theirs.shape
    share = double // 2
    width = 2 * chips * share
    for k in range(chips):
        start = pl.multiple_of((at_ref[0] ^ (2 * k + 1)) * share, share)
        for i in range(count):
            part = slice(i * CAP, (i + 1) * CAP)
            theirs[k, part, :share] = pieces[i][:, pl.ds(start, share)]
            theirs[k, part, share:] = pieces[i][:, pl.ds(width + start, share)]


def pack_kernel(count, at_ref, *refs):
    pieces, theirs, terms, payload = refs[:count], refs[count], refs[count + 1], refs[count + 2 :]
    chips, _, double = theirs.shape
    share = double // 2
    width = 2 * chips * share
    for k in range(chips):
        start = pl.multiple_of((at_ref[0] ^ (2 * k)) * share, share)
        for i in range(count):
            part = slice(i * CAP, (i + 1) * CAP)
            payload[k][part, :share] = pieces[i][:, pl.ds(start, share)]
            payload[k][part, share:double] = pieces[i][:, pl.ds(width + start, share)]
        payload[k][:, double : 2 * double] = theirs[k]
        payload[k][:, 2 * double :] = terms[...]


def slices_of(pieces, width, share, flips):
    at = lax.axis_index("dp").astype(i32)
    rows = jnp.concatenate(pieces)
    return [
        jnp.concatenate(
            [
                lax.dynamic_slice_in_dim(rows, base + (at ^ flip) * share, share, axis=1)
                for base in (0, width)
            ],
            axis=1,
        )
        for flip in flips
    ]


def cut(pieces, width):
    size = lax.axis_size("dp")
    share = width // size
    if share % LANES:
        return jnp.stack(slices_of(pieces, width, share, range(1, size, 2)))
    return pl.pallas_call(
        functools.partial(cut_kernel, len(pieces)),
        out_shape=jax.ShapeDtypeStruct((size // 2, len(pieces) * CAP, 2 * share), bf16),
        in_specs=[SMEM] + [VMEM] * len(pieces),
        out_specs=VMEM,
        compiler_params=PARAMS,
        cost_estimate=SMALL,
    )(lax.axis_index("dp").astype(i32).reshape(1), *pieces)


def pack(pieces, theirs, terms, width):
    return list(packed(pieces, theirs, terms, width))


def packed(pieces, theirs, terms, width):
    size = lax.axis_size("dp")
    share = width // size
    if share % LANES:
        own = slices_of(pieces, width, share, range(0, size, 2))
        return [jnp.concatenate([own[k], theirs[k], terms], axis=1) for k in range(size // 2)]
    shape = jax.ShapeDtypeStruct((terms.shape[0], 4 * share + terms.shape[1]), bf16)
    return pl.pallas_call(
        functools.partial(pack_kernel, len(pieces)),
        out_shape=[shape] * (size // 2),
        in_specs=[SMEM] + [VMEM] * (len(pieces) + 2),
        out_specs=[VMEM] * (size // 2),
        compiler_params=PARAMS,
        cost_estimate=SMALL,
    )(lax.axis_index("dp").astype(i32).reshape(1), *pieces, theirs, terms)


def sum_kernel(chips, share, units, scale, first, *refs):
    got, others = refs[:chips], refs[chips]
    past = () if first else refs[chips + 1 : chips + 4]
    outs = refs[-5:-2]
    cols, terms = refs[-2:]
    rows = got[0].shape[0]
    for k in range(chips):
        for core in range(2):
            part = slice((2 * k + core) * rows, (2 * k + core + 1) * rows)
            cols[part, :] = got[k][:, 2 * core * share : 2 * (core + 1) * share]
        terms[2 * k * rows : (2 * k + 1) * rows, :] = got[k][:, 4 * share :]
        terms[(2 * k + 1) * rows : (2 * k + 2) * rows, :] = others[k * rows : (k + 1) * rows, :]
    for i in range(3):
        column = share if i == 2 else 0
        total = lax.dot_general(
            cols[:, column : column + share], terms[:, i * units : (i + 1) * units],
            (((0,), (0,)), ((), ())), preferred_element_type=f32,
        )
        if not first:
            total += past[i][...]
        outs[i][...] = total if scale is None else total * scale


def weight_sums(got, others, past, share, scale):
    chips = len(got)
    rows = got[0].shape[0]
    units = others.shape[1] // 3
    if share % LANES:
        wide = [jnp.concatenate([g[:, 2 * c * share : 2 * (c + 1) * share] for g in got]) for c in range(2)]
        near = jnp.concatenate([g[:, 4 * share :] for g in got])
        sums = []
        for i in range(3):
            total = 0.0 if past is None else past[i]
            for cols, terms in zip(wide, (near, others)):
                column = share if i == 2 else 0
                total += lax.dot_general(
                    cols[:, column : column + share], terms[:, i * units : (i + 1) * units],
                    (((0,), (0,)), ((), ())), preferred_element_type=f32,
                )
            sums.append(total if scale is None else total * scale)
        return sums
    past = [] if past is None else list(past)
    return pl.pallas_call(
        functools.partial(sum_kernel, chips, share, units, scale, not past),
        out_shape=[jax.ShapeDtypeStruct((share, units), f32)] * 3,
        in_specs=[VMEM] * (chips + 1 + len(past)),
        out_specs=[VMEM] * 3,
        scratch_shapes=[
            pltpu.VMEM((2 * chips * rows, 2 * share), bf16),
            pltpu.VMEM((2 * chips * rows, 3 * units), bf16),
        ],
        compiler_params=PARAMS,
        cost_estimate=SMALL,
    )(*got, others, *past)


def place_kernel(n_expert, me_ref, route_ref, prob_ref, tok_ref, cot_ref, placing_ref, *pieces):
    quarters = n_expert // HOT
    count, width = tok_ref.shape
    route = route_ref[...]
    hot = (route == lax.broadcasted_iota(i32, (16, count), 0)).astype(f32)
    before = lax.broadcasted_iota(i32, (count, count), 0) < lax.broadcasted_iota(i32, (count, count), 1)
    earlier = jnp.dot(hot.astype(bf16), before.astype(f32).astype(bf16), preferred_element_type=f32)
    rank = jnp.sum(earlier * hot, axis=0, keepdims=True).astype(i32)
    slot = lax.broadcasted_iota(i32, (CAP, count), 0)
    prob = prob_ref[...].astype(f32)
    for k in range(n_expert):
        owner = lax.rem(me_ref[0] + k, n_expert) // quarters
        block = jnp.where((route == owner) & (rank == slot), 1.0, 0.0)
        placing_ref[k * CAP : (k + 1) * CAP, :] = block.astype(bf16)
        slot_prob = jnp.sum(block * prob, axis=1, keepdims=True)
        pieces[k][:, 2 * width :] = jnp.broadcast_to(slot_prob, (CAP, LANES)).astype(bf16)
    for start, source in ((0, tok_ref), (width, cot_ref)):
        for at in range(0, width, 512):
            part = jnp.dot(placing_ref[...], source[:, at : at + 512], preferred_element_type=f32)
            part = part.astype(bf16)
            for k in range(n_expert):
                pieces[k][:, start + at : start + at + 512] = part[k * CAP : (k + 1) * CAP]


def place(me, route, prob, tokens, cotangent, n_expert):
    count, width = tokens.shape
    outs = pl.pallas_call(
        functools.partial(place_kernel, n_expert),
        out_shape=[jax.ShapeDtypeStruct((n_expert * CAP, count), bf16)]
        + [jax.ShapeDtypeStruct((CAP, 2 * width + LANES), bf16)] * n_expert,
        in_specs=[SMEM] + [VMEM] * 4,
        out_specs=[VMEM] * (n_expert + 1),
        cost_estimate=SMALL,
    )(me.reshape(1), route.reshape(1, count), prob.reshape(1, count), tokens, cotangent)
    return outs[0], outs[1:]


def halves(whole):
    high = whole.astype(bf16)
    return high, (whole - high.astype(f32)).astype(bf16)


def weight_scratch(count, depth, units):
    return [
        pltpu.VMEM((count, depth, units), f32),
        pltpu.SemaphoreType.DMA((count, depth // BLOCK)),
    ]


def fetch(weights, buffer, arrived):
    copies = []
    for at in range(weights[0].shape[0] // BLOCK):
        here = slice(at * BLOCK, (at + 1) * BLOCK)
        for i, weight in enumerate(weights):
            copy = pltpu.make_async_copy(weight.at[here, :], buffer.at[i, here, :], arrived.at[i, at])
            copy.start()
            copies.append(copy)
    return copies


def times_weights(factors, buffer, copies):
    depth = buffer.shape[1]
    for at in range(depth // BLOCK):
        here = slice(at * BLOCK, (at + 1) * BLOCK)
        for i, (rows, total) in enumerate(factors):
            copies[at * len(factors) + i].wait()
            high, low = halves(buffer[i, here, :])
            row = rows[:, here]
            part = jnp.dot(row, high, preferred_element_type=f32)
            part += jnp.dot(row, low, preferred_element_type=f32)
            if at == 0:
                total[...] = part
            else:
                total[...] += part


def gate_factors(gate, up, prob):
    sig = jax.nn.sigmoid(gate)
    act = gate * sig
    hidden = act * up
    return prob * act, prob * (up * sig * (1.0 + gate * (1.0 - sig))), hidden


def against(left, right):
    return lax.dot_general(left, right, (((1,), (1,)), ((), ())), preferred_element_type=f32)


def chunk_kernel(count, *refs):
    pieces, weights, terms_ref = refs[:count], refs[count : count + 3], refs[count + 3]
    outs = refs[count + 4 : 2 * count + 4]
    tok, cot, gate_sum, up_sum, back_sum, low_ref, buffer, arrived = refs[2 * count + 4 :]
    depth, units = weights[0].shape
    copies = fetch(weights, buffer, arrived)
    for k, piece in enumerate(pieces):
        part = slice(k * CAP, (k + 1) * CAP)
        tok[part, :] = piece[:, :depth]
        cot[part, :] = piece[:, depth : 2 * depth]
    times_weights(((tok, gate_sum), (tok, up_sum), (cot, back_sum)), buffer, copies)
    for k, piece in enumerate(pieces):
        part = slice(k * CAP, (k + 1) * CAP)
        prob = piece[:, 2 * depth :].astype(f32)[:, :1]
        act, slope, hidden = gate_factors(gate_sum[part, :], up_sum[part, :], prob)
        back = back_sum[part, :]
        total = jnp.sum(hidden * back, axis=1, keepdims=True)
        outs[k][:, depth:] = jnp.broadcast_to(total, (CAP, LANES)).astype(outs[k].dtype)
        for at, factor in ((0, slope), (units, act)):
            high, low = halves(factor * back)
            terms_ref[part, at : at + units] = high
            low_ref[part, at : at + units] = low
        terms_ref[part, 2 * units :] = (prob * hidden).astype(bf16)
    for at in range(0, depth, BLOCK):
        total = None
        for i in range(2):
            high, low = halves(buffer[i, at : at + BLOCK, :])
            grad_hi = terms_ref[:, i * units : (i + 1) * units]
            grad_lo = low_ref[:, i * units : (i + 1) * units]
            both = against(high, jnp.concatenate([grad_hi, grad_lo], axis=0)).T
            part = both[: count * CAP] + both[count * CAP :] + against(low, grad_hi).T
            total = part if total is None else total + part
        for k, out in enumerate(outs):
            out[:, at : at + BLOCK] = total[k * CAP : (k + 1) * CAP].astype(out.dtype)


def chunk_rows(pieces, weights, back_type, passes):
    count = len(pieces)
    depth, units = weights[0].shape
    rows = count * CAP
    outs = pl.pallas_call(
        functools.partial(chunk_kernel, count),
        out_shape=[jax.ShapeDtypeStruct((rows, 3 * units), bf16)]
        + [jax.ShapeDtypeStruct((CAP, depth + LANES), back_type)] * count,
        in_specs=[VMEM] * count + [HBM] * 3,
        out_specs=[VMEM] * (count + 1),
        scratch_shapes=[pltpu.VMEM((rows, depth), bf16)] * 2
        + [pltpu.VMEM((rows, units), f32)] * 3
        + [pltpu.VMEM((rows, 2 * units), bf16)]
        + weight_scratch(3, depth, units),
        compiler_params=ALONE,
        cost_estimate=pl.CostEstimate(flops=passes * 192 * depth * units, bytes_accessed=MIB, transcendentals=0),
    )(*pieces, *weights)
    return outs[0], outs[1:]


def take_kernel(n_expert, placing_ref, *refs):
    pieces = refs[:n_expert]
    out_ref, prob_ref, rows = refs[n_expert:]
    count, width = out_ref.shape
    exact = rows.dtype != bf16
    for k in range(n_expert):
        rows[k * CAP : (k + 1) * CAP, :] = pieces[k][...]
    placing = placing_ref[...].astype(rows.dtype)
    for at in range(0, width, 512):
        part = lax.dot_general(
            placing, rows[:, at : at + 512], (((0,), (0,)), ((), ())),
            precision=highest if exact else None, preferred_element_type=f32,
        )
        out_ref[:, at : at + 512] = part.astype(bf16)
    column = rows[:, width:].astype(f32)[:, :1]
    prob_ref[...] = jnp.sum(placing_ref[...].astype(f32) * column, axis=0, keepdims=True).astype(bf16)


def take(placing, pieces):
    n_expert = len(pieces)
    count = placing.shape[1]
    width = pieces[0].shape[1] - LANES
    grad, prob = pl.pallas_call(
        functools.partial(take_kernel, n_expert),
        out_shape=[
            jax.ShapeDtypeStruct((count, width), bf16),
            jax.ShapeDtypeStruct((1, count), bf16),
        ],
        in_specs=[VMEM] * (n_expert + 1),
        out_specs=[VMEM] * 2,
        scratch_shapes=[pltpu.VMEM((n_expert * CAP, width + LANES), pieces[0].dtype)],
        compiler_params=pltpu.CompilerParams(vmem_limit_bytes=32 * MIB) if pieces[0].dtype != bf16 else PARAMS,
        cost_estimate=SMALL,
    )(placing, *pieces)
    return grad, prob.reshape(count)


def shards(tokens, cotangent, route, prob, w_gate, w_up, w_down):
    n_expert = lax.axis_size("expert")
    n_dp = lax.axis_size("dp")
    width = tokens.shape[1]
    share = width // n_dp
    scale = 1.0 / math.sqrt(tokens.shape[0] * n_dp * n_expert)
    back_type = bf16 if n_expert == HOT else f32
    me = lax.axis_index("expert").astype(i32)
    weights = (w_gate[0], w_up[0], w_down[0])
    chips = range(n_dp // 2)
    home = [None] * n_expert

    def exchange(payload):
        return [payload[0]] + [flipped(payload[k], "dp", 2 * k) for k in chips[1:]]

    def swap(*groups):
        terms = [g[:, 4 * share :] for got in groups for g in got]
        other = flipped(jnp.concatenate(terms), "dp", 1)
        cuts, at = [], 0
        for got in groups:
            count = len(got) * got[0].shape[0]
            cuts.append(other[at : at + count])
            at += count
        return cuts

    def give_back(home, shifts, back):
        home = list(home)
        for i, k in enumerate(shifts):
            home[k] = shifted(back[i], "expert", n_expert - k)
        return home

    placing, pieces = place(me, route, prob, tokens, cotangent, n_expert)
    odd = list(range(1, n_expert, 2))
    even = list(range(2, n_expert, 2))
    first = [shifted(pieces[k], "expert", k) for k in odd]

    terms, back = chunk_rows(pieces[:1], weights, back_type, 36)
    home[0] = back[0]
    own, terms = lax.optimization_barrier((pieces[0], terms))
    theirs = flipped(cut([own], width), "dp", 1)
    payload = pack([own], theirs, terms, width)
    late, payload[-1], first, _ = lax.optimization_barrier(
        ([pieces[k] for k in even], payload[-1], first, payload[0])
    )
    second = [shifted(piece, "expert", k) for piece, k in zip(late, even)]
    got_local = exchange(payload)

    theirs = flipped(cut(first, width), "dp", 1)
    terms, back = chunk_rows(first, weights, back_type, 24)
    payload = pack(first, theirs, terms, width)
    payload, got_local = lax.optimization_barrier((payload, got_local))
    got_first = exchange(payload)

    second, back, _ = lax.optimization_barrier((second, back, payload))
    home = give_back(home, odd, back)
    theirs = flipped(cut(second, width), "dp", 1)
    terms, back = chunk_rows(second, weights, back_type, 12)
    payload, got_first, back, home = lax.optimization_barrier(
        (pack(second, theirs, terms, width), got_first, back, home)
    )
    home = give_back(home, even, back)
    got_second = exchange(payload)
    local_other, first_other = swap(got_local, got_first)
    sums = weight_sums(got_local, local_other, None, share, None)
    sums = weight_sums(got_first, first_other, sums, share, None)
    got_second, home, sums = lax.optimization_barrier((got_second, home, sums))
    sums = weight_sums(got_second, swap(got_second)[0], sums, share, scale)

    grad_input, grad_prob = take(placing, home)
    return (grad_input, grad_prob, *[total[None] for total in sums])


def solution(mesh):
    placed = (
        P(("dp", "expert"), None),
        P(("dp", "expert"), None),
        P(("dp", "expert"), None),
        P(("dp", "expert")),
        P("expert", None, None),
        P("expert", None, None),
        P("expert", None, None),
    )
    return jax.shard_map(
        shards,
        mesh=mesh,
        in_specs=placed,
        out_specs=(
            P(("dp", "expert"), None),
            P(("dp", "expert")),
            P("expert", "dp", None),
            P("expert", "dp", None),
            P("expert", "dp", None),
        ),
        check_vma=False,
    )
```

```python
import functools
import math

import jax
import jax.numpy as jnp
from jax import lax
from jax.experimental import pallas as pl
from jax.experimental.pallas import tpu as pltpu
from jax.sharding import PartitionSpec as P

HOT = 4
CAP = 48
LANES = 128
BLOCK = 256
MIB = 1 << 20

highest = lax.Precision.HIGHEST
f32 = jnp.float32
bf16 = jnp.bfloat16
i32 = jnp.int32
VMEM = pl.BlockSpec(memory_space=pltpu.VMEM)
SMEM = pl.BlockSpec(memory_space=pltpu.SMEM)
HBM = pl.BlockSpec(memory_space=pltpu.HBM)
PARAMS = pltpu.CompilerParams(vmem_limit_bytes=14 * MIB)
ALONE = pltpu.CompilerParams(vmem_limit_bytes=52 * MIB)
SMALL = pl.CostEstimate(flops=0, bytes_accessed=1024, transcendentals=0)


def shifted(values, axis, by):
    size = lax.axis_size(axis)
    return lax.ppermute(values, axis, [(i, (i + by) % size) for i in range(size)])


def flipped(values, axis, mask):
    size = lax.axis_size(axis)
    return lax.ppermute(values, axis, [(i, i ^ mask) for i in range(size)])


def cut_kernel(count, at_ref, *refs):
    pieces, theirs = refs[:count], refs[count]
    chips, _, double = theirs.shape
    share = double // 2
    width = 2 * chips * share
    for k in range(chips):
        start = pl.multiple_of((at_ref[0] ^ (2 * k + 1)) * share, share)
        for i in range(count):
            part = slice(i * CAP, (i + 1) * CAP)
            theirs[k, part, :share] = pieces[i][:, pl.ds(start, share)]
            theirs[k, part, share:] = pieces[i][:, pl.ds(width + start, share)]


def pack_kernel(count, at_ref, *refs):
    pieces, theirs = refs[:count], refs[count]
    chips, _, double = theirs.shape
    payload, terms = refs[-chips:], refs[count + 1 : -chips]
    share = double // 2
    width = 2 * chips * share
    for k in range(chips):
        start = pl.multiple_of((at_ref[0] ^ (2 * k)) * share, share)
        for i in range(count):
            part = slice(i * CAP, (i + 1) * CAP)
            payload[k][part, :share] = pieces[i][:, pl.ds(start, share)]
            payload[k][part, share:double] = pieces[i][:, pl.ds(width + start, share)]
        payload[k][:, double : 2 * double] = theirs[k]
        for term in terms:
            payload[k][:, 2 * double :] = term[...]


def slices_of(pieces, width, share, flips):
    at = lax.axis_index("dp").astype(i32)
    rows = jnp.concatenate(pieces)
    return [
        jnp.concatenate(
            [
                lax.dynamic_slice_in_dim(rows, base + (at ^ flip) * share, share, axis=1)
                for base in (0, width)
            ],
            axis=1,
        )
        for flip in flips
    ]


def cut(pieces, width):
    size = lax.axis_size("dp")
    share = width // size
    if share % LANES:
        return jnp.stack(slices_of(pieces, width, share, range(1, size, 2)))
    return pl.pallas_call(
        functools.partial(cut_kernel, len(pieces)),
        out_shape=jax.ShapeDtypeStruct((size // 2, len(pieces) * CAP, 2 * share), bf16),
        in_specs=[SMEM] + [VMEM] * len(pieces),
        out_specs=VMEM,
        compiler_params=PARAMS,
        cost_estimate=SMALL,
    )(lax.axis_index("dp").astype(i32).reshape(1), *pieces)


def pack(pieces, theirs, width, *terms):
    size = lax.axis_size("dp")
    share = width // size
    if share % LANES:
        own = slices_of(pieces, width, share, range(0, size, 2))
        return [jnp.concatenate([own[k], theirs[k], *terms], axis=1) for k in range(size // 2)]
    wide = 4 * share + sum(term.shape[1] for term in terms)
    shape = jax.ShapeDtypeStruct((theirs.shape[1], wide), bf16)
    return list(
        pl.pallas_call(
            functools.partial(pack_kernel, len(pieces)),
            out_shape=[shape] * (size // 2),
            in_specs=[SMEM] + [VMEM] * (len(pieces) + 1 + len(terms)),
            out_specs=[VMEM] * (size // 2),
            compiler_params=PARAMS,
            cost_estimate=SMALL,
        )(lax.axis_index("dp").astype(i32).reshape(1), *pieces, theirs, *terms)
    )


def sum_kernel(chips, share, units, scale, first, *refs):
    got, near, others = refs[:chips], refs[chips : 2 * chips], refs[2 * chips]
    past = () if first else refs[2 * chips + 1 : 2 * chips + 4]
    outs = refs[-5:-2]
    cols, terms = refs[-2:]
    rows = got[0].shape[0]
    start = near[0].shape[1] - 3 * units
    for k in range(chips):
        for core in range(2):
            part = slice((2 * k + core) * rows, (2 * k + core + 1) * rows)
            cols[part, :] = got[k][:, 2 * core * share : 2 * (core + 1) * share]
        terms[2 * k * rows : (2 * k + 1) * rows, :] = near[k][:, start:]
        terms[(2 * k + 1) * rows : (2 * k + 2) * rows, :] = others[k * rows : (k + 1) * rows, :]
    for i in range(3):
        column = share if i == 2 else 0
        total = lax.dot_general(
            cols[:, column : column + share], terms[:, i * units : (i + 1) * units],
            (((0,), (0,)), ((), ())), preferred_element_type=f32,
        )
        if not first:
            total += past[i][...]
        outs[i][...] = total if scale is None else total * scale


def weight_sums(got, near, others, past, share, scale):
    chips = len(got)
    rows = got[0].shape[0]
    units = others.shape[1] // 3
    if share % LANES:
        wide = [jnp.concatenate([g[:, 2 * c * share : 2 * (c + 1) * share] for g in got]) for c in range(2)]
        own = jnp.concatenate([n[:, -3 * units :] for n in near])
        sums = []
        for i in range(3):
            total = 0.0 if past is None else past[i]
            for cols, terms in zip(wide, (own, others)):
                column = share if i == 2 else 0
                total += lax.dot_general(
                    cols[:, column : column + share], terms[:, i * units : (i + 1) * units],
                    (((0,), (0,)), ((), ())), preferred_element_type=f32,
                )
            sums.append(total if scale is None else total * scale)
        return sums
    past = [] if past is None else list(past)
    return pl.pallas_call(
        functools.partial(sum_kernel, chips, share, units, scale, not past),
        out_shape=[jax.ShapeDtypeStruct((share, units), f32)] * 3,
        in_specs=[VMEM] * (2 * chips + 1 + len(past)),
        out_specs=[VMEM] * 3,
        scratch_shapes=[
            pltpu.VMEM((2 * chips * rows, 2 * share), bf16),
            pltpu.VMEM((2 * chips * rows, 3 * units), bf16),
        ],
        compiler_params=PARAMS,
        cost_estimate=SMALL,
    )(*got, *near, others, *past)


def place_kernel(n_expert, me_ref, route_ref, prob_ref, tok_ref, cot_ref, placing_ref, *pieces):
    quarters = n_expert // HOT
    count, width = tok_ref.shape
    route = route_ref[...]
    hot = (route == lax.broadcasted_iota(i32, (16, count), 0)).astype(f32)
    before = lax.broadcasted_iota(i32, (count, count), 0) < lax.broadcasted_iota(i32, (count, count), 1)
    earlier = jnp.dot(hot.astype(bf16), before.astype(f32).astype(bf16), preferred_element_type=f32)
    rank = jnp.sum(earlier * hot, axis=0, keepdims=True).astype(i32)
    slot = lax.broadcasted_iota(i32, (CAP, count), 0)
    prob = prob_ref[...].astype(f32)
    for k in range(n_expert):
        owner = lax.rem(me_ref[0] + k, n_expert) // quarters
        block = jnp.where((route == owner) & (rank == slot), 1.0, 0.0)
        placing_ref[k * CAP : (k + 1) * CAP, :] = block.astype(bf16)
        slot_prob = jnp.sum(block * prob, axis=1, keepdims=True)
        pieces[k][:, 2 * width :] = jnp.broadcast_to(slot_prob, (CAP, LANES)).astype(bf16)
    for start, source in ((0, tok_ref), (width, cot_ref)):
        for at in range(0, width, 512):
            part = jnp.dot(placing_ref[...], source[:, at : at + 512], preferred_element_type=f32)
            part = part.astype(bf16)
            for k in range(n_expert):
                pieces[k][:, start + at : start + at + 512] = part[k * CAP : (k + 1) * CAP]


def place(me, route, prob, tokens, cotangent, n_expert):
    count, width = tokens.shape
    outs = pl.pallas_call(
        functools.partial(place_kernel, n_expert),
        out_shape=[jax.ShapeDtypeStruct((n_expert * CAP, count), bf16)]
        + [jax.ShapeDtypeStruct((CAP, 2 * width + LANES), bf16)] * n_expert,
        in_specs=[SMEM] + [VMEM] * 4,
        out_specs=[VMEM] * (n_expert + 1),
        cost_estimate=SMALL,
    )(me.reshape(1), route.reshape(1, count), prob.reshape(1, count), tokens, cotangent)
    return outs[0], outs[1:]


def halves(whole):
    high = whole.astype(bf16)
    return high, (whole - high.astype(f32)).astype(bf16)


def weight_scratch(count, depth, units):
    return [
        pltpu.VMEM((count, depth, units), f32),
        pltpu.SemaphoreType.DMA((count, depth // BLOCK)),
    ]


def fetch(weights, buffer, arrived):
    copies = []
    for at in range(weights[0].shape[0] // BLOCK):
        here = slice(at * BLOCK, (at + 1) * BLOCK)
        for i, weight in enumerate(weights):
            copy = pltpu.make_async_copy(weight.at[here, :], buffer.at[i, here, :], arrived.at[i, at])
            copy.start()
            copies.append(copy)
    return copies


def times_weights(factors, buffer, copies):
    depth = buffer.shape[1]
    for at in range(depth // BLOCK):
        here = slice(at * BLOCK, (at + 1) * BLOCK)
        for i, (rows, total) in enumerate(factors):
            copies[at * len(factors) + i].wait()
            high, low = halves(buffer[i, here, :])
            row = rows[:, here]
            part = jnp.dot(row, high, preferred_element_type=f32)
            part += jnp.dot(row, low, preferred_element_type=f32)
            if at == 0:
                total[...] = part
            else:
                total[...] += part


def gate_factors(gate, up, prob):
    sig = jax.nn.sigmoid(gate)
    act = gate * sig
    hidden = act * up
    return prob * act, prob * (up * sig * (1.0 + gate * (1.0 - sig))), hidden


def against(left, right):
    return lax.dot_general(left, right, (((1,), (1,)), ((), ())), preferred_element_type=f32)


def chunk_kernel(count, *refs):
    pieces, weights, terms_ref = refs[:count], refs[count : count + 3], refs[count + 3]
    outs = refs[count + 4 : 2 * count + 4]
    tok, cot, gate_sum, up_sum, back_sum, low_ref, buffer, arrived = refs[2 * count + 4 :]
    depth, units = weights[0].shape
    copies = fetch(weights, buffer, arrived)
    for k, piece in enumerate(pieces):
        part = slice(k * CAP, (k + 1) * CAP)
        tok[part, :] = piece[:, :depth]
        cot[part, :] = piece[:, depth : 2 * depth]
    times_weights(((tok, gate_sum), (tok, up_sum), (cot, back_sum)), buffer, copies)
    for k, piece in enumerate(pieces):
        part = slice(k * CAP, (k + 1) * CAP)
        prob = piece[:, 2 * depth :].astype(f32)[:, :1]
        act, slope, hidden = gate_factors(gate_sum[part, :], up_sum[part, :], prob)
        back = back_sum[part, :]
        total = jnp.sum(hidden * back, axis=1, keepdims=True)
        outs[k][:, depth:] = jnp.broadcast_to(total, (CAP, LANES)).astype(outs[k].dtype)
        for at, factor in ((0, slope), (units, act)):
            high, low = halves(factor * back)
            terms_ref[part, at : at + units] = high
            low_ref[part, at : at + units] = low
        terms_ref[part, 2 * units :] = (prob * hidden).astype(bf16)
    for at in range(0, depth, BLOCK):
        total = None
        for i in range(2):
            high, low = halves(buffer[i, at : at + BLOCK, :])
            grad_hi = terms_ref[:, i * units : (i + 1) * units]
            grad_lo = low_ref[:, i * units : (i + 1) * units]
            both = against(high, jnp.concatenate([grad_hi, grad_lo], axis=0)).T
            part = both[: count * CAP] + both[count * CAP :] + against(low, grad_hi).T
            total = part if total is None else total + part
        for k, out in enumerate(outs):
            out[:, at : at + BLOCK] = total[k * CAP : (k + 1) * CAP].astype(out.dtype)


def chunk_rows(pieces, weights, back_type, passes):
    count = len(pieces)
    depth, units = weights[0].shape
    rows = count * CAP
    outs = pl.pallas_call(
        functools.partial(chunk_kernel, count),
        out_shape=[jax.ShapeDtypeStruct((rows, 3 * units), bf16)]
        + [jax.ShapeDtypeStruct((CAP, depth + LANES), back_type)] * count,
        in_specs=[VMEM] * count + [HBM] * 3,
        out_specs=[VMEM] * (count + 1),
        scratch_shapes=[pltpu.VMEM((rows, depth), bf16)] * 2
        + [pltpu.VMEM((rows, units), f32)] * 3
        + [pltpu.VMEM((rows, 2 * units), bf16)]
        + weight_scratch(3, depth, units),
        compiler_params=ALONE,
        cost_estimate=pl.CostEstimate(flops=passes * 192 * depth * units, bytes_accessed=MIB, transcendentals=0),
    )(*pieces, *weights)
    return outs[0], outs[1:]


def take_kernel(n_expert, placing_ref, *refs):
    pieces = refs[:n_expert]
    out_ref, prob_ref, rows = refs[n_expert:]
    count, width = out_ref.shape
    exact = rows.dtype != bf16
    for k in range(n_expert):
        rows[k * CAP : (k + 1) * CAP, :] = pieces[k][...]
    placing = placing_ref[...].astype(rows.dtype)
    for at in range(0, width, 512):
        part = lax.dot_general(
            placing, rows[:, at : at + 512], (((0,), (0,)), ((), ())),
            precision=highest if exact else None, preferred_element_type=f32,
        )
        out_ref[:, at : at + 512] = part.astype(bf16)
    column = rows[:, width:].astype(f32)[:, :1]
    prob_ref[...] = jnp.sum(placing_ref[...].astype(f32) * column, axis=0, keepdims=True).astype(bf16)


def take(placing, pieces):
    n_expert = len(pieces)
    count = placing.shape[1]
    width = pieces[0].shape[1] - LANES
    grad, prob = pl.pallas_call(
        functools.partial(take_kernel, n_expert),
        out_shape=[
            jax.ShapeDtypeStruct((count, width), bf16),
            jax.ShapeDtypeStruct((1, count), bf16),
        ],
        in_specs=[VMEM] * (n_expert + 1),
        out_specs=[VMEM] * 2,
        scratch_shapes=[pltpu.VMEM((n_expert * CAP, width + LANES), pieces[0].dtype)],
        compiler_params=pltpu.CompilerParams(vmem_limit_bytes=32 * MIB) if pieces[0].dtype != bf16 else PARAMS,
        cost_estimate=SMALL,
    )(placing, *pieces)
    return grad, prob.reshape(count)


def shards(tokens, cotangent, route, prob, w_gate, w_up, w_down):
    n_expert = lax.axis_size("expert")
    n_dp = lax.axis_size("dp")
    width = tokens.shape[1]
    units = w_gate.shape[2]
    share = width // n_dp
    scale = 1.0 / math.sqrt(tokens.shape[0] * n_dp * n_expert)
    back_type = bf16 if n_expert == HOT else f32
    me = lax.axis_index("expert").astype(i32)
    weights = (w_gate[0], w_up[0], w_down[0])
    chips = range(n_dp // 2)
    home = [None] * n_expert

    def exchange(payload):
        return [payload[0]] + [flipped(part, "dp", 2 * k) for k, part in enumerate(payload) if k]

    def swap(*groups):
        terms = [near[:, -3 * units :] for group in groups for near in group]
        other = flipped(jnp.concatenate(terms), "dp", 1)
        cuts, at = [], 0
        for group in groups:
            count = len(group) * group[0].shape[0]
            cuts.append(other[at : at + count])
            at += count
        return cuts

    def give_back(home, shifts, back):
        home = list(home)
        for i, k in enumerate(shifts):
            home[k] = shifted(back[i], "expert", n_expert - k)
        return home

    placing, pieces = place(me, route, prob, tokens, cotangent, n_expert)
    odd = list(range(1, n_expert, 2))
    even = list(range(2, n_expert, 2))
    first = [shifted(pieces[k], "expert", k) for k in odd]

    terms, back = chunk_rows(pieces[:1], weights, back_type, 36)
    home[0] = back[0]
    own, terms = lax.optimization_barrier((pieces[0], terms))
    theirs = flipped(cut([own], width), "dp", 1)
    payload = pack([own], theirs, width, terms)
    near_local = exchange(payload[:-1])
    late, first, near_local, payload[-1] = lax.optimization_barrier(
        ([pieces[k] for k in even], first, near_local, payload[-1])
    )
    got_local = near_local + [flipped(payload[-1], "dp", 2 * chips[-1])]
    second = [shifted(piece, "expert", k) for piece, k in zip(late, even)]

    theirs = flipped(cut(first, width), "dp", 1)
    got_first = exchange(pack(first, theirs, width))
    terms, back = chunk_rows(first, weights, back_type, 24)
    terms, got_first, got_local = lax.optimization_barrier((terms, got_first, got_local))
    near_first = exchange([terms] * len(chips))

    second, back, _ = lax.optimization_barrier((second, back, terms))
    home = give_back(home, odd, back)
    theirs = flipped(cut(second, width), "dp", 1)
    terms, back_even = chunk_rows(second, weights, back_type, 12)
    payload, near_first, back_even, home = lax.optimization_barrier(
        (pack(second, theirs, width, terms), near_first, back_even, home)
    )
    home = give_back(home, even, back_even)
    got_second = exchange(payload)
    local_other, first_other = swap(got_local, near_first)
    sums = weight_sums(got_local, got_local, local_other, None, share, None)
    sums = weight_sums(got_first, near_first, first_other, sums, share, None)
    got_second, home, sums = lax.optimization_barrier((got_second, home, sums))
    sums = weight_sums(got_second, got_second, swap(got_second)[0], sums, share, scale)

    grad_input, grad_prob = take(placing, home)
    return (grad_input, grad_prob, *[total[None] for total in sums])


def solution(mesh):
    placed = (
        P(("dp", "expert"), None),
        P(("dp", "expert"), None),
        P(("dp", "expert"), None),
        P(("dp", "expert")),
        P("expert", None, None),
        P("expert", None, None),
        P("expert", None, None),
    )
    return jax.shard_map(
        shards,
        mesh=mesh,
        in_specs=placed,
        out_specs=(
            P(("dp", "expert"), None),
            P(("dp", "expert")),
            P("expert", "dp", None),
            P("expert", "dp", None),
            P("expert", "dp", None),
        ),
        check_vma=False,
    )
```

```python
import functools
import math

import jax
import jax.numpy as jnp
from jax import lax
from jax.experimental import pallas as pl
from jax.experimental.pallas import tpu as pltpu
from jax.sharding import PartitionSpec as P

HOT = 4
CAP = 48
LANES = 128
BLOCK = 512
MIB = 1 << 20

highest = lax.Precision.HIGHEST
f32 = jnp.float32
bf16 = jnp.bfloat16
i32 = jnp.int32
VMEM = pl.BlockSpec(memory_space=pltpu.VMEM)
SMEM = pl.BlockSpec(memory_space=pltpu.SMEM)
HBM = pl.BlockSpec(memory_space=pltpu.HBM)
PARAMS = pltpu.CompilerParams(vmem_limit_bytes=14 * MIB)
ALONE = pltpu.CompilerParams(vmem_limit_bytes=52 * MIB)
SMALL = pl.CostEstimate(flops=0, bytes_accessed=1024, transcendentals=0)


def shifted(values, axis, by):
    size = lax.axis_size(axis)
    return lax.ppermute(values, axis, [(i, (i + by) % size) for i in range(size)])


def flipped(values, axis, mask):
    size = lax.axis_size(axis)
    return lax.ppermute(values, axis, [(i, i ^ mask) for i in range(size)])


def cut_kernel(count, at_ref, *refs):
    pieces, theirs = refs[:count], refs[count]
    chips, _, double = theirs.shape
    share = double // 2
    width = 2 * chips * share
    for k in range(chips):
        start = pl.multiple_of((at_ref[0] ^ (2 * k + 1)) * share, share)
        for i in range(count):
            part = slice(i * CAP, (i + 1) * CAP)
            theirs[k, part, :share] = pieces[i][:, pl.ds(start, share)]
            theirs[k, part, share:] = pieces[i][:, pl.ds(width + start, share)]


def pack_kernel(count, at_ref, *refs):
    pieces, theirs, terms, payload = refs[:count], refs[count], refs[count + 1], refs[count + 2 :]
    chips, _, double = theirs.shape
    share = double // 2
    width = 2 * chips * share
    for k in range(chips):
        start = pl.multiple_of((at_ref[0] ^ (2 * k)) * share, share)
        for i in range(count):
            part = slice(i * CAP, (i + 1) * CAP)
            payload[k][part, :share] = pieces[i][:, pl.ds(start, share)]
            payload[k][part, share:double] = pieces[i][:, pl.ds(width + start, share)]
        payload[k][:, double : 2 * double] = theirs[k]
        payload[k][:, 2 * double :] = terms[...]


def slices_of(pieces, width, share, flips):
    at = lax.axis_index("dp").astype(i32)
    rows = jnp.concatenate(pieces)
    return [
        jnp.concatenate(
            [
                lax.dynamic_slice_in_dim(rows, base + (at ^ flip) * share, share, axis=1)
                for base in (0, width)
            ],
            axis=1,
        )
        for flip in flips
    ]


def cut(pieces, width):
    size = lax.axis_size("dp")
    share = width // size
    if share % LANES:
        return jnp.stack(slices_of(pieces, width, share, range(1, size, 2)))
    return pl.pallas_call(
        functools.partial(cut_kernel, len(pieces)),
        out_shape=jax.ShapeDtypeStruct((size // 2, len(pieces) * CAP, 2 * share), bf16),
        in_specs=[SMEM] + [VMEM] * len(pieces),
        out_specs=VMEM,
        compiler_params=PARAMS,
        cost_estimate=SMALL,
    )(lax.axis_index("dp").astype(i32).reshape(1), *pieces)


def pack(pieces, theirs, terms, width):
    return list(packed(pieces, theirs, terms, width))


def packed(pieces, theirs, terms, width):
    size = lax.axis_size("dp")
    share = width // size
    if share % LANES:
        own = slices_of(pieces, width, share, range(0, size, 2))
        return [jnp.concatenate([own[k], theirs[k], terms], axis=1) for k in range(size // 2)]
    shape = jax.ShapeDtypeStruct((terms.shape[0], 4 * share + terms.shape[1]), bf16)
    return pl.pallas_call(
        functools.partial(pack_kernel, len(pieces)),
        out_shape=[shape] * (size // 2),
        in_specs=[SMEM] + [VMEM] * (len(pieces) + 2),
        out_specs=[VMEM] * (size // 2),
        compiler_params=PARAMS,
        cost_estimate=SMALL,
    )(lax.axis_index("dp").astype(i32).reshape(1), *pieces, theirs, terms)


def sum_kernel(chips, share, units, scale, first, *refs):
    got, others = refs[:chips], refs[chips]
    past = () if first else refs[chips + 1 : chips + 4]
    outs = refs[-5:-2]
    cols, terms = refs[-2:]
    rows = got[0].shape[0]
    for k in range(chips):
        for core in range(2):
            part = slice((2 * k + core) * rows, (2 * k + core + 1) * rows)
            cols[part, :] = got[k][:, 2 * core * share : 2 * (core + 1) * share]
        terms[2 * k * rows : (2 * k + 1) * rows, :] = got[k][:, 4 * share :]
        terms[(2 * k + 1) * rows : (2 * k + 2) * rows, :] = others[k * rows : (k + 1) * rows, :]
    for i in range(3):
        column = share if i == 2 else 0
        total = lax.dot_general(
            cols[:, column : column + share], terms[:, i * units : (i + 1) * units],
            (((0,), (0,)), ((), ())), preferred_element_type=f32,
        )
        if not first:
            total += past[i][...]
        outs[i][...] = total if scale is None else total * scale


def weight_sums(got, others, past, share, scale):
    chips = len(got)
    rows = got[0].shape[0]
    units = others.shape[1] // 3
    if share % LANES:
        wide = [jnp.concatenate([g[:, 2 * c * share : 2 * (c + 1) * share] for g in got]) for c in range(2)]
        near = jnp.concatenate([g[:, 4 * share :] for g in got])
        sums = []
        for i in range(3):
            total = 0.0 if past is None else past[i]
            for cols, terms in zip(wide, (near, others)):
                column = share if i == 2 else 0
                total += lax.dot_general(
                    cols[:, column : column + share], terms[:, i * units : (i + 1) * units],
                    (((0,), (0,)), ((), ())), preferred_element_type=f32,
                )
            sums.append(total if scale is None else total * scale)
        return sums
    past = [] if past is None else list(past)
    return pl.pallas_call(
        functools.partial(sum_kernel, chips, share, units, scale, not past),
        out_shape=[jax.ShapeDtypeStruct((share, units), f32)] * 3,
        in_specs=[VMEM] * (chips + 1 + len(past)),
        out_specs=[VMEM] * 3,
        scratch_shapes=[
            pltpu.VMEM((2 * chips * rows, 2 * share), bf16),
            pltpu.VMEM((2 * chips * rows, 3 * units), bf16),
        ],
        compiler_params=PARAMS,
        cost_estimate=SMALL,
    )(*got, others, *past)


def place_kernel(n_expert, me_ref, route_ref, prob_ref, tok_ref, cot_ref, placing_ref, *pieces):
    quarters = n_expert // HOT
    count, width = tok_ref.shape
    route = route_ref[...]
    hot = (route == lax.broadcasted_iota(i32, (16, count), 0)).astype(f32)
    before = lax.broadcasted_iota(i32, (count, count), 0) < lax.broadcasted_iota(i32, (count, count), 1)
    earlier = jnp.dot(hot.astype(bf16), before.astype(f32).astype(bf16), preferred_element_type=f32)
    rank = jnp.sum(earlier * hot, axis=0, keepdims=True).astype(i32)
    slot = lax.broadcasted_iota(i32, (CAP, count), 0)
    prob = prob_ref[...].astype(f32)
    for k in range(n_expert):
        owner = lax.rem(me_ref[0] + k, n_expert) // quarters
        block = jnp.where((route == owner) & (rank == slot), 1.0, 0.0)
        placing_ref[k * CAP : (k + 1) * CAP, :] = block.astype(bf16)
        slot_prob = jnp.sum(block * prob, axis=1, keepdims=True)
        pieces[k][:, 2 * width :] = jnp.broadcast_to(slot_prob, (CAP, LANES)).astype(bf16)
    for start, source in ((0, tok_ref), (width, cot_ref)):
        for at in range(0, width, 512):
            part = jnp.dot(placing_ref[...], source[:, at : at + 512], preferred_element_type=f32)
            part = part.astype(bf16)
            for k in range(n_expert):
                pieces[k][:, start + at : start + at + 512] = part[k * CAP : (k + 1) * CAP]


def place(me, route, prob, tokens, cotangent, n_expert):
    count, width = tokens.shape
    outs = pl.pallas_call(
        functools.partial(place_kernel, n_expert),
        out_shape=[jax.ShapeDtypeStruct((n_expert * CAP, count), bf16)]
        + [jax.ShapeDtypeStruct((CAP, 2 * width + LANES), bf16)] * n_expert,
        in_specs=[SMEM] + [VMEM] * 4,
        out_specs=[VMEM] * (n_expert + 1),
        cost_estimate=SMALL,
    )(me.reshape(1), route.reshape(1, count), prob.reshape(1, count), tokens, cotangent)
    return outs[0], outs[1:]


def halves(whole):
    high = whole.astype(bf16)
    return high, (whole - high.astype(f32)).astype(bf16)


def weight_scratch(count, depth, units):
    return [
        pltpu.VMEM((count, depth, units), f32),
        pltpu.SemaphoreType.DMA((count, depth // BLOCK)),
    ]


def fetch(weights, buffer, arrived):
    copies = []
    for at in range(weights[0].shape[0] // BLOCK):
        here = slice(at * BLOCK, (at + 1) * BLOCK)
        for i, weight in enumerate(weights):
            copy = pltpu.make_async_copy(weight.at[here, :], buffer.at[i, here, :], arrived.at[i, at])
            copy.start()
            copies.append(copy)
    return copies


def times_weights(factors, buffer, copies):
    depth = buffer.shape[1]
    for at in range(depth // BLOCK):
        here = slice(at * BLOCK, (at + 1) * BLOCK)
        for i, (rows, total) in enumerate(factors):
            copies[at * len(factors) + i].wait()
            high, low = halves(buffer[i, here, :])
            row = rows[:, here]
            part = jnp.dot(row, high, preferred_element_type=f32)
            part += jnp.dot(row, low, preferred_element_type=f32)
            if at == 0:
                total[...] = part
            else:
                total[...] += part


def gate_factors(gate, up, prob):
    sig = jax.nn.sigmoid(gate)
    act = gate * sig
    hidden = act * up
    return prob * act, prob * (up * sig * (1.0 + gate * (1.0 - sig))), hidden


def against(left, right):
    return lax.dot_general(left, right, (((1,), (1,)), ((), ())), preferred_element_type=f32)


def chunk_kernel(count, *refs):
    pieces, weights, terms_ref = refs[:count], refs[count : count + 3], refs[count + 3]
    outs = refs[count + 4 : 2 * count + 4]
    tok, cot, gate_sum, up_sum, back_sum, low_ref, buffer, arrived = refs[2 * count + 4 :]
    depth, units = weights[0].shape
    copies = fetch(weights, buffer, arrived)
    for k, piece in enumerate(pieces):
        part = slice(k * CAP, (k + 1) * CAP)
        tok[part, :] = piece[:, :depth]
        cot[part, :] = piece[:, depth : 2 * depth]
    times_weights(((tok, gate_sum), (tok, up_sum), (cot, back_sum)), buffer, copies)
    for k, piece in enumerate(pieces):
        part = slice(k * CAP, (k + 1) * CAP)
        prob = piece[:, 2 * depth :].astype(f32)[:, :1]
        act, slope, hidden = gate_factors(gate_sum[part, :], up_sum[part, :], prob)
        back = back_sum[part, :]
        total = jnp.sum(hidden * back, axis=1, keepdims=True)
        outs[k][:, depth:] = jnp.broadcast_to(total, (CAP, LANES)).astype(outs[k].dtype)
        for at, factor in ((0, slope), (units, act)):
            high, low = halves(factor * back)
            terms_ref[part, at : at + units] = high
            low_ref[part, at : at + units] = low
        terms_ref[part, 2 * units :] = (prob * hidden).astype(bf16)
    for at in range(0, depth, BLOCK):
        total = None
        for i in range(2):
            high, low = halves(buffer[i, at : at + BLOCK, :])
            grad_hi = terms_ref[:, i * units : (i + 1) * units]
            grad_lo = low_ref[:, i * units : (i + 1) * units]
            both = against(high, jnp.concatenate([grad_hi, grad_lo], axis=0)).T
            part = both[: count * CAP] + both[count * CAP :] + against(low, grad_hi).T
            total = part if total is None else total + part
        for k, out in enumerate(outs):
            out[:, at : at + BLOCK] = total[k * CAP : (k + 1) * CAP].astype(out.dtype)


def chunk_rows(pieces, weights, back_type, passes):
    count = len(pieces)
    depth, units = weights[0].shape
    rows = count * CAP
    outs = pl.pallas_call(
        functools.partial(chunk_kernel, count),
        out_shape=[jax.ShapeDtypeStruct((rows, 3 * units), bf16)]
        + [jax.ShapeDtypeStruct((CAP, depth + LANES), back_type)] * count,
        in_specs=[VMEM] * count + [HBM] * 3,
        out_specs=[VMEM] * (count + 1),
        scratch_shapes=[pltpu.VMEM((rows, depth), bf16)] * 2
        + [pltpu.VMEM((rows, units), f32)] * 3
        + [pltpu.VMEM((rows, 2 * units), bf16)]
        + weight_scratch(3, depth, units),
        compiler_params=ALONE,
        cost_estimate=pl.CostEstimate(flops=passes * 192 * depth * units, bytes_accessed=MIB, transcendentals=0),
    )(*pieces, *weights)
    return outs[0], outs[1:]


def take_kernel(n_expert, placing_ref, *refs):
    pieces = refs[:n_expert]
    out_ref, prob_ref, rows = refs[n_expert:]
    count, width = out_ref.shape
    exact = rows.dtype != bf16
    for k in range(n_expert):
        rows[k * CAP : (k + 1) * CAP, :] = pieces[k][...]
    placing = placing_ref[...].astype(rows.dtype)
    for at in range(0, width, 512):
        part = lax.dot_general(
            placing, rows[:, at : at + 512], (((0,), (0,)), ((), ())),
            precision=highest if exact else None, preferred_element_type=f32,
        )
        out_ref[:, at : at + 512] = part.astype(bf16)
    column = rows[:, width:].astype(f32)[:, :1]
    prob_ref[...] = jnp.sum(placing_ref[...].astype(f32) * column, axis=0, keepdims=True).astype(bf16)


def take(placing, pieces):
    n_expert = len(pieces)
    count = placing.shape[1]
    width = pieces[0].shape[1] - LANES
    grad, prob = pl.pallas_call(
        functools.partial(take_kernel, n_expert),
        out_shape=[
            jax.ShapeDtypeStruct((count, width), bf16),
            jax.ShapeDtypeStruct((1, count), bf16),
        ],
        in_specs=[VMEM] * (n_expert + 1),
        out_specs=[VMEM] * 2,
        scratch_shapes=[pltpu.VMEM((n_expert * CAP, width + LANES), pieces[0].dtype)],
        compiler_params=pltpu.CompilerParams(vmem_limit_bytes=32 * MIB) if pieces[0].dtype != bf16 else PARAMS,
        cost_estimate=SMALL,
    )(placing, *pieces)
    return grad, prob.reshape(count)


def shards(tokens, cotangent, route, prob, w_gate, w_up, w_down):
    n_expert = lax.axis_size("expert")
    n_dp = lax.axis_size("dp")
    width = tokens.shape[1]
    share = width // n_dp
    scale = 1.0 / math.sqrt(tokens.shape[0] * n_dp * n_expert)
    back_type = bf16 if n_expert == HOT else f32
    me = lax.axis_index("expert").astype(i32)
    weights = (w_gate[0], w_up[0], w_down[0])
    chips = range(n_dp // 2)
    home = [None] * n_expert

    def exchange(payload):
        return [payload[0]] + [flipped(payload[k], "dp", 2 * k) for k in chips[1:]]

    def swap(*groups):
        terms = [g[:, 4 * share :] for got in groups for g in got]
        other = flipped(jnp.concatenate(terms), "dp", 1)
        cuts, at = [], 0
        for got in groups:
            count = len(got) * got[0].shape[0]
            cuts.append(other[at : at + count])
            at += count
        return cuts

    def give_back(home, shifts, back):
        home = list(home)
        for i, k in enumerate(shifts):
            home[k] = shifted(back[i], "expert", n_expert - k)
        return home

    placing, pieces = place(me, route, prob, tokens, cotangent, n_expert)
    odd = list(range(1, n_expert, 2))
    even = list(range(2, n_expert, 2))
    first = [shifted(pieces[k], "expert", k) for k in odd]

    terms, back = chunk_rows(pieces[:1], weights, back_type, 36)
    home[0] = back[0]
    own, terms = lax.optimization_barrier((pieces[0], terms))
    theirs = flipped(cut([own], width), "dp", 1)
    payload = pack([own], theirs, terms, width)
    late, payload[-1], first, _ = lax.optimization_barrier(
        ([pieces[k] for k in even], payload[-1], first, payload[0])
    )
    second = [shifted(piece, "expert", k) for piece, k in zip(late, even)]
    got_local = exchange(payload)

    theirs = flipped(cut(first, width), "dp", 1)
    terms, back = chunk_rows(first, weights, back_type, 24)
    payload = pack(first, theirs, terms, width)
    payload, got_local = lax.optimization_barrier((payload, got_local))
    got_first = exchange(payload)

    second, back, _ = lax.optimization_barrier((second, back, payload))
    home = give_back(home, odd, back)
    theirs = flipped(cut(second, width), "dp", 1)
    terms, back = chunk_rows(second, weights, back_type, 12)
    payload, got_first, back, home = lax.optimization_barrier(
        (pack(second, theirs, terms, width), got_first, back, home)
    )
    home = give_back(home, even, back)
    got_second = exchange(payload)
    local_other, first_other = swap(got_local, got_first)
    sums = weight_sums(got_local, local_other, None, share, None)
    sums = weight_sums(got_first, first_other, sums, share, None)
    got_second, home, sums = lax.optimization_barrier((got_second, home, sums))
    sums = weight_sums(got_second, swap(got_second)[0], sums, share, scale)

    grad_input, grad_prob = take(placing, home)
    return (grad_input, grad_prob, *[total[None] for total in sums])


def solution(mesh):
    placed = (
        P(("dp", "expert"), None),
        P(("dp", "expert"), None),
        P(("dp", "expert"), None),
        P(("dp", "expert")),
        P("expert", None, None),
        P("expert", None, None),
        P("expert", None, None),
    )
    return jax.shard_map(
        shards,
        mesh=mesh,
        in_specs=placed,
        out_specs=(
            P(("dp", "expert"), None),
            P(("dp", "expert")),
            P("expert", "dp", None),
            P("expert", "dp", None),
            P("expert", "dp", None),
        ),
        check_vma=False,
    )
```
